32 devices in a mesh: lon: 8 (over y, x, core), lat: 4 (over z).
Axes of the slice: x: 2, y: 2, z: 4, core: 2. Of those that a mesh axis runs over, the one named last changes fastest.
Arguments:
- field: bfloat16 [16, 8192, 128], P('lat', 'lon'), may hold values from -6 to 6
- conv_weight: bfloat16 [2, 3, 3, 3, 128, 128], replicated, may hold values from -0.1875 to 0.1875
- conv_bias: float32 [2, 3, 128], replicated, may hold values from -3 to 3
- spec_real: bfloat16 [2, 128, 128, 128], P(None, 'lon'), may hold values from -1.5 to 1.5
- spec_imag: bfloat16 [2, 128, 128, 128], P(None, 'lon'), may hold values from -1.5 to 1.5
Outputs:
- result: bfloat16 [16, 8192, 128], P('lat', 'lon')
The draws below stay inside these ranges and needn't reach their ends.
All inputs are finite; a program needn't handle non-finite values.
Results may differ from the reference program's by a relative error of at most 0.0045.
Values may be sent and summed in bfloat16 or wider, within the bound.
No kernel may reach another device: no remote copies, remote signals or barrier semaphores. Data moves between devices by JAX's collectives and lax.ppermute only.
A program may use at most 64 MiB of HBM per device.

```python
import math
import jax
import jax.numpy as jnp
from jax import lax

C = 128
MODES = 128
BLOCKS = 2
CONVS = 3
NLAT = 16
NLON = 8192


def block_levels(key, extent, split, least, high):
    level = 1.0
    for dim, shards_of in split:
        draws = jax.random.uniform(jax.random.fold_in(jax.random.fold_in(key, 6), dim), (shards_of,), jnp.float32, least / len(split), high / len(split))
        level = level * jnp.repeat(jnp.exp(draws), extent[dim] // shards_of).reshape((-1,) + (1,) * (len(extent) - 1 - dim))
    return level


def scatter_about(rng, dims, width, bound, split=(), kind=jnp.bfloat16):
    entries = width * jax.random.normal(rng, dims, jnp.float32)
    if split:
        entries = entries * block_levels(rng, dims, split, -0.22, 0.18)
    return jnp.clip(entries, -bound, bound).astype(kind)


def setup_inputs(seed: int = 0) -> dict:
    seeds = jax.random.split(jax.random.key(seed), 6)
    field = scatter_about(seeds[0], (NLAT, NLON, C), 1.0, 6.0, ((0, 4), (1, 8)))
    conv_weight = scatter_about(seeds[1], (BLOCKS, CONVS, 3, 3, C, C), (9 * C) ** -0.5, 0.1875)
    conv_bias = scatter_about(seeds[2], (BLOCKS, CONVS, C), 0.5, 3.0, (), jnp.float32)
    spec_real = scatter_about(seeds[3], (BLOCKS, MODES, C, C), (C // 8) ** -0.5, 1.5, ((1, 8),))
    spec_imag = scatter_about(seeds[4], (BLOCKS, MODES, C, C), (C // 8) ** -0.5, 1.5, ((1, 8),))
    return {"field": field, "conv_weight": conv_weight, "conv_bias": conv_bias, "spec_real": spec_real, "spec_imag": spec_imag}


def make_tables(lon_total, mode_count):
    cells = jnp.arange(lon_total, dtype=jnp.int32)
    waves = jnp.arange(mode_count, dtype=jnp.int32)
    product = cells[:, None] * waves[None, :] % lon_total
    theta = product.astype(jnp.float32) * (2.0 * math.pi / lon_total)
    full = jnp.stack([jnp.cos(theta), -jnp.sin(theta)], axis=2)
    basis = full.reshape(lon_total, 2 * mode_count)
    weights = jnp.where(waves == 0, 1.0, 2.0).astype(jnp.float32)
    inverse = (full * weights[None, :, None]).reshape(lon_total, 2 * mode_count)
    return (basis, inverse)

def convolve(state, kernels, bias):
    padded = jnp.pad(state, ((1, 1), (0, 0), (0, 0)))
    padded = jnp.concatenate([padded[:, -1:], padded, padded[:, :1]], axis=1)
    rows_out = state.shape[0]
    cols_out = state.shape[1]
    running = jnp.zeros(state.shape[:2] + (kernels.shape[3],), jnp.float32)
    for tap_a in range(3):
        for tap_d in range(3):
            window = padded[tap_a:tap_a + rows_out, tap_d:tap_d + cols_out].astype(jnp.float32)
            running = running + jnp.einsum('rnc,cd->rnd', window, kernels[tap_a, tap_d].astype(jnp.float32))
    return jax.nn.silu(running + bias).astype(jnp.bfloat16)

def mix_modes(spectrum, real_weight, imag_weight):
    halves = spectrum.reshape(real_weight.shape[0], 2, spectrum.shape[1], spectrum.shape[2])
    real_in = halves[:, 0]
    imag_in = halves[:, 1]
    wr = real_weight.astype(jnp.float32)
    wi = imag_weight.astype(jnp.float32)
    high = lax.Precision.HIGHEST
    real_out = jnp.einsum('klc,kcd->kld', real_in, wr, precision=high) - jnp.einsum('klc,kcd->kld', imag_in, wi, precision=high)
    imag_out = jnp.einsum('klc,kcd->kld', real_in, wi, precision=high) + jnp.einsum('klc,kcd->kld', imag_in, wr, precision=high)
    stacked = jnp.stack([real_out, imag_out], axis=1)
    return stacked.reshape(spectrum.shape)

def reference(field, conv_weight, conv_bias, spec_real, spec_imag):
    basis, inverse = make_tables(NLON, MODES)
    scale = 1.0 / math.sqrt(NLON)
    high = lax.Precision.HIGHEST
    state = field
    for block_index in range(BLOCKS):
        hidden = state
        for layer_index in range(CONVS):
            hidden = convolve(hidden, conv_weight[block_index, layer_index], conv_bias[block_index, layer_index])
        spectrum = jnp.einsum('nj,lnc->jlc', basis, hidden.astype(jnp.float32), precision=high) * scale
        mixed = mix_modes(spectrum, spec_real[block_index], spec_imag[block_index])
        spectral = jnp.einsum('nj,jlc->lnc', inverse, mixed, precision=high) * scale
        state = jnp.tanh(state.astype(jnp.float32) + hidden.astype(jnp.float32) + spectral).astype(jnp.bfloat16)
    return state
```

```python
import math

import jax
import jax.numpy as jnp
import ml_dtypes
import numpy as np
from jax import lax
from jax.experimental import pallas as pl
from jax.experimental.pallas import tpu as pltpu
from jax.sharding import PartitionSpec as P

BLOCKS = 2
CONVS = 3
PAD = 16
BF = jnp.bfloat16
F32 = jnp.float32
VMEM = pl.BlockSpec(memory_space=pltpu.VMEM)
PARAMS = pltpu.CompilerParams(vmem_limit_bytes=56 << 20)


def tile_of(width):
    best = 16
    for size in range(16, 400, 16):
        if width % size == 0:
            best = size
    return best


def build_weights(kernels, packed, layer):
    c = kernels.shape[-1]
    zero = jnp.zeros((c, c), BF)
    for tap in range(3):
        w0, w1, w2 = (kernels[layer, a, tap] for a in range(3))
        o = 2 * c * tap
        packed[layer, o : o + c, :c] = w0
        packed[layer, o : o + c, c:] = zero
        packed[layer, o + c : o + 2 * c, :c] = w1
        packed[layer, o + c : o + 2 * c, c:] = w0
        o = 6 * c + 2 * c * tap
        packed[layer, o : o + c, :c] = w2
        packed[layer, o : o + c, c:] = w1
        packed[layer, o + c : o + 2 * c, :c] = zero
        packed[layer, o + c : o + 2 * c, c:] = w2


def put_row(wide, pair, half, parts):
    c = wide.shape[2] // 6
    lanes = slice(2 * c + half * c, 2 * c + (half + 1) * c)
    for start, value in parts:
        wide[pair, start : start + value.shape[0], lanes] = value


def spread(wide, pair, line, tile):
    c2 = wide.shape[2] // 3
    for start in range(0, wide.shape[1], tile):
        wide[pair, start : start + tile, :c2] = line[pl.ds(start + 7, tile)].astype(BF)
        wide[pair, start : start + tile, 2 * c2 :] = line[pl.ds(start + 9, tile)].astype(BF)


def clear_line(line):
    line[0:8] = jnp.zeros((8, line.shape[1]), F32)
    end = line.shape[0]
    line[end - 8 : end] = jnp.zeros((8, line.shape[1]), F32)


def conv_stack(first, second, line, packed, bias, edge, rows, emit):
    width = first.shape[1]
    c2 = first.shape[2] // 3
    tile = tile_of(width)
    top, bottom = edge[0:1], edge[1:2]
    one = jnp.ones_like(top)
    buffers = (first, second)
    for layer in range(CONVS):
        src, dst = buffers[layer % 2], buffers[(layer + 1) % 2]
        pairs = rows // 2 + 2 - layer
        both = jnp.concatenate([bias[layer : layer + 1]] * 2, axis=1)
        masks = {}
        if layer == 0:
            masks = {0: (top, top), pairs - 1: (bottom, bottom)}
        elif layer == 1:
            masks = {0: (top, one), pairs - 1: (one, bottom)}
        for pair in range(pairs):
            for start in range(0, width, tile):
                cells = slice(start, start + tile)
                left = jnp.concatenate([src[pair, cells], src[pair + 1, cells]], axis=1)
                y = jnp.dot(left, packed[layer], preferred_element_type=F32) + both
                y = 0.5 * y
                y = y * (1.0 + jnp.tanh(y))
                if pair in masks:
                    y = y * jnp.concatenate(masks[pair], axis=1)
                if layer == CONVS - 1:
                    emit(pair, start, y.astype(BF))
                else:
                    dst[pair, cells, c2 : 2 * c2] = y.astype(BF)
                    line[start + 8 : start + 8 + tile] = y
            if layer < CONVS - 1:
                spread(dst, pair, line, tile)


def transform(forward, held, pair, part):
    cells = forward.shape[1]
    c2 = held.shape[2]
    both = jnp.dot(forward[...], held[pair, PAD : PAD + cells], preferred_element_type=F32)
    modes2 = both.shape[0] // 2
    part[:, pair * c2 : (pair + 1) * c2] = (both[:modes2] + both[modes2:]).astype(BF)


def row_parts(row, rows, own, up, down, own_edge, up_edge, down_edge):
    if row < 0:
        body, edge, at = up, up_edge, row + 3
    elif row < rows:
        body, edge, at = own, own_edge, row
    else:
        body, edge, at = down, down_edge, row - rows
    cells = body.shape[1]
    return [(0, edge[at, :PAD]), (PAD, body[at]), (PAD + cells, edge[at, PAD:])]


def first_kernel(
    own, up, down, own_edge, up_edge, down_edge, kernels, bias, edge, forward,
    part, hidden, to_up, to_down, first, second, line, packed, held,
):
    rows, cells, c = own.shape
    width = cells + 2 * PAD
    tile = tile_of(width)
    for layer in range(CONVS):
        build_weights(kernels, packed, layer)
    clear_line(line)
    for pair in range(rows // 2 + 3):
        for half in range(2):
            parts = row_parts(
                2 * pair - 3 + half, rows, own, up, down, own_edge, up_edge, down_edge
            )
            put_row(first, pair, half, parts)
        line[8 : 8 + width] = first[pair, :, 2 * c : 4 * c].astype(F32)
        spread(first, pair, line, tile)

    def emit(pair, start, y):
        span = slice(start, start + tile)
        held[pair, span] = y
        for half in range(2):
            row = 2 * pair + half
            value = y[:, half * c : (half + 1) * c]
            hidden[row, span] = value
            if row < 3:
                to_down[row, span] = value
            if row >= rows - 3:
                to_up[row - (rows - 3), span] = value

    conv_stack(first, second, line, packed, bias, edge, rows, emit)
    for pair in range(rows // 2):
        transform(forward, held, pair, part)


def mix_kernel(gathered, turn, real, imag, *rest):
    outs, (spread_in, spread_out) = rest[:-2], rest[-2:]
    modes, c = real.shape[0], real.shape[1]
    summed = jnp.dot(turn[...], gathered[...], preferred_element_type=F32)
    summed = summed[: 2 * modes] + summed[2 * modes :]
    rows = summed.shape[1] // c
    for half in range(2):
        for row in range(rows):
            spread_in[pl.ds(half * rows + row, modes, stride=2 * rows), :] = summed[
                half * modes : (half + 1) * modes, row * c : (row + 1) * c
            ]
    sign = jnp.where(lax.broadcasted_iota(jnp.int32, (2 * rows, c), 0) < rows, -1.0, 1.0)
    for k in range(modes):
        wide = spread_in[2 * rows * k : 2 * rows * (k + 1)]
        high = wide.astype(BF)
        low = (wide - high.astype(F32)).astype(BF)
        both = jnp.concatenate([high, low], axis=0)
        weight = jnp.concatenate([real[k], imag[k]], axis=1)
        out = jnp.dot(both, weight, preferred_element_type=F32)
        out = out[: 2 * rows] + out[2 * rows :]
        turned = pltpu.roll(out[:, c:], rows, 0)
        spread_out[2 * rows * k : 2 * rows * (k + 1)] = out[:, :c] + sign * turned
    for half in range(2):
        for row in range(rows):
            value = spread_out[pl.ds(half * rows + row, modes, stride=2 * rows), :].astype(BF)
            span = slice(half * modes, (half + 1) * modes)
            outs[0][span, row * c : (row + 1) * c] = value
            if len(outs) > 1:
                if row < 3:
                    outs[2][span, row * c : (row + 1) * c] = value
                if row >= rows - 3:
                    at = row - (rows - 3)
                    outs[1][span, at * c : (at + 1) * c] = value


def middle_kernel(
    own, up, down, own_edge, up_edge, down_edge, hidden, from_up, from_down, mixed, inverse,
    kernels, bias, edge, forward, part, state, hidden_out,
    first, second, line, packed, held,
):
    rows, cells, c = own.shape
    width = cells + 2 * PAD
    tile = tile_of(width)
    for layer in range(CONVS):
        build_weights(kernels, packed, layer)
    clear_line(line)
    top, bottom = edge[0:1], edge[1:2]
    one = jnp.ones_like(top)

    def keep(row):
        return top if row < 0 else (one if row < rows else bottom)

    for pair in range(rows // 2 + 3):
        names = [2 * pair - 3, 2 * pair - 2]
        for half, row in enumerate(names):
            parts = row_parts(row, rows, own, up, down, own_edge, up_edge, down_edge)
            put_row(first, pair, half, parts)
        mask = jnp.concatenate([keep(row) for row in names], axis=1)
        for start in range(0, width, tile):
            span = slice(start, start + tile)
            old = first[pair, span, 2 * c : 4 * c].astype(F32)
            pieces = []
            for row in names:
                if row < 0:
                    pieces.append(from_up[row + 3, span])
                elif row < rows:
                    pieces.append(hidden[row, span])
                else:
                    pieces.append(from_down[row - rows, span])
            conv = jnp.concatenate(pieces, axis=1).astype(F32)
            wave = jnp.dot(
                inverse[span],
                mixed[:, 2 * c * pair : 2 * c * (pair + 1)],
                preferred_element_type=F32,
            )
            new = jnp.tanh(old + conv + wave)
            if min(names) < 0 or max(names) >= rows:
                new = new * mask
            first[pair, span, 2 * c : 4 * c] = new.astype(BF)
            line[start + 8 : start + 8 + tile] = new
        spread(first, pair, line, tile)
        for half, row in enumerate(names):
            if 0 <= row < rows:
                lanes = slice((2 + half) * c, (3 + half) * c)
                state[row] = first[pair, PAD : PAD + cells, lanes]

    def emit(pair, start, y):
        span = slice(start, start + tile)
        held[pair, span] = y
        for half in range(2):
            hidden_out[2 * pair + half, span] = y[:, half * c : (half + 1) * c]

    conv_stack(first, second, line, packed, bias, edge, rows, emit)
    for pair in range(rows // 2):
        transform(forward, held, pair, part)


def last_kernel(state, hidden, mixed, inverse, result):
    rows, cells, c = state.shape
    for pair in range(rows // 2):
        wave = jnp.dot(
            inverse[PAD : PAD + cells],
            mixed[:, 2 * c * pair : 2 * c * (pair + 1)],
            preferred_element_type=F32,
        )
        for half in range(2):
            row = 2 * pair + half
            total = state[row].astype(F32) + hidden[row, PAD : PAD + cells].astype(F32)
            total = total + wave[:, half * c : (half + 1) * c]
            result[row] = jnp.tanh(total).astype(BF)


def forward_table(cells, lon_total, modes, lon_size):
    waves = np.arange(modes)
    theta = (2 * np.pi / lon_total) * (np.outer(waves, np.arange(cells)) % lon_total)
    full = np.stack([np.cos(theta), -np.sin(theta)], 0)
    full = full.reshape(2, lon_size, modes // lon_size, cells).transpose(1, 0, 2, 3)
    full = full.reshape(2 * modes, cells).astype(np.float32)
    high = full.astype(ml_dtypes.bfloat16)
    low = (full - high.astype(np.float32)).astype(ml_dtypes.bfloat16)
    return np.concatenate([high, low], 0)


def turn_table(me, lon_size, local, scale):
    waves = me * local + jnp.arange(local, dtype=jnp.int32)
    source = jnp.arange(lon_size, dtype=jnp.int32)
    phase = (source[None, :] * waves[:, None] % lon_size).astype(F32)
    phase = phase * (2.0 * math.pi / lon_size)
    cos, sin = scale * jnp.cos(phase), scale * jnp.sin(phase)
    eye = jnp.eye(local, dtype=F32)
    cos, sin = cos[:, :, None] * eye[:, None, :], sin[:, :, None] * eye[:, None, :]
    real = jnp.stack([cos, sin], axis=2)
    imag = jnp.stack([-sin, cos], axis=2)
    full = jnp.concatenate([real, imag], axis=0).reshape(2 * local, lon_size * 2 * local)
    high = full.astype(BF)
    low = (full - high.astype(F32)).astype(BF)
    return jnp.concatenate([high, low], axis=0)


def inverse_table(first_cell, width, lon_total, modes, lon_size):
    column = jnp.arange(2 * modes, dtype=jnp.int32)
    local = modes // lon_size
    waves = column // (2 * local) * local + column % local
    imaginary = column // local % 2 == 1
    cells = first_cell + jnp.arange(width, dtype=jnp.int32)
    cells = (cells + lon_total) % lon_total
    product = cells[:, None] * waves[None, :] % lon_total
    theta = product.astype(F32) * (2.0 * math.pi / lon_total)
    weight = jnp.where(waves == 0, 1.0, 2.0).astype(F32)[None, :]
    return (jnp.where(imaginary[None, :], -jnp.sin(theta), jnp.cos(theta)) * weight).astype(BF)


def lat_moves(above, below):
    size = lax.axis_size("lat")
    up = [(i, i + 1) for i in range(size - 1)]
    down = [(i + 1, i) for i in range(size - 1)]
    return lax.ppermute(above, "lat", up), lax.ppermute(below, "lat", down)


def shape(*dims):
    return jax.ShapeDtypeStruct(dims, BF)


def conv_scratch(rows, width, c):
    return [
        pltpu.VMEM((rows // 2 + 3, width, 6 * c), BF),
        pltpu.VMEM((rows // 2 + 2, width, 6 * c), BF),
        pltpu.VMEM((width + 16, 2 * c), F32),
        pltpu.VMEM((CONVS, 12 * c, 2 * c), BF),
        pltpu.VMEM((rows // 2, width, 2 * c), BF),
    ]


def call(kernel, args, outs, scratch):
    return pl.pallas_call(
        kernel,
        out_shape=outs,
        in_specs=[VMEM] * len(args),
        out_specs=[VMEM] * len(outs),
        scratch_shapes=scratch,
        compiler_params=PARAMS,
    )(*args)


def per_device(field, conv_weight, conv_bias, spec_real, spec_imag):
    rows, cells, c = field.shape
    width = cells + 2 * PAD
    lon_size, lat_size = lax.axis_size("lon"), lax.axis_size("lat")
    lon_me, lat_me = lax.axis_index("lon"), lax.axis_index("lat")
    lon_total = cells * lon_size
    local = spec_real.shape[1]
    modes = local * lon_size

    up, down = lat_moves(field[rows - 3 :], field[:3])
    right = [(i, (i + 1) % lon_size) for i in range(lon_size)]
    left = [(j, i) for i, j in right]
    from_left = lax.ppermute(field[:, cells - PAD :], "lon", right)
    from_right = lax.ppermute(field[:, :PAD], "lon", left)
    own_edge = jnp.concatenate([from_left, from_right], axis=1)
    up_edge, down_edge = lat_moves(own_edge[rows - 3 :], own_edge[:3])

    forward = jnp.asarray(forward_table(cells, lon_total, modes, lon_size))
    turn = turn_table(lon_me, lon_size, local, 1.0 / lon_total)
    inverse = inverse_table(lon_me * cells - PAD, width, lon_total, modes, lon_size)
    flags = jnp.stack([lat_me > 0, lat_me < lat_size - 1]).astype(F32)
    edge = jnp.broadcast_to(flags[:, None], (2, c))

    pieces = (field, up, down, own_edge, up_edge, down_edge)
    part, hidden, to_up, to_down = call(
        first_kernel,
        pieces + (conv_weight[0], conv_bias[0], edge, forward),
        [
            shape(2 * modes, rows * c),
            shape(rows, width, c),
            shape(3, width, c),
            shape(3, width, c),
        ],
        conv_scratch(rows, width, c),
    )
    from_up, from_down = lat_moves(to_up, to_down)

    def mix(part, block, halo):
        chunks = part.reshape(lon_size, 2 * local, rows * c)
        chunks = lax.all_to_all(chunks, "lon", 0, 0)
        outs = [shape(2 * local, rows * c)]
        if halo:
            outs += [shape(2 * local, 3 * c)] * 2
        line = pltpu.VMEM((2 * rows * local, c), F32)
        got = call(
            mix_kernel,
            (chunks.reshape(2 * modes, rows * c), turn, spec_real[block], spec_imag[block]),
            outs,
            [line, line],
        )
        mixed = got[0]
        if halo:
            above, below = lat_moves(got[1], got[2])
            mixed = jnp.concatenate([above, mixed, below], axis=1)
        return lax.all_gather(mixed, "lon", axis=0, tiled=True)

    mixed = mix(part, 0, True)
    part, state, hidden = call(
        middle_kernel,
        pieces
        + (hidden, from_up, from_down, mixed, inverse)
        + (conv_weight[1], conv_bias[1], edge, forward),
        [shape(2 * modes, rows * c), shape(rows, cells, c), shape(rows, width, c)],
        conv_scratch(rows, width, c),
    )
    mixed = mix(part, 1, False)
    (result,) = call(last_kernel, (state, hidden, mixed, inverse), [shape(rows, cells, c)], [])
    return result


def solution(mesh):
    return jax.shard_map(
        per_device,
        mesh=mesh,
        in_specs=(
            P("lat", "lon", None),
            P(),
            P(),
            P(None, "lon", None, None),
            P(None, "lon", None, None),
        ),
        out_specs=P("lat", "lon", None),
        check_vma=False,
    )
```

```python
import math

import jax
import jax.numpy as jnp
import ml_dtypes
import numpy as np
from jax import lax
from jax.experimental import pallas as pl
from jax.experimental.pallas import tpu as pltpu
from jax.sharding import PartitionSpec as P

BLOCKS = 2
CONVS = 3
PAD = 16
RUNS = 16
HALO = 3
WINOGRAD = True
BF = jnp.bfloat16
F32 = jnp.float32
VMEM = pl.BlockSpec(memory_space=pltpu.VMEM)
SMEM = pl.BlockSpec(memory_space=pltpu.SMEM)
PARAMS = pltpu.CompilerParams(vmem_limit_bytes=56 << 20)


def tile_of(tiles):
    return max(n for n in range(1, 12) if tiles % n == 0) * RUNS


def pack_row(line, wide, row):
    c = line.shape[1]
    run = line.shape[0] // RUNS
    for cell in range(run):
        lanes = slice(cell % 2 * c, (cell % 2 + 1) * c)
        at = RUNS * (cell // 2 + 1)
        wide[row, at : at + RUNS, lanes] = line[pl.ds(cell, RUNS, stride=run), :].astype(BF)


def close_row(wide, row):
    c = wide.shape[2] // 2
    end = wide.shape[1] - RUNS
    before = wide[row, end - RUNS : end, c:].astype(F32)
    wide[row, 0:RUNS, c:] = pltpu.roll(before, 1, 0).astype(BF)
    after = wide[row, RUNS : 2 * RUNS, :c].astype(F32)
    wide[row, end : end + RUNS, :c] = pltpu.roll(after, RUNS - 1, 0).astype(BF)


def build_weights(kernels, block, packed, layer):
    c = kernels.shape[-1]
    zero = jnp.zeros((c, c), BF)
    for tap in range(3):
        g0, g1, g2 = (kernels[block, layer, a, tap].astype(F32) for a in range(3))
        if WINOGRAD:
            outer = g0 + g2
            parts = (0.5 * g0, 0.25 * (outer + g1), 0.25 * (outer - g1), 0.5 * g2)
        else:
            parts = (0.5 * g0, 0.5 * g1, 0.5 * g2)
        for i, part in enumerate(parts):
            value = part.astype(BF)
            for cell in range(2):
                source = cell + tap - 1
                at = {0: 0, 1: c, 2: 2 * c, -1: 3 * c}[source]
                packed[layer, i, at : at + c, cell * c : (cell + 1) * c] = value
    for i in range(packed.shape[1]):
        packed[layer, i, 2 * c : 3 * c, :c] = zero
        packed[layer, i, 3 * c :, c:] = zero


def window(wide, row, start, size):
    c = wide.shape[2] // 2
    here = wide[row, start + RUNS : start + RUNS + size]
    after = wide[row, start + 2 * RUNS : start + 2 * RUNS + size, :c]
    before = wide[row, start : start + size, c:]
    return jnp.concatenate([here, after, before], axis=1)


def dot(a, b):
    return jnp.dot(a, b, preferred_element_type=F32)


def silu_of_half(half):
    return half + half * jnp.tanh(half)


def conv_pair(src, row, start, size, packed, layer):
    d = [window(src, row + i, start, size) for i in range(4)]
    if WINOGRAD:
        inputs = (d[0] - d[2], d[1] + d[2], d[2] - d[1], d[1] - d[3])
        m = [dot(x, packed[layer, i]) for i, x in enumerate(inputs)]
        return (m[1] + m[2]) + m[0], m[1] - m[2] - m[3]
    w = jnp.concatenate([packed[layer, i] for i in range(3)], axis=0)
    return tuple(dot(jnp.concatenate(d[i : i + 3], axis=1), w) for i in range(2))


def conv_stack(first, second, packed, bias, edge, rows, emit):
    width = first.shape[1] - 2 * RUNS
    tile = tile_of(width // RUNS)
    buffers = (first, second)
    for layer in range(CONVS):
        src, dst = buffers[layer % 2], buffers[(layer + 1) % 2]
        outs = rows + 2 * (CONVS - 1 - layer)
        halo = CONVS - 1 - layer
        both = 0.5 * jnp.concatenate([bias[layer : layer + 1]] * 2, axis=1)
        for pair in range(0, outs, 2):
            for start in range(0, width, tile):
                sums = conv_pair(src, pair, start, tile, packed, layer)
                for i, total in enumerate(sums):
                    row = pair + i - halo
                    y = silu_of_half(total + both)
                    if row < 0:
                        y = y * edge[0]
                    elif row >= rows:
                        y = y * edge[1]
                    if layer == CONVS - 1:
                        emit(row, start, y.astype(BF))
                    else:
                        dst[pair + i, start + RUNS : start + RUNS + tile] = y.astype(BF)
            if layer < CONVS - 1:
                for i in range(2):
                    close_row(dst, pair + i)


def transform(forward, leak, bias, held, part):
    rows, c = held.shape[0], held.shape[2] // 2
    half = 0.5 * bias[CONVS - 1 : CONVS]
    level = silu_of_half(half)
    for row in range(0, rows, 2):
        cells = [
            jnp.concatenate([held[row + i, :, e * c : (e + 1) * c] for i in range(2)], axis=1)
            for e in range(2)
        ]
        both = dot(forward[...], jnp.concatenate(cells, axis=0))
        modes2 = both.shape[0] // 2
        total = both[:modes2] + both[modes2:]
        total = total - leak[...] * jnp.concatenate([level, level], axis=1)
        part[:, row * c : (row + 2) * c] = total.astype(BF)


def first_kernel(
    own, up, down, own_edge, up_edge, down_edge, kernels, bias, edge, forward, leak,
    part, hidden, to_up, to_down, packed_field,
    first, second, line, packed, held,
):
    rows, cells, c = own.shape
    for layer in range(CONVS):
        build_weights(kernels, 0, packed, layer)
    for at in range(rows + 2 * HALO):
        row = at - HALO
        if row < 0:
            body, ends, source = up, up_edge, row + HALO
        elif row < rows:
            body, ends, source = own, own_edge, row
        else:
            body, ends, source = down, down_edge, row - rows
        line[at % 2, 0:PAD] = ends[source, :PAD].astype(F32)
        line[at % 2, PAD : PAD + cells] = body[source].astype(F32)
        line[at % 2, PAD + cells :] = ends[source, PAD:].astype(F32)
        pack_row(line.at[at % 2], first, at)
        close_row(first, at)
        packed_field[at] = first[at, RUNS : first.shape[1] - RUNS]

    def emit(row, start, y):
        span = slice(start, start + y.shape[0])
        held[row, span] = y
        hidden[row, span] = y
        if row < HALO:
            to_down[row, span] = y
        if row >= rows - HALO:
            to_up[row - (rows - HALO), span] = y

    conv_stack(first, second, packed, bias, edge, rows, emit)
    transform(forward, leak, bias, held, part)


def mix_kernel(gathered, turn, real, imag, bias, owner, *rest):
    outs, (spread_in, spread_out) = rest[:-2], rest[-2:]
    modes, c = real.shape[1], real.shape[2]
    summed = jnp.dot(turn[...], gathered[...], preferred_element_type=F32)
    summed = summed[: 2 * modes] + summed[2 * modes :]
    rows = summed.shape[1] // c
    level = owner[0] * silu_of_half(0.5 * bias[CONVS - 1 : CONVS])
    for half in range(2):
        for row in range(rows):
            spread_in[pl.ds(half * rows + row, modes, stride=2 * rows), :] = summed[
                half * modes : (half + 1) * modes, row * c : (row + 1) * c
            ]
    spread_in[0:rows] = spread_in[0:rows] + level
    sign = jnp.where(lax.broadcasted_iota(jnp.int32, (2 * rows, c), 0) < rows, -1.0, 1.0)
    for k in range(modes):
        wide = spread_in[2 * rows * k : 2 * rows * (k + 1)]
        high = wide.astype(BF)
        low = (wide - high.astype(F32)).astype(BF)
        both = jnp.concatenate([high, low], axis=0)
        weight = jnp.concatenate([real[0, k], imag[0, k]], axis=1)
        out = jnp.dot(both, weight, preferred_element_type=F32)
        out = out[: 2 * rows] + out[2 * rows :]
        turned = pltpu.roll(out[:, c:], rows, 0)
        spread_out[2 * rows * k : 2 * rows * (k + 1)] = out[:, :c] + sign * turned
    for half in range(2):
        for row in range(rows):
            value = spread_out[pl.ds(half * rows + row, modes, stride=2 * rows), :].astype(BF)
            span = slice(half * modes, (half + 1) * modes)
            outs[0][span, row * c : (row + 1) * c] = value
            if len(outs) > 1:
                if row < HALO:
                    outs[2][span, row * c : (row + 1) * c] = value
                if row >= rows - HALO:
                    at = row - (rows - HALO)
                    outs[1][span, at * c : (at + 1) * c] = value


def middle_kernel(
    packed_field, hidden, from_up, from_down, mixed, inverse,
    kernels, bias, edge, forward, leak,
    part, state, hidden_out,
    first, second, packed, held,
):
    rows, width, c = hidden.shape[0], hidden.shape[1], hidden.shape[2] // 2
    tile = tile_of(width // RUNS)
    for layer in range(CONVS):
        build_weights(kernels, 1, packed, layer)
    for at in range(0, rows + 2 * HALO, 2):
        lanes = slice(at * c, (at + 2) * c)
        for start in range(0, width, tile):
            span = slice(start, start + tile)
            waves = [dot(inverse[e, span], mixed[:, lanes]) for e in range(2)]
            for i in range(2):
                row = at + i - HALO
                if row < 0:
                    conv = from_up[row + HALO, span]
                elif row < rows:
                    conv = hidden[row, span]
                else:
                    conv = from_down[row - rows, span]
                wave = jnp.concatenate([w[:, i * c : (i + 1) * c] for w in waves], axis=1)
                new = packed_field[at + i, span].astype(F32) + conv.astype(F32) + wave
                new = jnp.tanh(new)
                if row < 0:
                    new = new * edge[0]
                elif row >= rows:
                    new = new * edge[1]
                new = new.astype(BF)
                first[at + i, start + RUNS : start + RUNS + tile] = new
                if 0 <= row < rows:
                    state[row, span] = new
        for i in range(2):
            close_row(first, at + i)

    def emit(row, start, y):
        span = slice(start, start + y.shape[0])
        held[row, span] = y
        hidden_out[row, span] = y

    conv_stack(first, second, packed, bias, edge, rows, emit)
    transform(forward, leak, bias, held, part)


def last_kernel(state, hidden, mixed, inverse, result, line):
    rows, width, c = state.shape[0], state.shape[1], state.shape[2] // 2
    cells = result.shape[1]
    run = 2 * width // RUNS
    for pair in range(0, rows, 2):
        waves = [dot(inverse[e], mixed[:, pair * c : (pair + 2) * c]) for e in range(2)]
        for i in range(2):
            row = pair + i
            for e in range(2):
                lanes = slice(e * c, (e + 1) * c)
                total = state[row, :, lanes].astype(F32) + hidden[row, :, lanes].astype(F32)
                total = jnp.tanh(total + waves[e][:, i * c : (i + 1) * c])
                for u in range(width // RUNS):
                    value = total[u * RUNS : (u + 1) * RUNS]
                    line[i, pl.ds(2 * u + e, RUNS, stride=run), :] = value
            result[row] = line[i, PAD : PAD + cells].astype(BF)


def cell_order(width):
    run = width // RUNS
    cell = np.arange(width // 2) // RUNS * 2 + np.arange(width // 2) % RUNS * run
    return np.stack([cell, cell + 1])


def forward_table(cells, lon_total, modes, lon_size):
    order = cell_order(cells + 2 * PAD).reshape(-1) - PAD
    inside = (order >= 0) & (order < cells)
    waves = np.arange(modes)
    theta = (2 * np.pi / lon_total) * (np.outer(waves, order) % lon_total)
    full = np.stack([np.cos(theta), -np.sin(theta)], 0) * inside
    full = full.reshape(2, lon_size, modes // lon_size, -1).transpose(1, 0, 2, 3)
    full = full.reshape(2 * modes, -1).astype(np.float32)
    leak = full.astype(np.float64).sum(1, keepdims=True).astype(np.float32)
    high = full.astype(ml_dtypes.bfloat16)
    low = (full - high.astype(np.float32)).astype(ml_dtypes.bfloat16)
    return np.concatenate([high, low], 0), leak


def turn_table(me, lon_size, local, scale):
    waves = me * local + jnp.arange(local, dtype=jnp.int32)
    source = jnp.arange(lon_size, dtype=jnp.int32)
    phase = (source[None, :] * waves[:, None] % lon_size).astype(F32)
    phase = phase * (2.0 * math.pi / lon_size)
    cos, sin = scale * jnp.cos(phase), scale * jnp.sin(phase)
    eye = jnp.eye(local, dtype=F32)
    cos, sin = cos[:, :, None] * eye[:, None, :], sin[:, :, None] * eye[:, None, :]
    real = jnp.stack([cos, sin], axis=2)
    imag = jnp.stack([-sin, cos], axis=2)
    full = jnp.concatenate([real, imag], axis=0).reshape(2 * local, lon_size * 2 * local)
    high = full.astype(BF)
    low = (full - high.astype(F32)).astype(BF)
    return jnp.concatenate([high, low], axis=0)


def inverse_table(first_cell, width, lon_total, modes, lon_size):
    column = np.arange(2 * modes)
    local = modes // lon_size
    waves = column // (2 * local) * local + column % local
    imaginary = column // local % 2 == 1
    cells = first_cell + lon_total + jnp.asarray(cell_order(width), jnp.int32)
    product = cells[:, :, None] % lon_total * waves.astype(np.int32) % lon_total
    theta = product.astype(F32) * (2.0 * math.pi / lon_total)
    weight = np.where(waves == 0, 1.0, 2.0).astype(np.float32)
    return (jnp.where(imaginary, -jnp.sin(theta), jnp.cos(theta)) * weight).astype(BF)


def lat_moves(above, below):
    size = lax.axis_size("lat")
    up = [(i, i + 1) for i in range(size - 1)]
    down = [(i + 1, i) for i in range(size - 1)]
    return lax.ppermute(above, "lat", up), lax.ppermute(below, "lat", down)


def shape(*dims):
    return jax.ShapeDtypeStruct(dims, BF)


def conv_scratch(rows, width, c):
    return [
        pltpu.VMEM((rows + 2 * HALO, width // 2 + 2 * RUNS, 2 * c), BF),
        pltpu.VMEM((rows + 2 * HALO - 2, width // 2 + 2 * RUNS, 2 * c), BF),
        pltpu.VMEM((CONVS, 4 if WINOGRAD else 3, 4 * c, 2 * c), BF),
        pltpu.VMEM((rows, width // 2, 2 * c), BF),
    ]


def call(kernel, args, outs, scratch, in_specs=None, grid=()):
    return pl.pallas_call(
        kernel,
        grid=grid,
        out_shape=outs,
        in_specs=in_specs or [VMEM] * len(args),
        out_specs=[VMEM] * len(outs),
        scratch_shapes=scratch,
        compiler_params=PARAMS,
    )(*args)


def per_device(field, conv_weight, conv_bias, spec_real, spec_imag):
    rows, cells, c = field.shape
    width = cells + 2 * PAD
    half = width // 2
    lon_size, lat_size = lax.axis_size("lon"), lax.axis_size("lat")
    lon_me, lat_me = lax.axis_index("lon"), lax.axis_index("lat")
    lon_total = cells * lon_size
    local = spec_real.shape[1]
    modes = local * lon_size

    above, below = field[rows - HALO :], field[:HALO]
    up, down = lat_moves(above, below)
    above, below, last, leading = lax.optimization_barrier(
        (above, below, field[:, cells - PAD :], field[:, :PAD])
    )
    right = [(i, (i + 1) % lon_size) for i in range(lon_size)]
    left = [(j, i) for i, j in right]
    from_left = lax.ppermute(last, "lon", right)
    from_right = lax.ppermute(leading, "lon", left)
    own_edge = jnp.concatenate([from_left, from_right], axis=1)
    up_edge, down_edge = lat_moves(own_edge[rows - HALO :], own_edge[:HALO])

    forward, leak = forward_table(cells, lon_total, modes, lon_size)
    forward, leak = jnp.asarray(forward), jnp.asarray(leak)
    turn = turn_table(lon_me, lon_size, local, 1.0 / lon_total)
    inverse = inverse_table(lon_me * cells - PAD, width, lon_total, modes, lon_size)
    edge = jnp.stack([lat_me > 0, lat_me < lat_size - 1]).astype(F32)
    owner = (lon_me == 0).astype(F32).reshape(1)
    up, turn, inverse, edge, owner = lax.optimization_barrier((up, turn, inverse, edge, owner))

    part, hidden, to_up, to_down, packed_field = call(
        first_kernel,
        (field, up, down, own_edge, up_edge, down_edge)
        + (conv_weight, conv_bias[0], edge, forward, leak),
        [
            shape(2 * modes, rows * c),
            shape(rows, half, 2 * c),
            shape(HALO, half, 2 * c),
            shape(HALO, half, 2 * c),
            shape(rows + 2 * HALO, half, 2 * c),
        ],
        (lambda s: s[:2] + [pltpu.VMEM((2, width, c), F32)] + s[2:])(conv_scratch(rows, width, c)),
        in_specs=[VMEM] * 8 + [SMEM] + [VMEM] * 2,
    )
    from_up, from_down = lat_moves(to_up, to_down)

    def mix(part, block, halo):
        chunks = part.reshape(lon_size, 2 * local, rows * c)
        chunks = lax.all_to_all(chunks, "lon", 0, 0)
        widths = [rows * c] + ([HALO * c] * 2 if halo else [])
        line = pltpu.VMEM((2 * rows * local, c), F32)
        weights = pl.BlockSpec((1, local, c, c), lambda i: (block, 0, 0, 0))
        got = call(
            mix_kernel,
            (chunks.reshape(2 * modes, rows * c), turn, spec_real, spec_imag)
            + (conv_bias[block], owner),
            [shape(2 * local, n) for n in widths],
            [line, line],
            in_specs=[VMEM, VMEM, weights, weights, VMEM, SMEM],
            grid=(1,),
        )
        mixed = got[0]
        if halo:
            above, below = lat_moves(got[1], got[2])
            mixed = jnp.concatenate([above, mixed, below], axis=1)
        return lax.all_gather(mixed, "lon", axis=0, tiled=True)

    mixed = mix(part, 0, True)
    part, state, hidden = call(
        middle_kernel,
        (packed_field, hidden, from_up, from_down, mixed, inverse)
        + (conv_weight, conv_bias[1], edge, forward, leak),
        [shape(2 * modes, rows * c), shape(rows, half, 2 * c), shape(rows, half, 2 * c)],
        conv_scratch(rows, width, c),
        in_specs=[VMEM] * 8 + [SMEM] + [VMEM] * 2,
    )
    mixed = mix(part, 1, False)
    (result,) = call(
        last_kernel,
        (state, hidden, mixed, inverse),
        [shape(rows, cells, c)],
        [pltpu.VMEM((2, width, c), F32)],
    )
    return result


def solution(mesh):
    return jax.shard_map(
        per_device,
        mesh=mesh,
        in_specs=(
            P("lat", "lon", None),
            P(),
            P(),
            P(None, "lon", None, None),
            P(None, "lon", None, None),
        ),
        out_specs=P("lat", "lon", None),
        check_vma=False,
    )
```

```python
import math

import jax
import jax.numpy as jnp
import ml_dtypes
import numpy as np
from jax import lax
from jax.experimental import pallas as pl
from jax.experimental.pallas import tpu as pltpu
from jax.sharding import PartitionSpec as P

BLOCKS = 2
CONVS = 3
PAD = 16
RUNS = 16
HALO = 3
WINOGRAD = True
BF = jnp.bfloat16
F32 = jnp.float32
VMEM = pl.BlockSpec(memory_space=pltpu.VMEM)
ANY = pl.BlockSpec(memory_space=pl.ANY)
HBM = pl.BlockSpec(memory_space=pltpu.HBM)
PARAMS = pltpu.CompilerParams(vmem_limit_bytes=28 << 20)


def tile_of(tiles):
    return max(n for n in range(1, 12) if tiles % n == 0) * RUNS


def pack_row(line, wide, row):
    c = line.shape[1]
    run = line.shape[0] // RUNS
    for cell in range(run):
        lanes = slice(cell % 2 * c, (cell % 2 + 1) * c)
        at = RUNS * (cell // 2 + 1)
        wide[row, at : at + RUNS, lanes] = line[pl.ds(cell, RUNS, stride=run), :].astype(BF)


def close_row(wide, row):
    c = wide.shape[2] // 2
    end = wide.shape[1] - RUNS
    before = wide[row, end - RUNS : end, c:].astype(F32)
    wide[row, 0:RUNS, c:] = pltpu.roll(before, 1, 0).astype(BF)
    after = wide[row, RUNS : 2 * RUNS, :c].astype(F32)
    wide[row, end : end + RUNS, :c] = pltpu.roll(after, RUNS - 1, 0).astype(BF)


def build_weights(kernels, block, packed, layer):
    c = kernels.shape[-1]
    zero = jnp.zeros((c, c), BF)
    for tap in range(3):
        g0, g1, g2 = (kernels[block, layer, a, tap].astype(F32) for a in range(3))
        if WINOGRAD:
            outer = g0 + g2
            parts = (0.5 * g0, 0.25 * (outer + g1), 0.25 * (outer - g1), 0.5 * g2)
        else:
            parts = (0.5 * g0, 0.5 * g1, 0.5 * g2)
        for i, part in enumerate(parts):
            value = part.astype(BF)
            for cell in range(2):
                source = cell + tap - 1
                at = {0: 0, 1: c, 2: 2 * c, -1: 3 * c}[source]
                packed[layer, i, at : at + c, cell * c : (cell + 1) * c] = value
    for i in range(packed.shape[1]):
        packed[layer, i, 2 * c : 3 * c, :c] = zero
        packed[layer, i, 3 * c :, c:] = zero


def window(wide, row, start, size):
    c = wide.shape[2] // 2
    here = wide[row, start + RUNS : start + RUNS + size]
    after = wide[row, start + 2 * RUNS : start + 2 * RUNS + size, :c]
    before = wide[row, start : start + size, c:]
    return jnp.concatenate([here, after, before], axis=1)


def dot(a, b):
    return jnp.dot(a, b, preferred_element_type=F32)


def silu_of_half(half):
    return half + half * jnp.tanh(half)


def conv_pair(src, row, start, size, packed, layer):
    d = [window(src, row + i, start, size) for i in range(4)]
    if WINOGRAD:
        inputs = (d[0] - d[2], d[1] + d[2], d[2] - d[1], d[1] - d[3])
        m = [dot(x, packed[layer, i]) for i, x in enumerate(inputs)]
        return (m[1] + m[2]) + m[0], m[1] - m[2] - m[3]
    w = jnp.concatenate([packed[layer, i] for i in range(3)], axis=0)
    return tuple(dot(jnp.concatenate(d[i : i + 3], axis=1), w) for i in range(2))


def conv_stack(first, second, packed, bias, edge, rows, emit):
    width = first.shape[1] - 2 * RUNS
    tile = tile_of(width // RUNS)
    buffers = (first, second)
    for layer in range(CONVS):
        src, dst = buffers[layer % 2], buffers[(layer + 1) % 2]
        outs = rows + 2 * (CONVS - 1 - layer)
        halo = CONVS - 1 - layer
        both = 0.5 * jnp.concatenate([bias[layer : layer + 1]] * 2, axis=1)
        for pair in range(0, outs, 2):
            for start in range(0, width, tile):
                sums = conv_pair(src, pair, start, tile, packed, layer)
                for i, total in enumerate(sums):
                    row = pair + i - halo
                    y = silu_of_half(total + both)
                    if row < 0:
                        y = y * edge[0]
                    elif row >= rows:
                        y = y * edge[1]
                    if layer == CONVS - 1:
                        emit(row, start, y.astype(BF))
                    else:
                        dst[pair + i, start + RUNS : start + RUNS + tile] = y.astype(BF)
            if layer < CONVS - 1:
                for i in range(2):
                    close_row(dst, pair + i)


def transform(forward, leak, bias, held, part):
    rows, c = held.shape[0], held.shape[2] // 2
    half = 0.5 * bias[CONVS - 1 : CONVS]
    level = silu_of_half(half)
    for row in range(0, rows, 2):
        cells = [
            jnp.concatenate([held[row + i, :, e * c : (e + 1) * c] for i in range(2)], axis=1)
            for e in range(2)
        ]
        both = dot(forward[...], jnp.concatenate(cells, axis=0))
        modes2 = both.shape[0] // 2
        total = both[:modes2] + both[modes2:]
        total = total - leak[...] * jnp.concatenate([level, level], axis=1)
        part[:, row * c : (row + 2) * c] = total.astype(BF)


def first_kernel(
    own, far_up, far_down, own_edge, up_edge, down_edge, kernels, bias, forward, leak,
    part, hidden, to_up, to_down, packed_field,
    first, second, line, packed, held, up, down, sems,
):
    rows, cells, c = own.shape
    edge = lat_edges()
    copies = [
        pltpu.make_async_copy(far_up, up, sems.at[0]),
        pltpu.make_async_copy(far_down, down, sems.at[1]),
    ]
    for copy in copies:
        copy.start()
    for layer in range(CONVS):
        build_weights(kernels, 0, packed, layer)
    order = [*range(HALO, HALO + rows), *range(HALO), *range(rows + HALO, rows + 2 * HALO)]
    for at in order:
        row = at - HALO
        if row == -HALO:
            copies[0].wait()
        if row == rows:
            copies[1].wait()
        if row < 0:
            body, ends, source = up, up_edge, row + HALO
        elif row < rows:
            body, ends, source = own, own_edge, row
        else:
            body, ends, source = down, down_edge, row - rows
        line[at % 2, 0:PAD] = ends[source, :PAD].astype(F32)
        line[at % 2, PAD : PAD + cells] = body[source].astype(F32)
        line[at % 2, PAD + cells :] = ends[source, PAD:].astype(F32)
        pack_row(line.at[at % 2], first, at)
        close_row(first, at)
        packed_field[at] = first[at, RUNS : first.shape[1] - RUNS]

    def emit(row, start, y):
        span = slice(start, start + y.shape[0])
        held[row, span] = y
        hidden[row, span] = y
        if row < HALO:
            to_down[row, span] = y
        if row >= rows - HALO:
            to_up[row - (rows - HALO), span] = y

    conv_stack(first, second, packed, bias, edge, rows, emit)
    transform(forward, leak, bias, held, part)


def mix_kernel(gathered, turn, real, imag, bias, *rest):
    me = lax.axis_index("lon")
    outs, (spread_in, spread_out) = rest[:-2], rest[-2:]
    modes, c = real.shape[1], real.shape[2]
    summed = jnp.dot(turn[me], gathered[...], preferred_element_type=F32)
    summed = summed[: 2 * modes] + summed[2 * modes :]
    rows = summed.shape[1] // c
    level = (me == 0).astype(F32) * silu_of_half(0.5 * bias[CONVS - 1 : CONVS])
    for half in range(2):
        for row in range(rows):
            spread_in[pl.ds(half * rows + row, modes, stride=2 * rows), :] = summed[
                half * modes : (half + 1) * modes, row * c : (row + 1) * c
            ]
    spread_in[0:rows] = spread_in[0:rows] + level
    sign = jnp.where(lax.broadcasted_iota(jnp.int32, (2 * rows, c), 0) < rows, -1.0, 1.0)
    for k in range(modes):
        wide = spread_in[2 * rows * k : 2 * rows * (k + 1)]
        high = wide.astype(BF)
        low = (wide - high.astype(F32)).astype(BF)
        both = jnp.concatenate([high, low], axis=0)
        weight = jnp.concatenate([real[0, k], imag[0, k]], axis=1)
        out = jnp.dot(both, weight, preferred_element_type=F32)
        out = out[: 2 * rows] + out[2 * rows :]
        turned = pltpu.roll(out[:, c:], rows, 0)
        spread_out[2 * rows * k : 2 * rows * (k + 1)] = out[:, :c] + sign * turned
    for half in range(2):
        for row in range(rows):
            value = spread_out[pl.ds(half * rows + row, modes, stride=2 * rows), :].astype(BF)
            span = slice(half * modes, (half + 1) * modes)
            outs[0][span, row * c : (row + 1) * c] = value
            if len(outs) > 1:
                if row < HALO:
                    outs[2][span, row * c : (row + 1) * c] = value
                if row >= rows - HALO:
                    at = row - (rows - HALO)
                    outs[1][span, at * c : (at + 1) * c] = value


def middle_kernel(
    packed_field, hidden, from_up, from_down, mixed, inverse,
    kernels, bias, forward, leak,
    part, state, hidden_out,
    first, second, packed, held,
):
    edge = lat_edges()
    rows, width, c = hidden.shape[0], hidden.shape[1], hidden.shape[2] // 2
    tile = tile_of(width // RUNS)
    for layer in range(CONVS):
        build_weights(kernels, 1, packed, layer)
    for at in range(0, rows + 2 * HALO, 2):
        lanes = slice(at * c, (at + 2) * c)
        for start in range(0, width, tile):
            span = slice(start, start + tile)
            waves = [dot(inverse[e, span], mixed[:, lanes]) for e in range(2)]
            for i in range(2):
                row = at + i - HALO
                if row < 0:
                    conv = from_up[row + HALO, span]
                elif row < rows:
                    conv = hidden[row, span]
                else:
                    conv = from_down[row - rows, span]
                wave = jnp.concatenate([w[:, i * c : (i + 1) * c] for w in waves], axis=1)
                new = packed_field[at + i, span].astype(F32) + conv.astype(F32) + wave
                new = jnp.tanh(new)
                if row < 0:
                    new = new * edge[0]
                elif row >= rows:
                    new = new * edge[1]
                new = new.astype(BF)
                first[at + i, start + RUNS : start + RUNS + tile] = new
                if 0 <= row < rows:
                    state[row, span] = new
        for i in range(2):
            close_row(first, at + i)

    def emit(row, start, y):
        span = slice(start, start + y.shape[0])
        held[row, span] = y
        hidden_out[row, span] = y

    conv_stack(first, second, packed, bias, edge, rows, emit)
    transform(forward, leak, bias, held, part)


def last_kernel(state, hidden, mixed, inverse, result, line):
    rows, width, c = state.shape[0], state.shape[1], state.shape[2] // 2
    cells = result.shape[1]
    run = 2 * width // RUNS
    for pair in range(0, rows, 2):
        waves = [dot(inverse[e], mixed[:, pair * c : (pair + 2) * c]) for e in range(2)]
        for i in range(2):
            row = pair + i
            for e in range(2):
                lanes = slice(e * c, (e + 1) * c)
                total = state[row, :, lanes].astype(F32) + hidden[row, :, lanes].astype(F32)
                total = jnp.tanh(total + waves[e][:, i * c : (i + 1) * c])
                for u in range(width // RUNS):
                    value = total[u * RUNS : (u + 1) * RUNS]
                    line[i, pl.ds(2 * u + e, RUNS, stride=run), :] = value
            result[row] = line[i, PAD : PAD + cells].astype(BF)


def cell_order(width):
    run = width // RUNS
    cell = np.arange(width // 2) // RUNS * 2 + np.arange(width // 2) % RUNS * run
    return np.stack([cell, cell + 1])


def forward_table(cells, lon_total, modes, lon_size):
    order = cell_order(cells + 2 * PAD).reshape(-1) - PAD
    inside = (order >= 0) & (order < cells)
    waves = np.arange(modes)
    theta = (2 * np.pi / lon_total) * (np.outer(waves, order) % lon_total)
    full = np.stack([np.cos(theta), -np.sin(theta)], 0) * inside
    full = full.reshape(2, lon_size, modes // lon_size, -1).transpose(1, 0, 2, 3)
    full = full.reshape(2 * modes, -1).astype(np.float32)
    leak = full.astype(np.float64).sum(1, keepdims=True).astype(np.float32)
    high = full.astype(ml_dtypes.bfloat16)
    low = (full - high.astype(np.float32)).astype(ml_dtypes.bfloat16)
    return np.concatenate([high, low], 0), leak


def turn_table(lon_size, local, scale):
    waves = np.arange(lon_size)[:, None, None] * local + np.arange(local)[:, None]
    phase = np.arange(lon_size) * waves % lon_size * (2 * np.pi / lon_size)
    cos, sin = scale * np.cos(phase), scale * np.sin(phase)
    eye = np.eye(local)
    cos, sin = (x[:, :, :, None] * eye[:, None, :] for x in (cos, sin))
    real = np.stack([cos, sin], axis=3)
    imag = np.stack([-sin, cos], axis=3)
    full = np.concatenate([real, imag], axis=1)
    full = full.reshape(lon_size, 2 * local, lon_size * 2 * local).astype(np.float32)
    high = full.astype(ml_dtypes.bfloat16)
    low = (full - high.astype(np.float32)).astype(ml_dtypes.bfloat16)
    return np.concatenate([high, low], axis=1)


def inverse_parts(cells, lon_total, modes, lon_size):
    column = np.arange(2 * modes)
    local = modes // lon_size
    waves = column // (2 * local) * local + column % local
    imaginary = column // local % 2 == 1
    order = cell_order(cells + 2 * PAD) - PAD
    theta = (2 * np.pi / lon_total) * (order[:, :, None] * waves % lon_total)
    weight = np.where(waves == 0, 1.0, 2.0)
    cos, sin = weight * np.cos(theta), weight * np.sin(theta)
    by_cos = np.where(imaginary, -sin, cos).astype(np.float32)
    by_sin = np.where(imaginary, -cos, -sin).astype(np.float32)
    return waves.astype(np.int32), by_cos, by_sin


def phase_table(cells, lon_total, modes, lon_size):
    waves = inverse_parts(cells, lon_total, modes, lon_size)[0]
    phase = np.arange(lon_size)[:, None] * waves % lon_size * (2 * np.pi / lon_size)
    return np.stack([np.cos(phase), np.sin(phase)], 1).astype(np.float32)


def slice_kernel(field, above, below, sems):
    rows = field.shape[0]
    first = pltpu.make_async_copy(field.at[rows - HALO :], above, sems.at[0])
    second = pltpu.make_async_copy(field.at[:HALO], below, sems.at[1])
    first.start()
    second.start()
    first.wait()
    second.wait()


def side_kernel(field, after, last, leading, sems):
    cells = field.shape[1]
    first = pltpu.make_async_copy(field.at[:, cells - PAD :], last, sems.at[0])
    second = pltpu.make_async_copy(field.at[:, :PAD], leading, sems.at[1])
    first.start()
    second.start()
    first.wait()
    second.wait()


def edge_kernel(from_left, from_right, by_cos, by_sin, phase, edges, above, below, inverse):
    rows = from_left.shape[0]
    for row in range(rows):
        both = jnp.concatenate([from_left[row], from_right[row]], axis=0)
        edges[row] = both
        if row < HALO:
            below[row] = both
        if row >= rows - HALO:
            above[row - (rows - HALO)] = both
    turn = phase[lax.axis_index("lon")]
    for e in range(2):
        inverse[e] = (by_cos[e] * turn[0:1] + by_sin[e] * turn[1:2]).astype(BF)


def lat_edges():
    me, size = lax.axis_index("lat"), lax.axis_size("lat")
    return [(me > 0).astype(F32), (me < size - 1).astype(F32)]


def lat_moves(above, below):
    size = lax.axis_size("lat")
    up = [(i, i + 1) for i in range(size - 1)]
    down = [(i + 1, i) for i in range(size - 1)]
    return lax.ppermute(above, "lat", up), lax.ppermute(below, "lat", down)


def shape(*dims):
    return jax.ShapeDtypeStruct(dims, BF)


def conv_scratch(rows, width, c):
    got = middle_scratch(rows, width, c)
    return got[:2] + [pltpu.VMEM((2, width, c), F32)] + got[2:]


def middle_scratch(rows, width, c):
    return [
        pltpu.VMEM((rows + 2 * HALO, width // 2 + 2 * RUNS, 2 * c), BF),
        pltpu.VMEM((rows + 2 * HALO - 2, width // 2 + 2 * RUNS, 2 * c), BF),
        pltpu.VMEM((CONVS, 4 if WINOGRAD else 3, 4 * c, 2 * c), BF),
        pltpu.VMEM((rows, width // 2, 2 * c), BF),
    ]


def call(kernel, args, outs, scratch, in_specs=None, out_specs=None, grid=()):
    return pl.pallas_call(
        kernel,
        grid=grid,
        out_shape=outs,
        in_specs=in_specs or [VMEM] * len(args),
        out_specs=out_specs or [VMEM] * len(outs),
        scratch_shapes=scratch,
        compiler_params=PARAMS,
    )(*(jnp.asarray(arg) for arg in args))


def per_device(field, conv_weight, conv_bias, spec_real, spec_imag):
    rows, cells, c = field.shape
    width = cells + 2 * PAD
    half = width // 2
    lon_size = lax.axis_size("lon")
    lon_total = cells * lon_size
    local = spec_real.shape[1]
    modes = local * lon_size

    above, below = call(
        slice_kernel,
        (field,),
        [shape(HALO, cells, c)] * 2,
        [pltpu.SemaphoreType.DMA((2,))],
        in_specs=[HBM],
        out_specs=[ANY] * 2,
    )
    up, down = lat_moves(above, below)
    last, leading = call(
        side_kernel,
        (field, above),
        [shape(rows, PAD, c)] * 2,
        [pltpu.SemaphoreType.DMA((2,))],
        in_specs=[HBM, ANY],
        out_specs=[ANY] * 2,
    )
    right = [(i, (i + 1) % lon_size) for i in range(lon_size)]
    left = [(j, i) for i, j in right]
    from_left = lax.ppermute(last, "lon", right)
    from_right = lax.ppermute(leading, "lon", left)
    tables = (cells, lon_total, modes, lon_size)
    _, by_cos, by_sin = inverse_parts(*tables)
    own_edge, above, below, inverse = call(
        edge_kernel,
        (from_left, from_right, by_cos, by_sin, phase_table(*tables)),
        [shape(rows, 2 * PAD, c)] + [shape(HALO, 2 * PAD, c)] * 2 + [shape(2, half, 2 * modes)],
        [],
    )
    up_edge, down_edge = lat_moves(above, below)
    forward, leak = forward_table(*tables)
    turn = turn_table(lon_size, local, 1.0 / lon_total)

    part, hidden, to_up, to_down, packed_field = call(
        first_kernel,
        (field, up, down, own_edge, up_edge, down_edge)
        + (conv_weight, conv_bias[0], forward, leak),
        [
            shape(2 * modes, rows * c),
            shape(rows, half, 2 * c),
            shape(HALO, half, 2 * c),
            shape(HALO, half, 2 * c),
            shape(rows + 2 * HALO, half, 2 * c),
        ],
        conv_scratch(rows, width, c)
        + [pltpu.VMEM((HALO, cells, c), BF)] * 2
        + [pltpu.SemaphoreType.DMA((2,))],
        in_specs=[VMEM, ANY, ANY] + [VMEM] * 7,
    )
    from_up, from_down = lat_moves(to_up, to_down)

    def mix(part, block, halo):
        chunks = part.reshape(lon_size, 2 * local, rows * c)
        chunks = lax.all_to_all(chunks, "lon", 0, 0)
        widths = [rows * c] + ([HALO * c] * 2 if halo else [])
        line = pltpu.VMEM((2 * rows * local, c), F32)
        weights = pl.BlockSpec((1, local, c, c), lambda i: (block, 0, 0, 0))
        got = call(
            mix_kernel,
            (chunks.reshape(2 * modes, rows * c), turn, spec_real, spec_imag)
            + (conv_bias[block],),
            [shape(2 * local, n) for n in widths],
            [line, line],
            in_specs=[VMEM, VMEM, weights, weights, VMEM],
            grid=(1,),
        )
        mixed = got[0]
        if halo:
            above, below = lat_moves(got[1], got[2])
            mixed = jnp.concatenate([above, mixed, below], axis=1)
        return lax.all_gather(mixed, "lon", axis=0, tiled=True)

    mixed = mix(part, 0, True)
    part, state, hidden = call(
        middle_kernel,
        (packed_field, hidden, from_up, from_down, mixed, inverse)
        + (conv_weight, conv_bias[1], forward, leak),
        [shape(2 * modes, rows * c), shape(rows, half, 2 * c), shape(rows, half, 2 * c)],
        middle_scratch(rows, width, c),
    )
    mixed = mix(part, 1, False)
    (result,) = call(
        last_kernel,
        (state, hidden, mixed, inverse),
        [shape(rows, cells, c)],
        [pltpu.VMEM((2, width, c), F32)],
    )
    return result


def solution(mesh):
    return jax.shard_map(
        per_device,
        mesh=mesh,
        in_specs=(
            P("lat", "lon", None),
            P(),
            P(),
            P(None, "lon", None, None),
            P(None, "lon", None, None),
        ),
        out_specs=P("lat", "lon", None),
        check_vma=False,
    )
```

```python
import math

import jax
import jax.numpy as jnp
import ml_dtypes
import numpy as np
from jax import lax
from jax.experimental import pallas as pl
from jax.experimental.pallas import tpu as pltpu
from jax.sharding import PartitionSpec as P

BLOCKS = 2
CONVS = 3
PAD = 16
RUNS = 16
HALO = 3
WINOGRAD = True
BF = jnp.bfloat16
F32 = jnp.float32
VMEM = pl.BlockSpec(memory_space=pltpu.VMEM)
ANY = pl.BlockSpec(memory_space=pl.ANY)
HBM = pl.BlockSpec(memory_space=pltpu.HBM)
DMA = pltpu.SemaphoreType.DMA
PARAMS = pltpu.CompilerParams(vmem_limit_bytes=28 << 20)


def tile_of(tiles):
    return max(n for n in range(1, 12) if tiles % n == 0) * RUNS


def pack_row(line, wide, row):
    c = line.shape[1]
    run = line.shape[0] // RUNS
    for cell in range(run):
        lanes = slice(cell % 2 * c, (cell % 2 + 1) * c)
        at = RUNS * (cell // 2 + 1)
        wide[row, at : at + RUNS, lanes] = line[pl.ds(cell, RUNS, stride=run), :].astype(BF)


def close_row(wide, row):
    c = wide.shape[2] // 2
    end = wide.shape[1] - RUNS
    before = wide[row, end - RUNS : end, c:].astype(F32)
    wide[row, 0:RUNS, c:] = pltpu.roll(before, 1, 0).astype(BF)
    after = wide[row, RUNS : 2 * RUNS, :c].astype(F32)
    wide[row, end : end + RUNS, :c] = pltpu.roll(after, RUNS - 1, 0).astype(BF)


def build_weights(kernels, block, packed, layer):
    c = kernels.shape[-1]
    zero = jnp.zeros((c, c), BF)
    for tap in range(3):
        g0, g1, g2 = (kernels[block, layer, a, tap].astype(F32) for a in range(3))
        if WINOGRAD:
            outer = g0 + g2
            parts = (0.5 * g0, 0.25 * (outer + g1), 0.25 * (outer - g1), 0.5 * g2)
        else:
            parts = (0.5 * g0, 0.5 * g1, 0.5 * g2)
        for i, part in enumerate(parts):
            value = part.astype(BF)
            for cell in range(2):
                source = cell + tap - 1
                at = {0: 0, 1: c, 2: 2 * c, -1: 3 * c}[source]
                packed[layer, i, at : at + c, cell * c : (cell + 1) * c] = value
    for i in range(packed.shape[1]):
        packed[layer, i, 2 * c : 3 * c, :c] = zero
        packed[layer, i, 3 * c :, c:] = zero


def window(wide, row, start, size):
    c = wide.shape[2] // 2
    here = wide[row, start + RUNS : start + RUNS + size]
    after = wide[row, start + 2 * RUNS : start + 2 * RUNS + size, :c]
    before = wide[row, start : start + size, c:]
    return jnp.concatenate([here, after, before], axis=1)


def dot(a, b):
    return jnp.dot(a, b, preferred_element_type=F32)


def silu_of_half(half):
    return half + half * jnp.tanh(half)


def conv_pair(d, packed, layer):
    if WINOGRAD:
        inputs = (d[0] - d[2], d[1] + d[2], d[2] - d[1], d[1] - d[3])
        m = [dot(x, packed[layer, i]) for i, x in enumerate(inputs)]
        return (m[1] + m[2]) + m[0], m[1] - m[2] - m[3]
    w = jnp.concatenate([packed[layer, i] for i in range(3)], axis=0)
    return tuple(dot(jnp.concatenate(d[i : i + 3], axis=1), w) for i in range(2))


class Rows:
    def __init__(self, *held):
        self.at = {}
        for ref, first in held:
            self.at.update({first + i: (ref, i) for i in range(ref.shape[0])})

    def __getitem__(self, row):
        return self.at[row]


def conv_rows(src, dst, span, layer, packed, bias, edge, rows):
    ref = src[span[0]][0]
    width = ref.shape[1] - 2 * RUNS
    tile = tile_of(width // RUNS)
    both = 0.5 * jnp.concatenate([bias[layer : layer + 1]] * 2, axis=1)
    for pair in range(*span, 2):
        for start in range(0, width, tile):
            sums = conv_pair(
                [window(*src[pair + i - 1], start, tile) for i in range(4)], packed, layer
            )
            for i, total in enumerate(sums):
                row = pair + i
                y = silu_of_half(total + both)
                if row < 0:
                    y = y * edge[0]
                elif row >= rows:
                    y = y * edge[1]
                if callable(dst):
                    dst(row, start, y.astype(BF))
                else:
                    ref, at = dst[row]
                    ref[at, start + RUNS : start + RUNS + tile] = y.astype(BF)
        if not callable(dst):
            for i in range(2):
                close_row(*dst[pair + i])


def transform(forward, leak, bias, held, kept, sent):
    core = lax.rem(lax.axis_index("lon"), 2)
    rows, c = held.shape[0], held.shape[2] // 2
    half = 0.5 * bias[CONVS - 1 : CONVS]
    level = silu_of_half(half)
    for row in range(0, rows, 2):
        cells = [
            jnp.concatenate([held[row + i, :, e * c : (e + 1) * c] for i in range(2)], axis=1)
            for e in range(2)
        ]
        both = dot(forward[core], jnp.concatenate(cells, axis=0))
        modes2 = both.shape[0] // 2
        total = both[:modes2] + both[modes2:]
        total = total - leak[core] * jnp.concatenate([level, level], axis=1)
        lanes = slice(row * c, (row + 2) * c)
        kept[:, lanes] = total[: modes2 // 2]
        sent[:, lanes] = total[modes2 // 2 :]


def pack_cells(body, ends, source, line, wide, at):
    cells = body.shape[1]
    line[0:PAD] = ends[source, :PAD].astype(F32)
    line[PAD : PAD + cells] = body[source].astype(F32)
    line[PAD + cells :] = ends[source, PAD:].astype(F32)
    pack_row(line, wide, at)
    close_row(wide, at)


def lower_part(field, first, second, packed, bias, edge, rows):
    x, y, z = Rows((field, 0)), Rows((first, 2)), Rows((second, 3))
    conv_rows(x, y, (2, rows + 2), 0, packed, bias, edge, rows)
    conv_rows(y, z, (3, rows + 1), 1, packed, bias, edge, rows)


def upper_part(before, field, first, second, more, packed, bias, edge, emit):
    rows = field.shape[0] - HALO
    x = Rows((before, -HALO), (field, 0))
    y = Rows((more[0], -2), (first, 2))
    z = Rows((more[1], -1), (second, 3))
    conv_rows(x, y, (-2, 2), 0, packed, bias, edge, rows)
    conv_rows(y, z, (-1, 3), 1, packed, bias, edge, rows)
    conv_rows(z, emit, (0, rows), 2, packed, bias, edge, rows)


def prepare_kernel(own, own_edge, kernels, field, packed, later, line):
    for layer in range(CONVS):
        build_weights(kernels, 0, packed, layer)
        build_weights(kernels, 1, later, layer)
    for row in range(own.shape[0]):
        pack_cells(own, own_edge, row, line.at[row % 2], field, row)


def first_lower_kernel(down, down_edge, own, packed, bias, after, field, first, second, line):
    rows = own.shape[0]
    field[:rows] = own[...]
    for row in range(HALO):
        pack_cells(down, down_edge, row, line.at[row % 2], field, rows + row)
    lower_part(field, first, second, packed, bias, lat_edges(), rows)


def first_upper_kernel(
    up, up_edge, field, first, second, packed, bias, forward, leak,
    kept, sent, hidden, to_up, to_down, before,
    line, more, most, held,
):
    rows = field.shape[0] - HALO
    for row in range(HALO):
        pack_cells(up, up_edge, row, line.at[row % 2], before, row)

    def emit(row, start, y):
        span = slice(start, start + y.shape[0])
        held[row, span] = y
        hidden[row, span] = y
        if row < HALO:
            to_down[row, span] = y
        if row >= rows - HALO:
            to_up[row - (rows - HALO), span] = y

    upper_part(before, field, first, second, (more, most), packed, bias, lat_edges(), emit)
    transform(forward, leak, bias, held, kept, sent)


def pair_kernel(kept, got, *outs):
    chip = lax.div(lax.axis_index("lon"), 2)
    rows = outs[0].shape[0]
    for step, out in enumerate(outs):
        span = pl.ds(pl.multiple_of((chip ^ step) * rows, rows), rows)
        out[...] = (kept[span, :] + got[span, :]).astype(BF)


def mix_kernel(turn, real, imag, bias, *rest):
    *sums, mixed, spread_in, spread_out = rest
    me = lax.axis_index("lon")
    modes, c = real.shape[1], real.shape[2]
    summed = dot(turn[me], jnp.concatenate([x[...] for x in sums], axis=0))
    summed = summed[: 2 * modes] + summed[2 * modes :]
    rows = summed.shape[1] // c
    level = (me == 0).astype(F32) * silu_of_half(0.5 * bias[CONVS - 1 : CONVS])
    for half in range(2):
        for row in range(rows):
            spread_in[pl.ds(half * rows + row, modes, stride=2 * rows), :] = summed[
                half * modes : (half + 1) * modes, row * c : (row + 1) * c
            ]
    spread_in[0:rows] = spread_in[0:rows] + level
    sign = jnp.where(lax.broadcasted_iota(jnp.int32, (2 * rows, c), 0) < rows, -1.0, 1.0)
    for k in range(modes):
        wide = spread_in[2 * rows * k : 2 * rows * (k + 1)]
        high = wide.astype(BF)
        low = (wide - high.astype(F32)).astype(BF)
        both = jnp.concatenate([high, low], axis=0)
        weight = jnp.concatenate([real[0, k], imag[0, k]], axis=1)
        out = jnp.dot(both, weight, preferred_element_type=F32)
        out = out[: 2 * rows] + out[2 * rows :]
        turned = pltpu.roll(out[:, c:], rows, 0)
        spread_out[2 * rows * k : 2 * rows * (k + 1)] = out[:, :c] + sign * turned
    for half in range(2):
        for row in range(rows):
            value = spread_out[pl.ds(half * rows + row, modes, stride=2 * rows), :].astype(BF)
            span = slice(half * modes, (half + 1) * modes)
            mixed[span, row * c : (row + 1) * c] = value


def halo_kernel(mixed, out):
    lanes = out.shape[1]
    even = lax.rem(lax.axis_index("lon"), 2) == 0

    @pl.when(even)
    def _():
        out[...] = mixed[:, mixed.shape[1] - lanes :]

    @pl.when(jnp.logical_not(even))
    def _():
        out[...] = mixed[:, :lanes]


def pick(mine, other, first):
    even = lax.rem(lax.axis_index("lon"), 2) == 0
    return jnp.where(even == first, mine[...], other[...])


def next_state(old, conv, mixed, inverse, new, at, count, mask):
    c = mixed.shape[1] // conv[0].shape[0]
    width = conv[0].shape[1]
    tile = tile_of(width // RUNS)
    for pair in range(0, count, 2):
        lanes = slice(pair * c, min(pair + 2, count) * c)
        for start in range(0, width, tile):
            span = slice(start, start + tile)
            wide = slice(start + RUNS, start + RUNS + tile)
            waves = [dot(inverse[e, span], mixed[:, lanes]) for e in range(2)]
            for i in range(min(2, count - pair)):
                wave = jnp.concatenate([w[:, i * c : (i + 1) * c] for w in waves], axis=1)
                total = old[0][old[1] + pair + i, wide].astype(F32)
                total = total + conv[0][pair + i, span].astype(F32) + wave
                total = jnp.tanh(total)
                if mask is not None:
                    total = total * mask
                new[at + pair + i, wide] = total.astype(BF)
        for i in range(min(2, count - pair)):
            close_row(new, at + pair + i)


def middle_own_kernel(field, hidden, mixed, inverse, state):
    next_state((field, 0), (hidden,), mixed, inverse, state, 0, hidden.shape[0], None)


def middle_lower_kernel(
    field, from_down, mine, other, own, inverse, packed, bias, state, first, second, mixed_down
):
    rows = own.shape[0]
    edge = lat_edges()
    state[:rows] = own[...]
    mixed_down[...] = pick(mine, other, False)
    next_state((field, rows), (from_down,), mixed_down, inverse, state, rows, HALO, edge[1])
    lower_part(state, first, second, packed, bias, edge, rows)


def middle_upper_kernel(
    before, from_up, mine, other, inverse, state, first, second, packed, bias, forward, leak,
    kept, sent, hidden, above, mixed_up, more, most, held,
):
    edge = lat_edges()
    mixed_up[...] = pick(mine, other, True)
    next_state((before, 0), (from_up,), mixed_up, inverse, above, 0, HALO, edge[0])

    def emit(row, start, y):
        span = slice(start, start + y.shape[0])
        held[row, span] = y
        hidden[row, span] = y

    upper_part(above, state, first, second, (more, most), packed, bias, edge, emit)
    transform(forward, leak, bias, held, kept, sent)


def last_kernel(state, hidden, mixed, inverse, result, line):
    rows, width, c = hidden.shape[0], hidden.shape[1], hidden.shape[2] // 2
    cells = result.shape[1]
    run = 2 * width // RUNS
    for pair in range(0, rows, 2):
        waves = [dot(inverse[e], mixed[:, pair * c : (pair + 2) * c]) for e in range(2)]
        for i in range(2):
            row = pair + i
            for e in range(2):
                lanes = slice(e * c, (e + 1) * c)
                total = state[row, RUNS : RUNS + width, lanes].astype(F32) + hidden[row, :, lanes].astype(F32)
                total = jnp.tanh(total + waves[e][:, i * c : (i + 1) * c])
                for u in range(width // RUNS):
                    value = total[u * RUNS : (u + 1) * RUNS]
                    line[i, pl.ds(2 * u + e, RUNS, stride=run), :] = value
            result[row] = line[i, PAD : PAD + cells].astype(BF)


def cell_order(width):
    run = width // RUNS
    cell = np.arange(width // 2) // RUNS * 2 + np.arange(width // 2) % RUNS * run
    return np.stack([cell, cell + 1])


def forward_table(cells, lon_total, modes, lon_size):
    order = cell_order(cells + 2 * PAD).reshape(-1) - PAD
    inside = (order >= 0) & (order < cells)
    waves = np.arange(modes)
    tables, leaks = [], []
    for core in range(2):
        theta = (2 * np.pi / lon_total) * (np.outer(waves, order + core * cells) % lon_total)
        full = np.stack([np.cos(theta), -np.sin(theta)], 0) * inside
        full = full.reshape(2, lon_size // 2, 2, modes // lon_size, -1)
        full = full.transpose(2, 1, 0, 3, 4)[[core, 1 - core]]
        full = full.reshape(2 * modes, -1).astype(np.float32)
        leaks.append(full.astype(np.float64).sum(1, keepdims=True).astype(np.float32))
        high = full.astype(ml_dtypes.bfloat16)
        low = (full - high.astype(np.float32)).astype(ml_dtypes.bfloat16)
        tables.append(np.concatenate([high, low], 0))
    return np.stack(tables), np.stack(leaks)


def turn_table(lon_size, local, scale):
    chips = lon_size // 2
    me = np.arange(lon_size)[:, None, None]
    waves = me * local + np.arange(local)[:, None]
    source = 2 * ((me // 2) ^ np.arange(chips))
    phase = source * waves % lon_size * (2 * np.pi / lon_size)
    cos, sin = scale * np.cos(phase), scale * np.sin(phase)
    eye = np.eye(local)
    cos, sin = (x[:, :, :, None] * eye[:, None, :] for x in (cos, sin))
    real = np.stack([cos, sin], axis=3)
    imag = np.stack([-sin, cos], axis=3)
    full = np.concatenate([real, imag], axis=1)
    full = full.reshape(lon_size, 2 * local, chips * 2 * local).astype(np.float32)
    high = full.astype(ml_dtypes.bfloat16)
    low = (full - high.astype(np.float32)).astype(ml_dtypes.bfloat16)
    return np.concatenate([high, low], axis=1)


def inverse_parts(cells, lon_total, modes, lon_size):
    column = np.arange(2 * modes)
    local = modes // lon_size
    waves = column // (2 * local) * local + column % local
    imaginary = column // local % 2 == 1
    order = cell_order(cells + 2 * PAD) - PAD
    theta = (2 * np.pi / lon_total) * (order[:, :, None] * waves % lon_total)
    weight = np.where(waves == 0, 1.0, 2.0)
    cos, sin = weight * np.cos(theta), weight * np.sin(theta)
    by_cos = np.where(imaginary, -sin, cos).astype(np.float32)
    by_sin = np.where(imaginary, -cos, -sin).astype(np.float32)
    return waves.astype(np.int32), by_cos, by_sin


def phase_table(cells, lon_total, modes, lon_size):
    waves = inverse_parts(cells, lon_total, modes, lon_size)[0]
    phase = np.arange(lon_size)[:, None] * waves % lon_size * (2 * np.pi / lon_size)
    return np.stack([np.cos(phase), np.sin(phase)], 1).astype(np.float32)


def slice_kernel(field, *rest):
    out, sem = rest[-2:]
    at = 0 if len(rest) == 2 else field.shape[0] - HALO
    copy = pltpu.make_async_copy(field.at[at : at + HALO], out, sem)
    copy.start()
    copy.wait()


def side_kernel(field, after, last, leading, sems):
    cells = field.shape[1]
    first = pltpu.make_async_copy(field.at[:, cells - PAD :], last, sems.at[0])
    second = pltpu.make_async_copy(field.at[:, :PAD], leading, sems.at[1])
    first.start()
    second.start()
    first.wait()
    second.wait()


def edge_kernel(from_left, from_right, edges, below):
    for row in range(from_left.shape[0]):
        both = jnp.concatenate([from_left[row], from_right[row]], axis=0)
        edges[row] = both
        if row < HALO:
            below[row] = both


def copy_kernel(edges, below, above):
    rows = edges.shape[0]
    above[...] = edges[rows - HALO :]


def inverse_kernel(parts, phase, after, inverse):
    turn = phase[lax.axis_index("lon")]
    for e in range(2):
        inverse[e] = (parts[0, e] * turn[0:1] + parts[1, e] * turn[1:2]).astype(BF)


def lat_edges():
    me, size = lax.axis_index("lat"), lax.axis_size("lat")
    return [(me > 0).astype(F32), (me < size - 1).astype(F32)]


def move(array, up):
    size = lax.axis_size("lat")
    pairs = [(i, i + 1) if up else (i + 1, i) for i in range(size - 1)]
    return lax.ppermute(array, "lat", pairs)


def shape(*dims):
    return jax.ShapeDtypeStruct(dims, BF)


def call(kernel, args, outs, scratch, in_specs=None, out_specs=None, grid=()):
    return pl.pallas_call(
        kernel,
        grid=grid,
        out_shape=outs,
        in_specs=in_specs or [VMEM] * len(args),
        out_specs=out_specs or [VMEM] * len(outs),
        scratch_shapes=scratch,
        compiler_params=PARAMS,
    )(*(jnp.asarray(arg) for arg in args))


def per_device(field, conv_weight, conv_bias, spec_real, spec_imag):
    rows, cells, c = field.shape
    width = cells + 2 * PAD
    half = width // 2
    lon_size = lax.axis_size("lon")
    lon_total = cells * lon_size
    local = spec_real.shape[1]
    modes = local * lon_size

    wide = half + 2 * RUNS
    below = call(
        slice_kernel, (field,), [shape(HALO, cells, c)], [DMA], in_specs=[HBM], out_specs=[ANY]
    )[0]
    down = move(below, False)
    above = call(
        slice_kernel,
        (field, below),
        [shape(HALO, cells, c)],
        [DMA],
        in_specs=[HBM, ANY],
        out_specs=[ANY],
    )[0]
    up = move(above, True)
    last, leading = call(
        side_kernel,
        (field, above),
        [shape(rows, PAD, c)] * 2,
        [pltpu.SemaphoreType.DMA((2,))],
        in_specs=[HBM, ANY],
        out_specs=[ANY] * 2,
    )
    right = [(i, (i + 1) % lon_size) for i in range(lon_size)]
    left = [(j, i) for i, j in right]
    from_left = lax.ppermute(last, "lon", right)
    from_right = lax.ppermute(leading, "lon", left)
    own_edge, below = call(
        edge_kernel,
        (from_left, from_right),
        [shape(rows, 2 * PAD, c), shape(HALO, 2 * PAD, c)],
        [],
    )
    down_edge = move(below, False)
    above = call(
        copy_kernel, (own_edge, below), [shape(HALO, 2 * PAD, c)], [], in_specs=[VMEM, ANY]
    )[0]
    up_edge = move(above, True)
    tables = (cells, lon_total, modes, lon_size)
    inverse = call(
        inverse_kernel,
        (np.stack(inverse_parts(*tables)[1:]), phase_table(*tables), above),
        [shape(2, half, 2 * modes)],
        [],
        in_specs=[VMEM, VMEM, ANY],
    )[0]
    forward, leak = forward_table(*tables)
    turn = turn_table(lon_size, local, 1.0 / lon_total)

    line = pltpu.VMEM((2, width, c), F32)
    weights = shape(CONVS, 4 if WINOGRAD else 3, 4 * c, 2 * c)
    lower = [shape(n, wide, 2 * c) for n in (rows + HALO, rows, rows - 2)]
    gathered = pltpu.VMEM((2 * modes, HALO * c), BF)
    upper = [pltpu.VMEM((4, wide, 2 * c), BF)] * 2 + [pltpu.VMEM((rows, half, 2 * c), BF)]
    hidden_shape = shape(rows, half, 2 * c)
    part_shape = [jax.ShapeDtypeStruct((modes, rows * c), F32)] * 2

    own_rows = shape(rows, wide, 2 * c)
    own, packed, later = call(
        prepare_kernel, (field, own_edge, conv_weight), [own_rows, weights, weights], [line]
    )
    low = call(
        first_lower_kernel,
        (down, down_edge, own, packed, conv_bias[0], inverse),
        lower,
        [line],
        in_specs=[VMEM] * 5 + [ANY],
    )
    kept, sent, hidden, to_up, to_down, before = call(
        first_upper_kernel,
        (up, up_edge, *low, packed, conv_bias[0], forward, leak),
        part_shape
        + [hidden_shape]
        + [shape(HALO, half, 2 * c)] * 2
        + [shape(HALO, wide, 2 * c)],
        [line] + upper,
    )
    from_down, from_up = move(to_down, False), move(to_up, True)

    def swap(array, step):
        return lax.ppermute(array, "lon", [(i, i ^ step) for i in range(lon_size)])

    def mix(kept, sent, block):
        chunk = shape(2 * local, rows * c)
        own, *others = call(pair_kernel, (kept, swap(sent, 1)), [chunk] * (lon_size // 2), [])
        sums = [own] + [swap(other, 2 * i + 2) for i, other in enumerate(others)]
        turned = pltpu.VMEM((2 * rows * local, c), F32)
        weights = pl.BlockSpec((1, local, c, c), lambda i: (block, 0, 0, 0))
        (mixed,) = call(
            mix_kernel,
            (turn, spec_real, spec_imag, conv_bias[block], *sums),
            [chunk],
            [turned, turned],
            in_specs=[VMEM, weights, weights] + [VMEM] * (1 + len(sums)),
            grid=(1,),
        )
        return lax.all_gather(mixed, "lon", axis=0, tiled=True)

    mixed = mix(kept, sent, 0)
    halo = call(halo_kernel, (mixed,), [shape(2 * modes, HALO * c)], [])[0]
    lat_size = lax.axis_size("lat")
    ways = []
    for i in range(lon_size):
        for j in range(lat_size - 1):
            here, there = i * lat_size + j, i * lat_size + j + 1
            ways.append((here, there) if i % 2 == 0 else (there, here))
    mine = lax.ppermute(halo, ("lon", "lat"), ways)
    other = swap(mine, 1)
    own = call(middle_own_kernel, (low[0], hidden, mixed, inverse), [own_rows], [])[0]
    state, *low = call(
        middle_lower_kernel,
        (low[0], from_down, mine, other, own, inverse, later, conv_bias[1]),
        lower,
        [gathered],
    )
    kept, sent, hidden = call(
        middle_upper_kernel,
        (before, from_up, mine, other, inverse, state, *low)
        + (later, conv_bias[1], forward, leak),
        part_shape + [hidden_shape],
        [pltpu.VMEM((HALO, wide, 2 * c), BF), gathered] + upper,
    )
    mixed = mix(kept, sent, 1)
    (result,) = call(
        last_kernel, (state, hidden, mixed, inverse), [shape(rows, cells, c)], [line]
    )
    return result


def solution(mesh):
    return jax.shard_map(
        per_device,
        mesh=mesh,
        in_specs=(
            P("lat", "lon", None),
            P(),
            P(),
            P(None, "lon", None, None),
            P(None, "lon", None, None),
        ),
        out_specs=P("lat", "lon", None),
        check_vma=False,
    )
```

```python
import math

import jax
import jax.numpy as jnp
import ml_dtypes
import numpy as np
from jax import lax
from jax.experimental import pallas as pl
from jax.experimental.pallas import tpu as pltpu
from jax.sharding import PartitionSpec as P

BLOCKS = 2
CONVS = 3
PAD = 16
RUNS = 16
HALO = 3
WINOGRAD = True
BF = jnp.bfloat16
F32 = jnp.float32
VMEM = pl.BlockSpec(memory_space=pltpu.VMEM)
ANY = pl.BlockSpec(memory_space=pl.ANY)
HBM = pl.BlockSpec(memory_space=pltpu.HBM)
DMA = pltpu.SemaphoreType.DMA
PARAMS = pltpu.CompilerParams(vmem_limit_bytes=28 << 20)


def odd_lat():
    return lax.rem(lax.axis_index("lat"), 2)


def flip(row, rows):
    return row + odd_lat() * (rows - 1 - 2 * row)


def tile_of(tiles):
    return max(n for n in range(1, 12) if tiles % n == 0) * RUNS


def pack_row(line, wide, row):
    c = line.shape[1]
    run = line.shape[0] // RUNS
    for cell in range(run):
        lanes = slice(cell % 2 * c, (cell % 2 + 1) * c)
        at = RUNS * (cell // 2 + 1)
        wide[row, at : at + RUNS, lanes] = line[pl.ds(cell, RUNS, stride=run), :].astype(BF)


def close_row(wide, row):
    c = wide.shape[2] // 2
    end = wide.shape[1] - RUNS
    before = wide[row, end - RUNS : end, c:].astype(F32)
    wide[row, 0:RUNS, c:] = pltpu.roll(before, 1, 0).astype(BF)
    after = wide[row, RUNS : 2 * RUNS, :c].astype(F32)
    wide[row, end : end + RUNS, :c] = pltpu.roll(after, RUNS - 1, 0).astype(BF)


def build_weights(kernels, block, packed, layer):
    c = kernels.shape[-1]
    zero = jnp.zeros((c, c), BF)
    for tap in range(3):
        g0, g1, g2 = (kernels[block, layer, flip(a, 3), tap].astype(F32) for a in range(3))
        if WINOGRAD:
            outer = g0 + g2
            parts = (0.5 * g0, 0.25 * (outer + g1), 0.25 * (outer - g1), 0.5 * g2)
        else:
            parts = (0.5 * g0, 0.5 * g1, 0.5 * g2)
        for i, part in enumerate(parts):
            value = part.astype(BF)
            for cell in range(2):
                source = cell + tap - 1
                at = {0: 0, 1: c, 2: 2 * c, -1: 3 * c}[source]
                packed[layer, i, at : at + c, cell * c : (cell + 1) * c] = value
    for i in range(packed.shape[1]):
        packed[layer, i, 2 * c : 3 * c, :c] = zero
        packed[layer, i, 3 * c :, c:] = zero


def window(wide, row, start, size):
    c = wide.shape[2] // 2
    here = wide[row, start + RUNS : start + RUNS + size]
    after = wide[row, start + 2 * RUNS : start + 2 * RUNS + size, :c]
    before = wide[row, start : start + size, c:]
    return jnp.concatenate([here, after, before], axis=1)


def dot(a, b):
    return jnp.dot(a, b, preferred_element_type=F32)


def silu_of_half(half):
    return half + half * jnp.tanh(half)


def conv_pair(d, packed, layer):
    if WINOGRAD:
        inputs = (d[0] - d[2], d[1] + d[2], d[2] - d[1], d[1] - d[3])
        m = [dot(x, packed[layer, i]) for i, x in enumerate(inputs)]
        return (m[1] + m[2]) + m[0], m[1] - m[2] - m[3]
    w = jnp.concatenate([packed[layer, i] for i in range(3)], axis=0)
    return tuple(dot(jnp.concatenate(d[i : i + 3], axis=1), w) for i in range(2))


class Rows:
    def __init__(self, *held):
        self.at = {}
        for ref, first in held:
            self.at.update({first + i: (ref, i) for i in range(ref.shape[0])})

    def __getitem__(self, row):
        return self.at[row]


def conv_rows(src, dst, span, layer, packed, bias, edge, rows):
    ref = src[span[0]][0]
    width = ref.shape[1] - 2 * RUNS
    tile = tile_of(width // RUNS)
    both = 0.5 * jnp.concatenate([bias[layer : layer + 1]] * 2, axis=1)
    for pair in range(*span, 2):
        for start in range(0, width, tile):
            sums = conv_pair(
                [window(*src[pair + i - 1], start, tile) for i in range(4)], packed, layer
            )
            for i, total in enumerate(sums):
                row = pair + i
                y = silu_of_half(total + both)
                if row < 0:
                    y = y * edge[0]
                elif row >= rows:
                    y = y * edge[1]
                if callable(dst):
                    dst(row, start, y.astype(BF))
                else:
                    ref, at = dst[row]
                    ref[at, start + RUNS : start + RUNS + tile] = y.astype(BF)
        if not callable(dst):
            for i in range(2):
                close_row(*dst[pair + i])


def transform(forward, leak, bias, held, kept, sent):
    core = lax.rem(lax.axis_index("lon"), 2)
    rows, c = held.shape[0], held.shape[2] // 2
    half = 0.5 * bias[CONVS - 1 : CONVS]
    level = silu_of_half(half)
    for row in range(0, rows, 2):
        cells = [
            jnp.concatenate([held[row + i, :, e * c : (e + 1) * c] for i in range(2)], axis=1)
            for e in range(2)
        ]
        both = dot(forward[core], jnp.concatenate(cells, axis=0))
        modes2 = both.shape[0] // 2
        total = both[:modes2] + both[modes2:]
        total = total - leak[core] * jnp.concatenate([level, level], axis=1)
        lanes = slice(row * c, (row + 2) * c)
        kept[:, lanes] = total[: modes2 // 2]
        sent[:, lanes] = total[modes2 // 2 :]


def pack_cells(body, ends, source, line, wide, at):
    cells = body.shape[1]
    line[0:PAD] = ends[source, :PAD].astype(F32)
    line[PAD : PAD + cells] = body[source].astype(F32)
    line[PAD + cells :] = ends[source, PAD:].astype(F32)
    pack_row(line, wide, at)
    close_row(wide, at)


def lower_part(field, first, second, packed, bias, edge, rows):
    x, y, z = Rows((field, 0)), Rows((first, 2)), Rows((second, 3))
    conv_rows(x, y, (2, rows + 2), 0, packed, bias, edge, rows)
    conv_rows(y, z, (3, rows + 1), 1, packed, bias, edge, rows)


def upper_part(before, field, first, second, more, packed, bias, edge, emit):
    rows = field.shape[0] - HALO
    x = Rows((before, -HALO), (field, 0))
    y = Rows((more[0], -2), (first, 2))
    z = Rows((more[1], -1), (second, 3))
    conv_rows(x, y, (-2, 2), 0, packed, bias, edge, rows)
    conv_rows(y, z, (-1, 3), 1, packed, bias, edge, rows)
    conv_rows(z, emit, (0, rows), 2, packed, bias, edge, rows)


def prepare_kernel(own, own_edge, kernels, field, packed, later, line):
    rows = own.shape[0]
    for layer in range(CONVS):
        build_weights(kernels, 0, packed, layer)
        build_weights(kernels, 1, later, layer)
    for row in range(rows):
        pack_cells(own, own_edge, flip(row, rows), line.at[row % 2], field, row)


def first_lower_kernel(down, down_edge, own, packed, bias, after, field, first, second, line):
    rows = own.shape[0]
    field[:rows] = own[...]
    for row in range(HALO):
        pack_cells(down, down_edge, flip(row, HALO), line.at[row % 2], field, rows + row)
    lower_part(field, first, second, packed, bias, lat_edges(), rows)


def first_upper_kernel(
    up, up_edge, field, first, second, packed, bias, forward, leak,
    kept, sent, hidden, to_partner, to_other, before,
    line, more, most, held,
):
    rows = field.shape[0] - HALO
    for row in range(HALO):
        pack_cells(up, up_edge, flip(row, HALO), line.at[row % 2], before, row)

    def emit(row, start, y):
        span = slice(start, start + y.shape[0])
        held[row, span] = y
        hidden[row, span] = y
        if row < HALO:
            to_other[HALO - 1 - row, span] = y
        if row >= rows - HALO:
            to_partner[rows - 1 - row, span] = y

    upper_part(before, field, first, second, (more, most), packed, bias, lat_edges(), emit)
    transform(forward, leak, bias, held, kept, sent)


def pair_kernel(kept, got, *outs):
    chip = lax.div(lax.axis_index("lon"), 2)
    rows = outs[0].shape[0]
    for step, out in enumerate(outs):
        span = pl.ds(pl.multiple_of((chip ^ step) * rows, rows), rows)
        out[...] = (kept[span, :] + got[span, :]).astype(BF)


def mix_kernel(turn, real, imag, bias, *rest):
    *sums, mixed, spread_in, spread_out = rest
    me = lax.axis_index("lon")
    modes, c = real.shape[1], real.shape[2]
    summed = dot(turn[me], jnp.concatenate([x[...] for x in sums], axis=0))
    summed = summed[: 2 * modes] + summed[2 * modes :]
    rows = summed.shape[1] // c
    level = (me == 0).astype(F32) * silu_of_half(0.5 * bias[CONVS - 1 : CONVS])
    for half in range(2):
        for row in range(rows):
            spread_in[pl.ds(half * rows + row, modes, stride=2 * rows), :] = summed[
                half * modes : (half + 1) * modes, row * c : (row + 1) * c
            ]
    spread_in[0:rows] = spread_in[0:rows] + level
    sign = jnp.where(lax.broadcasted_iota(jnp.int32, (2 * rows, c), 0) < rows, -1.0, 1.0)
    for k in range(modes):
        wide = spread_in[2 * rows * k : 2 * rows * (k + 1)]
        high = wide.astype(BF)
        low = (wide - high.astype(F32)).astype(BF)
        both = jnp.concatenate([high, low], axis=0)
        weight = jnp.concatenate([real[0, k], imag[0, k]], axis=1)
        out = jnp.dot(both, weight, preferred_element_type=F32)
        out = out[: 2 * rows] + out[2 * rows :]
        turned = pltpu.roll(out[:, c:], rows, 0)
        spread_out[2 * rows * k : 2 * rows * (k + 1)] = out[:, :c] + sign * turned
    for half in range(2):
        for row in range(rows):
            value = spread_out[pl.ds(half * rows + row, modes, stride=2 * rows), :].astype(BF)
            span = slice(half * modes, (half + 1) * modes)
            mixed[span, row * c : (row + 1) * c] = value


def halo_kernel(mixed, out):
    c = out.shape[1] // HALO
    rows = mixed.shape[1] // c
    even = lax.rem(lax.axis_index("lon"), 2) == 0
    for at in range(HALO):
        last = mixed[:, (rows - 1 - at) * c : (rows - at) * c]
        leading = mixed[:, (HALO - 1 - at) * c : (HALO - at) * c]
        out[:, at * c : (at + 1) * c] = jnp.where(even, last, leading)


def pick(mine, other, first):
    even = lax.rem(lax.axis_index("lon"), 2) == 0
    return jnp.where(even == first, mine[...], other[...])


def next_state(old, conv, mixed, inverse, new, at, count, mask):
    c = mixed.shape[1] // conv[0].shape[0]
    width = conv[0].shape[1]
    tile = tile_of(width // RUNS)
    for pair in range(0, count, 2):
        lanes = slice(pair * c, min(pair + 2, count) * c)
        for start in range(0, width, tile):
            span = slice(start, start + tile)
            wide = slice(start + RUNS, start + RUNS + tile)
            waves = [dot(inverse[e, span], mixed[:, lanes]) for e in range(2)]
            for i in range(min(2, count - pair)):
                wave = jnp.concatenate([w[:, i * c : (i + 1) * c] for w in waves], axis=1)
                total = old[0][old[1] + pair + i, wide].astype(F32)
                total = total + conv[0][pair + i, span].astype(F32) + wave
                total = jnp.tanh(total)
                if mask is not None:
                    total = total * mask
                new[at + pair + i, wide] = total.astype(BF)
        for i in range(min(2, count - pair)):
            close_row(new, at + pair + i)


def middle_own_kernel(field, hidden, mixed, inverse, state):
    next_state((field, 0), (hidden,), mixed, inverse, state, 0, hidden.shape[0], None)


def middle_lower_kernel(
    field, from_down, mine, other, own, inverse, packed, bias, state, first, second, mixed_down
):
    rows = own.shape[0]
    edge = lat_edges()
    state[:rows] = own[...]
    mixed_down[...] = pick(mine, other, True)
    next_state((field, rows), (from_down,), mixed_down, inverse, state, rows, HALO, edge[1])
    lower_part(state, first, second, packed, bias, edge, rows)


def middle_upper_kernel(
    before, from_up, mine, other, inverse, state, first, second, packed, bias, forward, leak,
    kept, sent, hidden, above, mixed_up, more, most, held,
):
    edge = lat_edges()
    mixed_up[...] = pick(mine, other, False)
    next_state((before, 0), (from_up,), mixed_up, inverse, above, 0, HALO, edge[0])

    def emit(row, start, y):
        span = slice(start, start + y.shape[0])
        held[row, span] = y
        hidden[row, span] = y

    upper_part(above, state, first, second, (more, most), packed, bias, edge, emit)
    transform(forward, leak, bias, held, kept, sent)


def last_kernel(state, hidden, mixed, inverse, result, line):
    rows, width, c = hidden.shape[0], hidden.shape[1], hidden.shape[2] // 2
    cells = result.shape[1]
    run = 2 * width // RUNS
    for pair in range(0, rows, 2):
        waves = [dot(inverse[e], mixed[:, pair * c : (pair + 2) * c]) for e in range(2)]
        for i in range(2):
            row = pair + i
            for e in range(2):
                lanes = slice(e * c, (e + 1) * c)
                total = state[row, RUNS : RUNS + width, lanes].astype(F32) + hidden[row, :, lanes].astype(F32)
                total = jnp.tanh(total + waves[e][:, i * c : (i + 1) * c])
                for u in range(width // RUNS):
                    value = total[u * RUNS : (u + 1) * RUNS]
                    line[i, pl.ds(2 * u + e, RUNS, stride=run), :] = value
            result[flip(row, rows)] = line[i, PAD : PAD + cells].astype(BF)


def cell_order(width):
    run = width // RUNS
    cell = np.arange(width // 2) // RUNS * 2 + np.arange(width // 2) % RUNS * run
    return np.stack([cell, cell + 1])


def forward_table(cells, lon_total, modes, lon_size):
    order = cell_order(cells + 2 * PAD).reshape(-1) - PAD
    inside = (order >= 0) & (order < cells)
    waves = np.arange(modes)
    tables, leaks = [], []
    for core in range(2):
        theta = (2 * np.pi / lon_total) * (np.outer(waves, order + core * cells) % lon_total)
        full = np.stack([np.cos(theta), -np.sin(theta)], 0) * inside
        full = full.reshape(2, lon_size // 2, 2, modes // lon_size, -1)
        full = full.transpose(2, 1, 0, 3, 4)[[core, 1 - core]]
        full = full.reshape(2 * modes, -1).astype(np.float32)
        leaks.append(full.astype(np.float64).sum(1, keepdims=True).astype(np.float32))
        high = full.astype(ml_dtypes.bfloat16)
        low = (full - high.astype(np.float32)).astype(ml_dtypes.bfloat16)
        tables.append(np.concatenate([high, low], 0))
    return np.stack(tables), np.stack(leaks)


def turn_table(lon_size, local, scale):
    chips = lon_size // 2
    me = np.arange(lon_size)[:, None, None]
    waves = me * local + np.arange(local)[:, None]
    source = 2 * ((me // 2) ^ np.arange(chips))
    phase = source * waves % lon_size * (2 * np.pi / lon_size)
    cos, sin = scale * np.cos(phase), scale * np.sin(phase)
    eye = np.eye(local)
    cos, sin = (x[:, :, :, None] * eye[:, None, :] for x in (cos, sin))
    real = np.stack([cos, sin], axis=3)
    imag = np.stack([-sin, cos], axis=3)
    full = np.concatenate([real, imag], axis=1)
    full = full.reshape(lon_size, 2 * local, chips * 2 * local).astype(np.float32)
    high = full.astype(ml_dtypes.bfloat16)
    low = (full - high.astype(np.float32)).astype(ml_dtypes.bfloat16)
    return np.concatenate([high, low], axis=1)


def inverse_parts(cells, lon_total, modes, lon_size):
    column = np.arange(2 * modes)
    local = modes // lon_size
    waves = column // (2 * local) * local + column % local
    imaginary = column // local % 2 == 1
    order = cell_order(cells + 2 * PAD) - PAD
    theta = (2 * np.pi / lon_total) * (order[:, :, None] * waves % lon_total)
    weight = np.where(waves == 0, 1.0, 2.0)
    cos, sin = weight * np.cos(theta), weight * np.sin(theta)
    by_cos = np.where(imaginary, -sin, cos).astype(np.float32)
    by_sin = np.where(imaginary, -cos, -sin).astype(np.float32)
    return waves.astype(np.int32), by_cos, by_sin


def phase_table(cells, lon_total, modes, lon_size):
    waves = inverse_parts(cells, lon_total, modes, lon_size)[0]
    phase = np.arange(lon_size)[:, None] * waves % lon_size * (2 * np.pi / lon_size)
    return np.stack([np.cos(phase), np.sin(phase)], 1).astype(np.float32)


def facing(rows, partner):
    odd = odd_lat()
    return (rows - HALO) * ((1 - odd) if partner else odd)


def slice_kernel(field, *rest):
    out, sem = rest[-2:]
    at = facing(field.shape[0], len(rest) == 2)
    copy = pltpu.make_async_copy(field.at[pl.ds(at, HALO)], out, sem)
    copy.start()
    copy.wait()


def side_kernel(field, after, last, leading, sems):
    cells = field.shape[1]
    first = pltpu.make_async_copy(field.at[:, cells - PAD :], last, sems.at[0])
    second = pltpu.make_async_copy(field.at[:, :PAD], leading, sems.at[1])
    first.start()
    second.start()
    first.wait()
    second.wait()


def edge_kernel(from_left, from_right, edges, near):
    rows = from_left.shape[0]
    for row in range(rows):
        edges[row] = jnp.concatenate([from_left[row], from_right[row]], axis=0)
    at = facing(rows, True)
    for row in range(HALO):
        near[row] = jnp.concatenate([from_left[at + row], from_right[at + row]], axis=0)


def copy_kernel(edges, near, other):
    at = facing(edges.shape[0], False)
    for row in range(HALO):
        other[row] = edges[at + row]


def inverse_kernel(parts, phase, after, inverse):
    turn = phase[lax.axis_index("lon")]
    for e in range(2):
        inverse[e] = (parts[0, e] * turn[0:1] + parts[1, e] * turn[1:2]).astype(BF)


def lat_edges():
    me, size, odd = lax.axis_index("lat"), lax.axis_size("lat"), odd_lat()
    after, before = (me < size - 1).astype(F32), (me > 0).astype(F32)
    even = (1 - odd).astype(F32)
    return [even * before + (1.0 - even) * after, even * after + (1.0 - even) * before]


def lat_pairs(partner):
    pairs = [(i, i + 1) for i in range(0 if partner else 1, lax.axis_size("lat") - 1, 2)]
    return pairs + [(j, i) for i, j in pairs]


def move(array, partner):
    return lax.ppermute(array, "lat", lat_pairs(partner))


def shape(*dims):
    return jax.ShapeDtypeStruct(dims, BF)


def call(kernel, args, outs, scratch, in_specs=None, out_specs=None, grid=()):
    return pl.pallas_call(
        kernel,
        grid=grid,
        out_shape=outs,
        in_specs=in_specs or [VMEM] * len(args),
        out_specs=out_specs or [VMEM] * len(outs),
        scratch_shapes=scratch,
        compiler_params=PARAMS,
    )(*(jnp.asarray(arg) for arg in args))


def per_device(field, conv_weight, conv_bias, spec_real, spec_imag):
    rows, cells, c = field.shape
    width = cells + 2 * PAD
    half = width // 2
    lon_size = lax.axis_size("lon")
    lon_total = cells * lon_size
    local = spec_real.shape[1]
    modes = local * lon_size

    wide = half + 2 * RUNS
    below = call(
        slice_kernel, (field,), [shape(HALO, cells, c)], [DMA], in_specs=[HBM], out_specs=[ANY]
    )[0]
    down = move(below, True)
    above = call(
        slice_kernel,
        (field, below),
        [shape(HALO, cells, c)],
        [DMA],
        in_specs=[HBM, ANY],
        out_specs=[ANY],
    )[0]
    up = move(above, False)
    last, leading = call(
        side_kernel,
        (field, above),
        [shape(rows, PAD, c)] * 2,
        [pltpu.SemaphoreType.DMA((2,))],
        in_specs=[HBM, ANY],
        out_specs=[ANY] * 2,
    )
    right = [(i, (i + 1) % lon_size) for i in range(lon_size)]
    left = [(j, i) for i, j in right]
    from_left = lax.ppermute(last, "lon", right)
    from_right = lax.ppermute(leading, "lon", left)
    own_edge, below = call(
        edge_kernel,
        (from_left, from_right),
        [shape(rows, 2 * PAD, c), shape(HALO, 2 * PAD, c)],
        [],
    )
    down_edge = move(below, True)
    above = call(
        copy_kernel, (own_edge, below), [shape(HALO, 2 * PAD, c)], [], in_specs=[VMEM, ANY]
    )[0]
    up_edge = move(above, False)
    tables = (cells, lon_total, modes, lon_size)
    inverse = call(
        inverse_kernel,
        (np.stack(inverse_parts(*tables)[1:]), phase_table(*tables), above),
        [shape(2, half, 2 * modes)],
        [],
        in_specs=[VMEM, VMEM, ANY],
    )[0]
    forward, leak = forward_table(*tables)
    turn = turn_table(lon_size, local, 1.0 / lon_total)

    line = pltpu.VMEM((2, width, c), F32)
    weights = shape(CONVS, 4 if WINOGRAD else 3, 4 * c, 2 * c)
    lower = [shape(n, wide, 2 * c) for n in (rows + HALO, rows, rows - 2)]
    gathered = pltpu.VMEM((2 * modes, HALO * c), BF)
    upper = [pltpu.VMEM((4, wide, 2 * c), BF)] * 2 + [pltpu.VMEM((rows, half, 2 * c), BF)]
    hidden_shape = shape(rows, half, 2 * c)
    part_shape = [jax.ShapeDtypeStruct((modes, rows * c), F32)] * 2

    own_rows = shape(rows, wide, 2 * c)
    own, packed, later = call(
        prepare_kernel, (field, own_edge, conv_weight), [own_rows, weights, weights], [line]
    )
    low = call(
        first_lower_kernel,
        (down, down_edge, own, packed, conv_bias[0], inverse),
        lower,
        [line],
        in_specs=[VMEM] * 5 + [ANY],
    )
    kept, sent, hidden, to_partner, to_other, before = call(
        first_upper_kernel,
        (up, up_edge, *low, packed, conv_bias[0], forward, leak),
        part_shape
        + [hidden_shape]
        + [shape(HALO, half, 2 * c)] * 2
        + [shape(HALO, wide, 2 * c)],
        [line] + upper,
    )
    from_down, from_up = move(to_partner, True), move(to_other, False)

    def swap(array, step):
        return lax.ppermute(array, "lon", [(i, i ^ step) for i in range(lon_size)])

    def mix(kept, sent, block):
        chunk = shape(2 * local, rows * c)
        own, *others = call(pair_kernel, (kept, swap(sent, 1)), [chunk] * (lon_size // 2), [])
        sums = [own] + [swap(other, 2 * i + 2) for i, other in enumerate(others)]
        turned = pltpu.VMEM((2 * rows * local, c), F32)
        weights = pl.BlockSpec((1, local, c, c), lambda i: (block, 0, 0, 0))
        (mixed,) = call(
            mix_kernel,
            (turn, spec_real, spec_imag, conv_bias[block], *sums),
            [chunk],
            [turned, turned],
            in_specs=[VMEM, weights, weights] + [VMEM] * (1 + len(sums)),
            grid=(1,),
        )
        return lax.all_gather(mixed, "lon", axis=0, tiled=True)

    mixed = mix(kept, sent, 0)
    halo = call(halo_kernel, (mixed,), [shape(2 * modes, HALO * c)], [])[0]
    lat_size = lax.axis_size("lat")
    ways = []
    for i in range(lon_size):
        ways += [(i * lat_size + j, i * lat_size + k) for j, k in lat_pairs(i % 2 == 0)]
    mine = lax.ppermute(halo, ("lon", "lat"), ways)
    other = swap(mine, 1)
    own = call(middle_own_kernel, (low[0], hidden, mixed, inverse), [own_rows], [])[0]
    state, *low = call(
        middle_lower_kernel,
        (low[0], from_down, mine, other, own, inverse, later, conv_bias[1]),
        lower,
        [gathered],
    )
    kept, sent, hidden = call(
        middle_upper_kernel,
        (before, from_up, mine, other, inverse, state, *low)
        + (later, conv_bias[1], forward, leak),
        part_shape + [hidden_shape],
        [pltpu.VMEM((HALO, wide, 2 * c), BF), gathered] + upper,
    )
    mixed = mix(kept, sent, 1)
    (result,) = call(
        last_kernel, (state, hidden, mixed, inverse), [shape(rows, cells, c)], [line]
    )
    return result


def solution(mesh):
    return jax.shard_map(
        per_device,
        mesh=mesh,
        in_specs=(
            P("lat", "lon", None),
            P(),
            P(),
            P(None, "lon", None, None),
            P(None, "lon", None, None),
        ),
        out_specs=P("lat", "lon", None),
        check_vma=False,
    )
```

```python
import math

import jax
import jax.numpy as jnp
import ml_dtypes
import numpy as np
from jax import lax
from jax.experimental import pallas as pl
from jax.experimental.pallas import tpu as pltpu
from jax.sharding import PartitionSpec as P

BLOCKS = 2
CONVS = 3
PAD = 16
RUNS = 16
HALO = 3
WINOGRAD = True
BF = jnp.bfloat16
F32 = jnp.float32
VMEM = pl.BlockSpec(memory_space=pltpu.VMEM)
ANY = pl.BlockSpec(memory_space=pl.ANY)
HBM = pl.BlockSpec(memory_space=pltpu.HBM)
DMA = pltpu.SemaphoreType.DMA
PARAMS = pltpu.CompilerParams(vmem_limit_bytes=28 << 20)


def odd_lat():
    return lax.rem(lax.axis_index("lat"), 2)


def flip(row, rows):
    return row + odd_lat() * (rows - 1 - 2 * row)


def tile_of(tiles):
    return max(n for n in range(1, 34) if tiles % n == 0) * RUNS


def pack_row(line, wide, row):
    c = line.shape[1]
    run = line.shape[0] // RUNS
    for cell in range(run):
        lanes = slice(cell % 2 * c, (cell % 2 + 1) * c)
        at = RUNS * (cell // 2 + 1)
        wide[row, at : at + RUNS, lanes] = line[pl.ds(cell, RUNS, stride=run), :].astype(BF)


def close_row(wide, row):
    c = wide.shape[2] // 2
    end = wide.shape[1] - RUNS
    before = wide[row, end - RUNS : end, c:].astype(F32)
    wide[row, 0:RUNS, c:] = pltpu.roll(before, 1, 0).astype(BF)
    after = wide[row, RUNS : 2 * RUNS, :c].astype(F32)
    wide[row, end : end + RUNS, :c] = pltpu.roll(after, RUNS - 1, 0).astype(BF)


def build_weights(kernels, block, packed, layer):
    c = kernels.shape[-1]
    zero = jnp.zeros((c, c), BF)
    for tap in range(3):
        g0, g1, g2 = (kernels[block, layer, flip(a, 3), tap].astype(F32) for a in range(3))
        if WINOGRAD:
            outer = g0 + g2
            parts = (0.5 * g0, 0.25 * (outer + g1), 0.25 * (outer - g1), 0.5 * g2)
        else:
            parts = (0.5 * g0, 0.5 * g1, 0.5 * g2)
        for i, part in enumerate(parts):
            value = part.astype(BF)
            for cell in range(2):
                source = cell + tap - 1
                at = {0: 0, 1: c, 2: 2 * c, -1: 3 * c}[source]
                packed[layer, i, at : at + c, cell * c : (cell + 1) * c] = value
    for i in range(packed.shape[1]):
        packed[layer, i, 2 * c : 3 * c, :c] = zero
        packed[layer, i, 3 * c :, c:] = zero


def window(wide, row, start, size):
    c = wide.shape[2] // 2
    here = wide[row, start + RUNS : start + RUNS + size]
    after = wide[row, start + 2 * RUNS : start + 2 * RUNS + size, :c]
    before = wide[row, start : start + size, c:]
    return jnp.concatenate([here, after, before], axis=1)


def dot(a, b):
    return jnp.dot(a, b, preferred_element_type=F32)


def silu_of_half(half):
    return half + half * jnp.tanh(half)


def conv_pair(d, packed, layer):
    if WINOGRAD:
        inputs = (d[0] - d[2], d[1] + d[2], d[2] - d[1], d[1] - d[3])
        m = [dot(x, packed[layer, i]) for i, x in enumerate(inputs)]
        return (m[1] + m[2]) + m[0], m[1] - m[2] - m[3]
    w = jnp.concatenate([packed[layer, i] for i in range(3)], axis=0)
    return tuple(dot(jnp.concatenate(d[i : i + 3], axis=1), w) for i in range(2))


class Rows:
    def __init__(self, *held):
        self.at = {}
        for ref, first in held:
            self.at.update({first + i: (ref, i) for i in range(ref.shape[0])})

    def __getitem__(self, row):
        return self.at[row]


def conv_rows(src, dst, span, layer, packed, bias, edge, rows):
    ref = src[span[0]][0]
    width = ref.shape[1] - 2 * RUNS
    tile = tile_of(width // RUNS)
    both = 0.5 * jnp.concatenate([bias[layer : layer + 1]] * 2, axis=1)
    for pair in range(*span, 2):
        for start in range(0, width, tile):
            sums = conv_pair(
                [window(*src[pair + i - 1], start, tile) for i in range(4)], packed, layer
            )
            for i, total in enumerate(sums):
                row = pair + i
                y = silu_of_half(total + both)
                if row < 0:
                    y = y * edge[0]
                elif row >= rows:
                    y = y * edge[1]
                if callable(dst):
                    dst(row, start, y.astype(BF))
                else:
                    ref, at = dst[row]
                    ref[at, start + RUNS : start + RUNS + tile] = y.astype(BF)
        if not callable(dst):
            for i in range(2):
                close_row(*dst[pair + i])


def transform(forward, leak, bias, held, kept, sent):
    core = lax.rem(lax.axis_index("lon"), 2)
    rows, c = held.shape[0], held.shape[2] // 2
    half = 0.5 * bias[CONVS - 1 : CONVS]
    level = silu_of_half(half)
    for row in range(0, rows, 2):
        cells = [
            jnp.concatenate([held[row + i, :, e * c : (e + 1) * c] for i in range(2)], axis=1)
            for e in range(2)
        ]
        total = dot(forward[core], jnp.concatenate(cells, axis=0))
        modes2 = total.shape[0]
        total = total - leak[core] * jnp.concatenate([level, level], axis=1)
        lanes = slice(row * c, (row + 2) * c)
        kept[:, lanes] = total[: modes2 // 2]
        sent[:, lanes] = total[modes2 // 2 :]


def pack_cells(body, ends, source, line, wide, at):
    cells = body.shape[1]
    line[0:PAD] = ends[source, :PAD].astype(F32)
    line[PAD : PAD + cells] = body[source].astype(F32)
    line[PAD + cells :] = ends[source, PAD:].astype(F32)
    pack_row(line, wide, at)
    close_row(wide, at)


def product(a, b, sign, start, tile, packed, layer, index):
    left, right = window(*a, start, tile), window(*b, start, tile)
    return dot(left + right if sign > 0 else left - right, packed[layer, index])


def put(dst, start, half, bias, layer):
    ref, at = dst
    both = 0.5 * jnp.concatenate([bias[layer : layer + 1]] * 2, axis=1)
    y = silu_of_half(half + both).astype(BF)
    ref[at, start + RUNS : start + RUNS + y.shape[0]] = y


def spans(ref):
    width = ref.shape[1] - 2 * RUNS
    tile = tile_of(width // RUNS)
    return [(start, tile) for start in range(0, width, tile)]


def early_part(field, inner, sums, packed, bias):
    x, y = Rows((field, 0)), Rows((inner, 1))
    for start, tile in spans(field):
        span = slice(start, start + tile)
        args = (start, tile, packed, 0)
        m1 = product(x[0], x[1], 1, *args, 1)
        m2 = product(x[1], x[0], -1, *args, 2)
        m3 = product(x[0], x[2], -1, *args, 3)
        sums[0, span] = m1 + m2
        put(y[1], start, m1 - m2 - m3, bias, 0)
        m0 = product(x[1], x[3], -1, *args, 0)
        m1 = product(x[2], x[3], 1, *args, 1)
        m2 = product(x[3], x[2], -1, *args, 2)
        sums[1, span] = m1 - m2
        put(y[2], start, (m1 + m2) + m0, bias, 0)
    close_row(*y[1])
    close_row(*y[2])
    for start, tile in spans(field):
        span = slice(start, start + tile)
        args = (start, tile, packed, 1)
        m1 = product(y[1], y[2], 1, *args, 1)
        m2 = product(y[2], y[1], -1, *args, 2)
        sums[2, span] = m1 + m2
        sums[3, span] = m1 - m2


def lower_part(field, inner, sums, first, second, packed, bias, edge, rows):
    x, y, z = Rows((field, 0)), Rows((inner, 1), (first, 3)), Rows((second, 3))
    for start, tile in spans(field):
        m3 = product(x[2], x[4], -1, start, tile, packed, 0, 3)
        put(y[3], start, sums[1, start : start + tile] - m3, bias, 0)
    close_row(*y[3])
    conv_rows(x, y, (4, 6), 0, packed, bias, edge, rows)
    conv_rows(y, z, (3, 5), 1, packed, bias, edge, rows)


def upper_part(before, field, inner, sums, first, second, more, packed, bias, edge, emit):
    rows = field.shape[0] - HALO
    x = Rows((before, -HALO), (field, 0))
    y = Rows((more[0], -2), (inner, 1), (first, 3))
    z = Rows((more[1], -1), (second, 3))
    conv_rows(x, y, (-2, 0), 0, packed, bias, edge, rows)
    for start, tile in spans(field):
        m0 = product(x[-1], x[1], -1, start, tile, packed, 0, 0)
        put(y[0], start, sums[0, start : start + tile] + m0, bias, 0)
    close_row(*y[0])
    conv_rows(y, z, (-1, 1), 1, packed, bias, edge, rows)
    for start, tile in spans(field):
        span = slice(start, start + tile)
        m0 = product(y[0], y[2], -1, start, tile, packed, 1, 0)
        m3 = product(y[1], y[3], -1, start, tile, packed, 1, 3)
        put(z[1], start, sums[2, span] + m0, bias, 1)
        put(z[2], start, sums[3, span] - m3, bias, 1)
    close_row(*z[1])
    close_row(*z[2])
    conv_rows(z, emit, (0, rows), 2, packed, bias, edge, rows)


def prepare_kernel(own, own_edge, kernels, bias, after, field, packed, later, inner, sums, line):
    rows = own.shape[0]
    for layer in range(CONVS):
        build_weights(kernels, 0, packed, layer)
        build_weights(kernels, 1, later, layer)
    for row in range(rows):
        pack_cells(own, own_edge, flip(row, rows), line.at[row % 2], field, row)
    early_part(field, inner, sums, packed, bias)


def first_lower_kernel(
    down, down_edge, own, packed, inner, sums, bias, field, first, second, line
):
    rows = own.shape[0]
    field[:rows] = own[...]
    for row in range(HALO):
        pack_cells(down, down_edge, flip(row, HALO), line.at[row % 2], field, rows + row)
    lower_part(field, inner, sums, first, second, packed, bias, lat_edges(), rows)


def first_upper_kernel(
    up, up_edge, field, first, second, inner, sums, packed, bias, forward, leak,
    kept, sent, hidden, to_partner, to_other, before,
    line, more, most, held,
):
    rows = field.shape[0] - HALO
    for row in range(HALO):
        pack_cells(up, up_edge, flip(row, HALO), line.at[row % 2], before, row)

    def emit(row, start, y):
        span = slice(start, start + y.shape[0])
        held[row, span] = y
        hidden[row, span] = y
        if row < HALO:
            to_other[HALO - 1 - row, span] = y
        if row >= rows - HALO:
            to_partner[rows - 1 - row, span] = y

    args = (before, field, inner, sums, first, second, (more, most), packed, bias)
    upper_part(*args, lat_edges(), emit)
    transform(forward, leak, bias, held, kept, sent)


def pair_kernel(kept, got, *outs):
    chip = lax.div(lax.axis_index("lon"), 2)
    rows = outs[0].shape[0]
    for step, out in enumerate(outs):
        span = pl.ds(pl.multiple_of((chip ^ step) * rows, rows), rows)
        out[...] = (kept[span, :] + got[span, :]).astype(BF)


def mix_kernel(turn, real, imag, bias, *rest):
    *sums, mixed, spread_in, spread_out = rest
    me = lax.axis_index("lon")
    modes, c = real.shape[1], real.shape[2]
    summed = dot(turn[me], jnp.concatenate([x[...] for x in sums], axis=0))
    summed = summed[: 2 * modes] + summed[2 * modes :]
    rows = summed.shape[1] // c
    level = (me == 0).astype(F32) * silu_of_half(0.5 * bias[CONVS - 1 : CONVS])
    for half in range(2):
        for row in range(rows):
            spread_in[pl.ds(half * rows + row, modes, stride=2 * rows), :] = summed[
                half * modes : (half + 1) * modes, row * c : (row + 1) * c
            ]
    spread_in[0:rows] = spread_in[0:rows] + level
    sign = jnp.where(lax.broadcasted_iota(jnp.int32, (2 * rows, c), 0) < rows, -1.0, 1.0)
    for k in range(modes):
        wide = spread_in[2 * rows * k : 2 * rows * (k + 1)]
        high = wide.astype(BF)
        low = (wide - high.astype(F32)).astype(BF)
        both = jnp.concatenate([high, low], axis=0)
        weight = jnp.concatenate([real[0, k], imag[0, k]], axis=1)
        out = jnp.dot(both, weight, preferred_element_type=F32)
        out = out[: 2 * rows] + out[2 * rows :]
        turned = pltpu.roll(out[:, c:], rows, 0)
        spread_out[2 * rows * k : 2 * rows * (k + 1)] = out[:, :c] + sign * turned
    for half in range(2):
        for row in range(rows):
            value = spread_out[pl.ds(half * rows + row, modes, stride=2 * rows), :].astype(BF)
            span = slice(half * modes, (half + 1) * modes)
            mixed[span, row * c : (row + 1) * c] = value


def halo_kernel(mixed, out):
    c = out.shape[1] // HALO
    rows = mixed.shape[1] // c
    even = lax.rem(lax.axis_index("lon"), 2) == 0
    for at in range(HALO):
        last = mixed[:, (rows - 1 - at) * c : (rows - at) * c]
        leading = mixed[:, (HALO - 1 - at) * c : (HALO - at) * c]
        out[:, at * c : (at + 1) * c] = jnp.where(even, last, leading)


def pick(mine, other, first):
    even = lax.rem(lax.axis_index("lon"), 2) == 0
    return jnp.where(even == first, mine[...], other[...])


def next_state(old, conv, mixed, inverse, new, at, count, mask):
    c = mixed.shape[1] // conv[0].shape[0]
    width = conv[0].shape[1]
    tile = tile_of(width // RUNS)
    for pair in range(0, count, 2):
        lanes = slice(pair * c, min(pair + 2, count) * c)
        for start in range(0, width, tile):
            span = slice(start, start + tile)
            wide = slice(start + RUNS, start + RUNS + tile)
            waves = [dot(inverse[e, span], mixed[:, lanes]) for e in range(2)]
            for i in range(min(2, count - pair)):
                wave = jnp.concatenate([w[:, i * c : (i + 1) * c] for w in waves], axis=1)
                total = old[0][old[1] + pair + i, wide].astype(F32)
                total = total + conv[0][pair + i, span].astype(F32) + wave
                total = jnp.tanh(total)
                if mask is not None:
                    total = total * mask
                new[at + pair + i, wide] = total.astype(BF)
        for i in range(min(2, count - pair)):
            close_row(new, at + pair + i)


def middle_own_kernel(field, hidden, mixed, inverse, packed, bias, state, inner, sums):
    next_state((field, 0), (hidden,), mixed, inverse, state, 0, hidden.shape[0], None)
    early_part(state, inner, sums, packed, bias)


def middle_lower_kernel(
    field, from_down, mine, other, own, inner, sums, inverse, packed, bias,
    state, first, second, mixed_down,
):
    rows = own.shape[0]
    edge = lat_edges()
    state[:rows] = own[...]
    mixed_down[...] = pick(mine, other, True)
    next_state((field, rows), (from_down,), mixed_down, inverse, state, rows, HALO, edge[1])
    lower_part(state, inner, sums, first, second, packed, bias, edge, rows)


def middle_upper_kernel(
    before, from_up, mine, other, inverse, state, first, second, inner, sums,
    packed, bias, forward, leak,
    kept, sent, hidden, above, mixed_up, more, most, held,
):
    edge = lat_edges()
    mixed_up[...] = pick(mine, other, False)
    next_state((before, 0), (from_up,), mixed_up, inverse, above, 0, HALO, edge[0])

    def emit(row, start, y):
        span = slice(start, start + y.shape[0])
        held[row, span] = y
        hidden[row, span] = y

    args = (above, state, inner, sums, first, second, (more, most), packed, bias)
    upper_part(*args, edge, emit)
    transform(forward, leak, bias, held, kept, sent)


def last_kernel(state, hidden, mixed, inverse, result, line, done, sems):
    rows, width, c = hidden.shape[0], hidden.shape[1], hidden.shape[2] // 2
    cells = result.shape[1]
    run = 2 * width // RUNS
    copies = []
    for pair in range(0, rows, 2):
        waves = [dot(inverse[e], mixed[:, pair * c : (pair + 2) * c]) for e in range(2)]
        for i in range(2):
            row = pair + i
            for e in range(2):
                lanes = slice(e * c, (e + 1) * c)
                total = state[row, RUNS : RUNS + width, lanes].astype(F32) + hidden[row, :, lanes].astype(F32)
                total = jnp.tanh(total + waves[e][:, i * c : (i + 1) * c])
                for u in range(width // RUNS):
                    value = total[u * RUNS : (u + 1) * RUNS]
                    line[i, pl.ds(2 * u + e, RUNS, stride=run), :] = value
            done[row] = line[i, PAD : PAD + cells].astype(BF)
            copy = pltpu.make_async_copy(done.at[row], result.at[flip(row, rows)], sems.at[row])
            copy.start()
            copies.append(copy)
    for copy in copies:
        copy.wait()


def cell_order(width):
    run = width // RUNS
    cell = np.arange(width // 2) // RUNS * 2 + np.arange(width // 2) % RUNS * run
    return np.stack([cell, cell + 1])


def forward_table(cells, lon_total, modes, lon_size):
    order = cell_order(cells + 2 * PAD).reshape(-1) - PAD
    inside = (order >= 0) & (order < cells)
    waves = np.arange(modes)
    tables, leaks = [], []
    for core in range(2):
        theta = (2 * np.pi / lon_total) * (np.outer(waves, order + core * cells) % lon_total)
        full = np.stack([np.cos(theta), -np.sin(theta)], 0) * inside
        full = full.reshape(2, lon_size // 2, 2, modes // lon_size, -1)
        full = full.transpose(2, 1, 0, 3, 4)[[core, 1 - core]]
        tables.append(full.reshape(2 * modes, -1).astype(ml_dtypes.bfloat16))
        leaks.append(tables[-1].astype(np.float64).sum(1, keepdims=True).astype(np.float32))
    return np.stack(tables), np.stack(leaks)


def turn_table(lon_size, local, scale):
    chips = lon_size // 2
    me = np.arange(lon_size)[:, None, None]
    waves = me * local + np.arange(local)[:, None]
    source = 2 * ((me // 2) ^ np.arange(chips))
    phase = source * waves % lon_size * (2 * np.pi / lon_size)
    cos, sin = scale * np.cos(phase), scale * np.sin(phase)
    eye = np.eye(local)
    cos, sin = (x[:, :, :, None] * eye[:, None, :] for x in (cos, sin))
    real = np.stack([cos, sin], axis=3)
    imag = np.stack([-sin, cos], axis=3)
    full = np.concatenate([real, imag], axis=1)
    full = full.reshape(lon_size, 2 * local, chips * 2 * local).astype(np.float32)
    high = full.astype(ml_dtypes.bfloat16)
    low = (full - high.astype(np.float32)).astype(ml_dtypes.bfloat16)
    return np.concatenate([high, low], axis=1)


def inverse_parts(cells, lon_total, modes, lon_size):
    column = np.arange(2 * modes)
    local = modes // lon_size
    waves = column // (2 * local) * local + column % local
    imaginary = column // local % 2 == 1
    order = cell_order(cells + 2 * PAD) - PAD
    theta = (2 * np.pi / lon_total) * (order[:, :, None] * waves % lon_total)
    weight = np.where(waves == 0, 1.0, 2.0)
    cos, sin = weight * np.cos(theta), weight * np.sin(theta)
    by_cos = np.where(imaginary, -sin, cos).astype(np.float32)
    by_sin = np.where(imaginary, -cos, -sin).astype(np.float32)
    return waves.astype(np.int32), by_cos, by_sin


def phase_table(cells, lon_total, modes, lon_size):
    waves = inverse_parts(cells, lon_total, modes, lon_size)[0]
    phase = np.arange(lon_size)[:, None] * waves % lon_size * (2 * np.pi / lon_size)
    return np.stack([np.cos(phase), np.sin(phase)], 1).astype(np.float32)


def facing(rows, partner):
    odd = odd_lat()
    return (rows - HALO) * ((1 - odd) if partner else odd)


def slice_kernel(field, *rest):
    out, sem = rest[-2:]
    at = facing(field.shape[0], len(rest) == 2)
    copy = pltpu.make_async_copy(field.at[pl.ds(at, HALO)], out, sem)
    copy.start()
    copy.wait()


def side_kernel(field, after, last, leading, sems):
    cells = field.shape[1]
    first = pltpu.make_async_copy(field.at[:, cells - PAD :], last, sems.at[0])
    second = pltpu.make_async_copy(field.at[:, :PAD], leading, sems.at[1])
    first.start()
    second.start()
    first.wait()
    second.wait()


def edge_kernel(from_left, from_right, edges, near):
    rows = from_left.shape[0]
    for row in range(rows):
        edges[row] = jnp.concatenate([from_left[row], from_right[row]], axis=0)
    at = facing(rows, True)
    for row in range(HALO):
        near[row] = jnp.concatenate([from_left[at + row], from_right[at + row]], axis=0)


def copy_kernel(edges, near, other):
    at = facing(edges.shape[0], False)
    for row in range(HALO):
        other[row] = edges[at + row]


def inverse_kernel(parts, phase, after, inverse):
    turn = phase[lax.axis_index("lon")]
    for e in range(2):
        inverse[e] = (parts[0, e] * turn[0:1] + parts[1, e] * turn[1:2]).astype(BF)


def lat_edges():
    me, size, odd = lax.axis_index("lat"), lax.axis_size("lat"), odd_lat()
    after, before = (me < size - 1).astype(F32), (me > 0).astype(F32)
    even = (1 - odd).astype(F32)
    return [even * before + (1.0 - even) * after, even * after + (1.0 - even) * before]


def lat_pairs(partner):
    pairs = [(i, i + 1) for i in range(0 if partner else 1, lax.axis_size("lat") - 1, 2)]
    return pairs + [(j, i) for i, j in pairs]


def move(array, partner):
    return lax.ppermute(array, "lat", lat_pairs(partner))


def shape(*dims):
    return jax.ShapeDtypeStruct(dims, BF)


def call(kernel, args, outs, scratch, in_specs=None, out_specs=None, grid=(), cost=0):
    estimate = pl.CostEstimate(flops=int(cost * 8e8), bytes_accessed=0, transcendentals=0)
    return pl.pallas_call(
        kernel,
        grid=grid,
        out_shape=outs,
        in_specs=in_specs or [VMEM] * len(args),
        out_specs=out_specs or [VMEM] * len(outs),
        scratch_shapes=scratch,
        compiler_params=PARAMS,
        cost_estimate=estimate if cost else None,
    )(*(jnp.asarray(arg) for arg in args))


def per_device(field, conv_weight, conv_bias, spec_real, spec_imag):
    rows, cells, c = field.shape
    width = cells + 2 * PAD
    half = width // 2
    lon_size = lax.axis_size("lon")
    lon_total = cells * lon_size
    local = spec_real.shape[1]
    modes = local * lon_size

    wide = half + 2 * RUNS
    below = call(
        slice_kernel, (field,), [shape(HALO, cells, c)], [DMA], in_specs=[HBM], out_specs=[ANY]
    )[0]
    down = move(below, True)
    above = call(
        slice_kernel,
        (field, below),
        [shape(HALO, cells, c)],
        [DMA],
        in_specs=[HBM, ANY],
        out_specs=[ANY],
    )[0]
    up = move(above, False)
    last, leading = call(
        side_kernel,
        (field, above),
        [shape(rows, PAD, c)] * 2,
        [pltpu.SemaphoreType.DMA((2,))],
        in_specs=[HBM, ANY],
        out_specs=[ANY] * 2,
    )
    right = [(i, (i + 1) % lon_size) for i in range(lon_size)]
    left = [(j, i) for i, j in right]
    from_left = lax.ppermute(last, "lon", right)
    from_right = lax.ppermute(leading, "lon", left)
    own_edge, below = call(
        edge_kernel,
        (from_left, from_right),
        [shape(rows, 2 * PAD, c), shape(HALO, 2 * PAD, c)],
        [],
    )
    down_edge = move(below, True)
    above = call(
        copy_kernel, (own_edge, below), [shape(HALO, 2 * PAD, c)], [], in_specs=[VMEM, ANY]
    )[0]
    up_edge = move(above, False)
    tables = (cells, lon_total, modes, lon_size)
    inverse = call(
        inverse_kernel,
        (np.stack(inverse_parts(*tables)[1:]), phase_table(*tables), above),
        [shape(2, half, 2 * modes)],
        [],
        in_specs=[VMEM, VMEM, ANY],
    )[0]
    forward, leak = forward_table(*tables)
    turn = turn_table(lon_size, local, 1.0 / lon_total)

    line = pltpu.VMEM((2, width, c), F32)
    weights = shape(CONVS, 4 if WINOGRAD else 3, 4 * c, 2 * c)
    lower = [shape(n, wide, 2 * c) for n in (rows + HALO, 3, 2)]
    early = [shape(2, wide, 2 * c), jax.ShapeDtypeStruct((4, half, 2 * c), F32)]
    gathered = pltpu.VMEM((2 * modes, HALO * c), BF)
    upper = [pltpu.VMEM((4, wide, 2 * c), BF)] * 2 + [pltpu.VMEM((rows, half, 2 * c), BF)]
    hidden_shape = shape(rows, half, 2 * c)
    part_shape = [jax.ShapeDtypeStruct((modes, rows * c), F32)] * 2

    own_rows = shape(rows, wide, 2 * c)
    own, packed, later, *inner = call(
        prepare_kernel,
        (field, own_edge, conv_weight, conv_bias[0], inverse),
        [own_rows, weights, weights] + early,
        [line],
        in_specs=[VMEM] * 4 + [ANY],
        cost=4,
    )
    low = call(
        first_lower_kernel,
        (down, down_edge, own, packed, *inner, conv_bias[0]),
        lower,
        [line],
    )
    kept, sent, hidden, to_partner, to_other, before = call(
        first_upper_kernel,
        (up, up_edge, *low, *inner, packed, conv_bias[0], forward, leak),
        part_shape
        + [hidden_shape]
        + [shape(HALO, half, 2 * c)] * 2
        + [shape(HALO, wide, 2 * c)],
        [line] + upper,
    )
    def swap(array, step):
        return lax.ppermute(array, "lon", [(i, i ^ step) for i in range(lon_size)])

    chunk = shape(2 * local, rows * c)

    def pair(kept, sent):
        return call(pair_kernel, (kept, swap(sent, 1)), [chunk] * (lon_size // 2), [])

    def mix(own, others, block):
        sums = [own] + [swap(other, 2 * i + 2) for i, other in enumerate(others)]
        turned = pltpu.VMEM((2 * rows * local, c), F32)
        weights = pl.BlockSpec((1, local, c, c), lambda i: (block, 0, 0, 0))
        (mixed,) = call(
            mix_kernel,
            (turn, spec_real, spec_imag, conv_bias[block], *sums),
            [chunk],
            [turned, turned],
            in_specs=[VMEM, weights, weights] + [VMEM] * (1 + len(sums)),
            grid=(1,),
        )
        return lax.all_gather(mixed, "lon", axis=0, tiled=True)

    own, *others = pair(kept, sent)
    to_partner, to_other, _ = lax.optimization_barrier((to_partner, to_other, own))
    from_down, from_up = move(to_partner, True), move(to_other, False)
    mixed = mix(own, others, 0)
    halo = call(halo_kernel, (mixed,), [shape(2 * modes, HALO * c)], [])[0]
    lat_size = lax.axis_size("lat")
    ways = []
    for i in range(lon_size):
        ways += [(i * lat_size + j, i * lat_size + k) for j, k in lat_pairs(i % 2 == 0)]
    mine = lax.ppermute(halo, ("lon", "lat"), ways)
    own, *inner = call(
        middle_own_kernel,
        (low[0], hidden, mixed, inverse, later, conv_bias[1]),
        [own_rows] + early,
        [],
        cost=3,
    )
    other = swap(lax.optimization_barrier((mine, own))[0], 1)
    state, *low = call(
        middle_lower_kernel,
        (low[0], from_down, mine, other, own, *inner, inverse, later, conv_bias[1]),
        lower,
        [gathered],
    )
    kept, sent, hidden = call(
        middle_upper_kernel,
        (before, from_up, mine, other, inverse, state, *low, *inner)
        + (later, conv_bias[1], forward, leak),
        part_shape + [hidden_shape],
        [pltpu.VMEM((HALO, wide, 2 * c), BF), gathered] + upper,
    )
    own, *others = pair(kept, sent)
    mixed = mix(own, others, 1)
    (result,) = call(
        last_kernel,
        (state, hidden, mixed, inverse),
        [shape(rows, cells, c)],
        [line, pltpu.VMEM((rows, cells, c), BF), pltpu.SemaphoreType.DMA((rows,))],
        out_specs=[ANY],
    )
    return result


def solution(mesh):
    return jax.shard_map(
        per_device,
        mesh=mesh,
        in_specs=(
            P("lat", "lon", None),
            P(),
            P(),
            P(None, "lon", None, None),
            P(None, "lon", None, None),
        ),
        out_specs=P("lat", "lon", None),
        check_vma=False,
    )
```

```python
import math

import jax
import jax.numpy as jnp
import ml_dtypes
import numpy as np
from jax import lax
from jax.experimental import pallas as pl
from jax.experimental.pallas import tpu as pltpu
from jax.sharding import PartitionSpec as P

BLOCKS = 2
CONVS = 3
PAD = 16
RUNS = 16
HALO = 3
WINOGRAD = True
BF = jnp.bfloat16
F32 = jnp.float32
VMEM = pl.BlockSpec(memory_space=pltpu.VMEM)
ANY = pl.BlockSpec(memory_space=pl.ANY)
HBM = pl.BlockSpec(memory_space=pltpu.HBM)
DMA = pltpu.SemaphoreType.DMA
PARAMS = pltpu.CompilerParams(vmem_limit_bytes=28 << 20)


def odd_lat():
    return lax.rem(lax.axis_index("lat"), 2)


def flip(row, rows):
    return row + odd_lat() * (rows - 1 - 2 * row)


def tile_of(tiles):
    return max(n for n in range(1, 34) if tiles % n == 0) * RUNS


def pack_row(line, wide, row):
    c = line.shape[1]
    run = 2 * (wide.shape[1] // RUNS - 2)
    for cell in range(run):
        lanes = slice(cell % 2 * c, (cell % 2 + 1) * c)
        at = RUNS * (cell // 2 + 1)
        wide[row, at : at + RUNS, lanes] = line[pl.ds(cell, RUNS, stride=run), :].astype(BF)


def close_row(wide, row):
    c = wide.shape[2] // 2
    end = wide.shape[1] - RUNS
    before = wide[row, end - RUNS : end, c:].astype(F32)
    wide[row, 0:RUNS, c:] = pltpu.roll(before, 1, 0).astype(BF)
    after = wide[row, RUNS : 2 * RUNS, :c].astype(F32)
    wide[row, end : end + RUNS, :c] = pltpu.roll(after, RUNS - 1, 0).astype(BF)


def build_weights(kernels, block, packed, layer):
    c = kernels.shape[-1]
    zero = jnp.zeros((c, c), BF)
    for tap in range(3):
        g0, g1, g2 = (kernels[block, layer, flip(a, 3), tap].astype(F32) for a in range(3))
        if WINOGRAD:
            outer = g0 + g2
            parts = (0.5 * g0, 0.25 * (outer + g1), 0.25 * (outer - g1), 0.5 * g2)
        else:
            parts = (0.5 * g0, 0.5 * g1, 0.5 * g2)
        for i, part in enumerate(parts):
            value = part.astype(BF)
            for cell in range(2):
                source = cell + tap - 1
                at = {0: 0, 1: c, 2: 2 * c, -1: 3 * c}[source]
                packed[layer, i, at : at + c, cell * c : (cell + 1) * c] = value
    for i in range(packed.shape[1]):
        packed[layer, i, 2 * c : 3 * c, :c] = zero
        packed[layer, i, 3 * c :, c:] = zero


def window(wide, row, start, size):
    c = wide.shape[2] // 2
    here = wide[row, start + RUNS : start + RUNS + size]
    after = wide[row, start + 2 * RUNS : start + 2 * RUNS + size, :c]
    before = wide[row, start : start + size, c:]
    return jnp.concatenate([here, after, before], axis=1)


def dot(a, b):
    return jnp.dot(a, b, preferred_element_type=F32)


def silu_of_half(half):
    return half + half * jnp.tanh(half)


def conv_pair(d, packed, layer):
    if WINOGRAD:
        inputs = (d[0] - d[2], d[1] + d[2], d[2] - d[1], d[1] - d[3])
        m = [dot(x, packed[layer, i]) for i, x in enumerate(inputs)]
        return (m[1] + m[2]) + m[0], m[1] - m[2] - m[3]
    w = jnp.concatenate([packed[layer, i] for i in range(3)], axis=0)
    return tuple(dot(jnp.concatenate(d[i : i + 3], axis=1), w) for i in range(2))


class Rows:
    def __init__(self, *held):
        self.at = {}
        for ref, first in held:
            self.at.update({first + i: (ref, i) for i in range(ref.shape[0])})

    def __getitem__(self, row):
        return self.at[row]


def conv_rows(src, dst, span, layer, packed, bias, edge, rows):
    ref = src[span[0]][0]
    width = ref.shape[1] - 2 * RUNS
    tile = tile_of(width // RUNS)
    both = 0.5 * jnp.concatenate([bias[layer : layer + 1]] * 2, axis=1)
    for pair in range(*span, 2):
        for start in range(0, width, tile):
            sums = conv_pair(
                [window(*src[pair + i - 1], start, tile) for i in range(4)], packed, layer
            )
            for i, total in enumerate(sums):
                row = pair + i
                y = silu_of_half(total + both)
                if row < 0:
                    y = y * edge[0]
                elif row >= rows:
                    y = y * edge[1]
                if callable(dst):
                    dst(row, start, y.astype(BF))
                else:
                    ref, at = dst[row]
                    ref[at, start + RUNS : start + RUNS + tile] = y.astype(BF)
        if not callable(dst):
            for i in range(2):
                close_row(*dst[pair + i])


def transform(forward, leak, bias, held, kept, sent):
    core = lax.rem(lax.axis_index("lon"), 2)
    rows, c = held.shape[0], held.shape[2] // 2
    half = 0.5 * bias[CONVS - 1 : CONVS]
    level = silu_of_half(half)
    for row in range(0, rows, 2):
        cells = [
            jnp.concatenate([held[row + i, :, e * c : (e + 1) * c] for i in range(2)], axis=1)
            for e in range(2)
        ]
        total = dot(forward[core], jnp.concatenate(cells, axis=0))
        modes2 = total.shape[0]
        total = total - leak[core] * jnp.concatenate([level, level], axis=1)
        lanes = slice(row * c, (row + 2) * c)
        kept[:, lanes] = total[: modes2 // 2]
        sent[:, lanes] = total[modes2 // 2 :]


def pack_cells(body, ends, source, line, wide, at):
    cells = body.shape[1]
    line[0:PAD] = ends[source, :PAD].astype(F32)
    line[PAD : PAD + cells] = body[source].astype(F32)
    line[PAD + cells : 2 * PAD + cells] = ends[source, PAD:].astype(F32)
    pack_row(line, wide, at)
    close_row(wide, at)


def product(a, b, sign, start, tile, packed, layer, index):
    left, right = window(*a, start, tile), window(*b, start, tile)
    return dot(left + right if sign > 0 else left - right, packed[layer, index])


def put(dst, start, half, bias, layer):
    ref, at = dst
    both = 0.5 * jnp.concatenate([bias[layer : layer + 1]] * 2, axis=1)
    y = silu_of_half(half + both).astype(BF)
    ref[at, start + RUNS : start + RUNS + y.shape[0]] = y


def spans(ref):
    width = ref.shape[1] - 2 * RUNS
    tile = tile_of(width // RUNS)
    return [(start, tile) for start in range(0, width, tile)]


def early_part(field, inner, sums, packed, bias):
    x, y = Rows((field, 0)), Rows((inner, 1))
    for start, tile in spans(field):
        span = slice(start, start + tile)
        args = (start, tile, packed, 0)
        m1 = product(x[0], x[1], 1, *args, 1)
        m2 = product(x[1], x[0], -1, *args, 2)
        m3 = product(x[0], x[2], -1, *args, 3)
        sums[0, span] = m1 + m2
        put(y[1], start, m1 - m2 - m3, bias, 0)
        m0 = product(x[1], x[3], -1, *args, 0)
        m1 = product(x[2], x[3], 1, *args, 1)
        m2 = product(x[3], x[2], -1, *args, 2)
        sums[1, span] = m1 - m2
        put(y[2], start, (m1 + m2) + m0, bias, 0)
    close_row(*y[1])
    close_row(*y[2])
    for start, tile in spans(field):
        span = slice(start, start + tile)
        args = (start, tile, packed, 1)
        m1 = product(y[1], y[2], 1, *args, 1)
        m2 = product(y[2], y[1], -1, *args, 2)
        sums[2, span] = m1 + m2
        sums[3, span] = m1 - m2


def lower_part(field, inner, sums, first, second, packed, bias, edge, rows):
    x, y, z = Rows((field, 0)), Rows((inner, 1), (first, 3)), Rows((second, 3))
    for start, tile in spans(field):
        m3 = product(x[2], x[4], -1, start, tile, packed, 0, 3)
        put(y[3], start, sums[1, start : start + tile] - m3, bias, 0)
    close_row(*y[3])
    conv_rows(x, y, (4, 6), 0, packed, bias, edge, rows)
    conv_rows(y, z, (3, 5), 1, packed, bias, edge, rows)


def upper_part(before, field, inner, sums, first, second, more, packed, bias, edge, emit):
    rows = field.shape[0] - HALO
    x = Rows((before, -HALO), (field, 0))
    y = Rows((more[0], -2), (inner, 1), (first, 3))
    z = Rows((more[1], -1), (second, 3))
    conv_rows(x, y, (-2, 0), 0, packed, bias, edge, rows)
    for start, tile in spans(field):
        m0 = product(x[-1], x[1], -1, start, tile, packed, 0, 0)
        put(y[0], start, sums[0, start : start + tile] + m0, bias, 0)
    close_row(*y[0])
    conv_rows(y, z, (-1, 1), 1, packed, bias, edge, rows)
    for start, tile in spans(field):
        span = slice(start, start + tile)
        m0 = product(y[0], y[2], -1, start, tile, packed, 1, 0)
        m3 = product(y[1], y[3], -1, start, tile, packed, 1, 3)
        put(z[1], start, sums[2, span] + m0, bias, 1)
        put(z[2], start, sums[3, span] - m3, bias, 1)
    close_row(*z[1])
    close_row(*z[2])
    conv_rows(z, emit, (0, rows), 2, packed, bias, edge, rows)


def prepare_kernel(own, own_edge, kernels, bias, after, field, packed, later, inner, sums, line):
    rows = own.shape[0]
    for layer in range(CONVS):
        build_weights(kernels, 0, packed, layer)
        build_weights(kernels, 1, later, layer)
    for row in range(rows):
        pack_cells(own, own_edge, flip(row, rows), line.at[row % 2], field, row)
    early_part(field, inner, sums, packed, bias)


def first_lower_kernel(
    down, down_edge, own, packed, inner, sums, bias, field, first, second, line
):
    rows = own.shape[0]
    field[:rows] = own[...]
    for row in range(HALO):
        pack_cells(down, down_edge, flip(row, HALO), line.at[row % 2], field, rows + row)
    lower_part(field, inner, sums, first, second, packed, bias, lat_edges(), rows)


def first_upper_kernel(
    up, up_edge, field, first, second, inner, sums, packed, bias, forward, leak,
    kept, sent, hidden, to_partner, to_other, before,
    line, more, most, held,
):
    rows = field.shape[0] - HALO
    for row in range(HALO):
        pack_cells(up, up_edge, flip(row, HALO), line.at[row % 2], before, row)

    def emit(row, start, y):
        span = slice(start, start + y.shape[0])
        held[row, span] = y
        hidden[row, span] = y
        if row < HALO:
            to_other[HALO - 1 - row, span] = y
        if row >= rows - HALO:
            to_partner[rows - 1 - row, span] = y

    args = (before, field, inner, sums, first, second, (more, most), packed, bias)
    upper_part(*args, lat_edges(), emit)
    transform(forward, leak, bias, held, kept, sent)


def pair_kernel(kept, got, *outs):
    chip = lax.div(lax.axis_index("lon"), 2)
    rows = outs[0].shape[0]
    for step, out in enumerate(outs):
        span = pl.ds(pl.multiple_of((chip ^ step) * rows, rows), rows)
        out[...] = (kept[span, :] + got[span, :]).astype(BF)


def mix_kernel(turn, real, imag, bias, *rest):
    *sums, mixed, spread_in, spread_out = rest
    me = lax.axis_index("lon")
    modes, c = real.shape[1], real.shape[2]
    summed = dot(turn[me], jnp.concatenate([x[...] for x in sums], axis=0))
    summed = summed[: 2 * modes] + summed[2 * modes :]
    rows = summed.shape[1] // c
    level = (me == 0).astype(F32) * silu_of_half(0.5 * bias[CONVS - 1 : CONVS])
    for half in range(2):
        for row in range(rows):
            spread_in[pl.ds(half * rows + row, modes, stride=2 * rows), :] = summed[
                half * modes : (half + 1) * modes, row * c : (row + 1) * c
            ]
    spread_in[0:rows] = spread_in[0:rows] + level
    sign = jnp.where(lax.broadcasted_iota(jnp.int32, (2 * rows, c), 0) < rows, -1.0, 1.0)
    for k in range(modes):
        wide = spread_in[2 * rows * k : 2 * rows * (k + 1)]
        high = wide.astype(BF)
        low = (wide - high.astype(F32)).astype(BF)
        both = jnp.concatenate([high, low], axis=0)
        weight = jnp.concatenate([real[0, k], imag[0, k]], axis=1)
        out = jnp.dot(both, weight, preferred_element_type=F32)
        out = out[: 2 * rows] + out[2 * rows :]
        turned = pltpu.roll(out[:, c:], rows, 0)
        spread_out[2 * rows * k : 2 * rows * (k + 1)] = out[:, :c] + sign * turned
    for row in range(rows):
        parts = [spread_out[pl.ds(i * rows + row, modes, stride=2 * rows), :] for i in range(2)]
        mixed[:, row * c : (row + 1) * c] = jnp.concatenate(parts, axis=0).astype(BF)


def halo_kernel(mixed, out):
    c = out.shape[1] // HALO
    rows = mixed.shape[1] // c
    even = lax.rem(lax.axis_index("lon"), 2) == 0
    for at in range(HALO):
        last = mixed[:, (rows - 1 - at) * c : (rows - at) * c]
        leading = mixed[:, (HALO - 1 - at) * c : (HALO - at) * c]
        out[:, at * c : (at + 1) * c] = jnp.where(even, last, leading)


def pick(mine, other, first):
    even = lax.rem(lax.axis_index("lon"), 2) == 0
    return jnp.where(even == first, mine[...], other[...])


def next_state(old, conv, mixed, inverse, new, at, count, mask):
    c = mixed.shape[1] // conv[0].shape[0]
    width = conv[0].shape[1]
    tile = tile_of(width // RUNS)
    for pair in range(0, count, 2):
        lanes = slice(pair * c, min(pair + 2, count) * c)
        for start in range(0, width, tile):
            span = slice(start, start + tile)
            wide = slice(start + RUNS, start + RUNS + tile)
            waves = [dot(inverse[e, span], mixed[:, lanes]) for e in range(2)]
            for i in range(min(2, count - pair)):
                wave = jnp.concatenate([w[:, i * c : (i + 1) * c] for w in waves], axis=1)
                total = old[0][old[1] + pair + i, wide].astype(F32)
                total = total + conv[0][pair + i, span].astype(F32) + wave
                total = jnp.tanh(total)
                if mask is not None:
                    total = total * mask
                new[at + pair + i, wide] = total.astype(BF)
        for i in range(min(2, count - pair)):
            close_row(new, at + pair + i)


def middle_own_kernel(field, hidden, mixed, inverse, packed, bias, state, inner, sums):
    next_state((field, 0), (hidden,), mixed, inverse, state, 0, hidden.shape[0], None)
    early_part(state, inner, sums, packed, bias)


def middle_lower_kernel(
    field, from_down, mine, other, own, inner, sums, inverse, packed, bias,
    state, first, second, mixed_down,
):
    rows = own.shape[0]
    edge = lat_edges()
    state[:rows] = own[...]
    mixed_down[...] = pick(mine, other, True)
    next_state((field, rows), (from_down,), mixed_down, inverse, state, rows, HALO, edge[1])
    lower_part(state, inner, sums, first, second, packed, bias, edge, rows)


def middle_upper_kernel(
    before, from_up, mine, other, inverse, state, first, second, inner, sums,
    packed, bias, forward, leak,
    kept, sent, hidden, above, mixed_up, more, most, held,
):
    edge = lat_edges()
    mixed_up[...] = pick(mine, other, False)
    next_state((before, 0), (from_up,), mixed_up, inverse, above, 0, HALO, edge[0])

    def emit(row, start, y):
        span = slice(start, start + y.shape[0])
        held[row, span] = y
        hidden[row, span] = y

    args = (above, state, inner, sums, first, second, (more, most), packed, bias)
    upper_part(*args, edge, emit)
    transform(forward, leak, bias, held, kept, sent)


def last_kernel(state, hidden, mixed, inverse, result, line, done, sems):
    rows, width, c = hidden.shape[0], hidden.shape[1], hidden.shape[2] // 2
    cells = result.shape[1]
    run = 2 * width // RUNS
    copies = []
    for pair in range(0, rows, 2):
        waves = [dot(inverse[e], mixed[:, pair * c : (pair + 2) * c]) for e in range(2)]
        for i in range(2):
            row = pair + i
            for e in range(2):
                lanes = slice(e * c, (e + 1) * c)
                total = state[row, RUNS : RUNS + width, lanes].astype(F32) + hidden[row, :, lanes].astype(F32)
                total = jnp.tanh(total + waves[e][:, i * c : (i + 1) * c])
                for u in range(width // RUNS):
                    value = total[u * RUNS : (u + 1) * RUNS]
                    line[i, pl.ds(2 * u + e, RUNS, stride=run), :] = value
            done[row] = line[i, PAD : PAD + cells].astype(BF)
            copy = pltpu.make_async_copy(done.at[row], result.at[flip(row, rows)], sems.at[row])
            copy.start()
            copies.append(copy)
    for copy in copies:
        copy.wait()


def cell_order(width):
    run = width // RUNS
    cell = np.arange(width // 2) // RUNS * 2 + np.arange(width // 2) % RUNS * run
    return np.stack([cell, cell + 1])


def forward_table(cells, lon_total, modes, lon_size):
    order = cell_order(cells + 2 * PAD).reshape(-1) - PAD
    inside = (order >= 0) & (order < cells)
    waves = np.arange(modes)
    tables, leaks = [], []
    for core in range(2):
        theta = (2 * np.pi / lon_total) * (np.outer(waves, order + core * cells) % lon_total)
        full = np.stack([np.cos(theta), -np.sin(theta)], 0) * inside
        full = full.reshape(2, lon_size // 2, 2, modes // lon_size, -1)
        full = full.transpose(2, 1, 0, 3, 4)[[core, 1 - core]]
        tables.append(full.reshape(2 * modes, -1).astype(ml_dtypes.bfloat16))
        leaks.append(tables[-1].astype(np.float64).sum(1, keepdims=True).astype(np.float32))
    return np.stack(tables), np.stack(leaks)


def turn_table(lon_size, local, scale):
    chips = lon_size // 2
    me = np.arange(lon_size)[:, None, None]
    waves = me * local + np.arange(local)[:, None]
    source = 2 * ((me // 2) ^ np.arange(chips))
    phase = source * waves % lon_size * (2 * np.pi / lon_size)
    cos, sin = scale * np.cos(phase), scale * np.sin(phase)
    eye = np.eye(local)
    cos, sin = (x[:, :, :, None] * eye[:, None, :] for x in (cos, sin))
    real = np.stack([cos, sin], axis=3)
    imag = np.stack([-sin, cos], axis=3)
    full = np.concatenate([real, imag], axis=1)
    full = full.reshape(lon_size, 2 * local, chips * 2 * local).astype(np.float32)
    high = full.astype(ml_dtypes.bfloat16)
    low = (full - high.astype(np.float32)).astype(ml_dtypes.bfloat16)
    return np.concatenate([high, low], axis=1)


def inverse_parts(cells, lon_total, modes, lon_size):
    column = np.arange(2 * modes)
    local = modes // lon_size
    waves = column // (2 * local) * local + column % local
    imaginary = column // local % 2 == 1
    order = cell_order(cells + 2 * PAD) - PAD
    theta = (2 * np.pi / lon_total) * (order[:, :, None] * waves % lon_total)
    weight = np.where(waves == 0, 1.0, 2.0)
    cos, sin = weight * np.cos(theta), weight * np.sin(theta)
    by_cos = np.where(imaginary, -sin, cos).astype(np.float32)
    by_sin = np.where(imaginary, -cos, -sin).astype(np.float32)
    return waves.astype(np.int32), by_cos, by_sin


def phase_table(cells, lon_total, modes, lon_size):
    waves = inverse_parts(cells, lon_total, modes, lon_size)[0]
    phase = np.arange(lon_size)[:, None] * waves % lon_size * (2 * np.pi / lon_size)
    return np.stack([np.cos(phase), np.sin(phase)], 1).astype(np.float32)


def facing(rows, partner):
    odd = odd_lat()
    return (rows - HALO) * ((1 - odd) if partner else odd)


def slice_kernel(field, *rest):
    out, sem = rest[-2:]
    at = facing(field.shape[0], len(rest) == 2)
    copy = pltpu.make_async_copy(field.at[pl.ds(at, HALO)], out, sem)
    copy.start()
    copy.wait()


def side_kernel(field, after, last, leading, sems):
    cells = field.shape[1]
    first = pltpu.make_async_copy(field.at[:, cells - PAD :], last, sems.at[0])
    second = pltpu.make_async_copy(field.at[:, :PAD], leading, sems.at[1])
    first.start()
    second.start()
    first.wait()
    second.wait()


def edge_kernel(from_left, from_right, edges, near):
    rows = from_left.shape[0]
    for row in range(rows):
        edges[row] = jnp.concatenate([from_left[row], from_right[row]], axis=0)
    at = facing(rows, True)
    for row in range(HALO):
        near[row] = jnp.concatenate([from_left[at + row], from_right[at + row]], axis=0)


def copy_kernel(edges, near, other):
    at = facing(edges.shape[0], False)
    for row in range(HALO):
        other[row] = edges[at + row]


def inverse_kernel(parts, phase, after, inverse):
    turn = phase[lax.axis_index("lon")]
    for e in range(2):
        inverse[e] = (parts[0, e] * turn[0:1] + parts[1, e] * turn[1:2]).astype(BF)


def lat_edges():
    me, size, odd = lax.axis_index("lat"), lax.axis_size("lat"), odd_lat()
    after, before = (me < size - 1).astype(F32), (me > 0).astype(F32)
    even = (1 - odd).astype(F32)
    return [even * before + (1.0 - even) * after, even * after + (1.0 - even) * before]


def lat_pairs(partner):
    pairs = [(i, i + 1) for i in range(0 if partner else 1, lax.axis_size("lat") - 1, 2)]
    return pairs + [(j, i) for i, j in pairs]


def move(array, partner):
    return lax.ppermute(array, "lat", lat_pairs(partner))


def shape(*dims):
    return jax.ShapeDtypeStruct(dims, BF)


def call(kernel, args, outs, scratch, in_specs=None, out_specs=None, grid=(), cost=0):
    estimate = pl.CostEstimate(flops=int(cost * 8e8), bytes_accessed=0, transcendentals=0)
    return pl.pallas_call(
        kernel,
        grid=grid,
        out_shape=outs,
        in_specs=in_specs or [VMEM] * len(args),
        out_specs=out_specs or [VMEM] * len(outs),
        scratch_shapes=scratch,
        compiler_params=PARAMS,
        cost_estimate=estimate if cost else None,
    )(*(jnp.asarray(arg) for arg in args))


def per_device(field, conv_weight, conv_bias, spec_real, spec_imag):
    rows, cells, c = field.shape
    width = cells + 2 * PAD
    half = width // 2
    lon_size = lax.axis_size("lon")
    lon_total = cells * lon_size
    local = spec_real.shape[1]
    modes = local * lon_size

    wide = half + 2 * RUNS
    below = call(
        slice_kernel, (field,), [shape(HALO, cells, c)], [DMA], in_specs=[HBM], out_specs=[ANY]
    )[0]
    down = move(below, True)
    above = call(
        slice_kernel,
        (field, below),
        [shape(HALO, cells, c)],
        [DMA],
        in_specs=[HBM, ANY],
        out_specs=[ANY],
    )[0]
    up = move(above, False)
    last, leading = call(
        side_kernel,
        (field, above),
        [shape(rows, PAD, c)] * 2,
        [pltpu.SemaphoreType.DMA((2,))],
        in_specs=[HBM, ANY],
        out_specs=[ANY] * 2,
    )
    right = [(i, (i + 1) % lon_size) for i in range(lon_size)]
    left = [(j, i) for i, j in right]
    from_left = lax.ppermute(last, "lon", right)
    from_right = lax.ppermute(leading, "lon", left)
    own_edge, below = call(
        edge_kernel,
        (from_left, from_right),
        [shape(rows, 2 * PAD, c), shape(HALO, 2 * PAD, c)],
        [],
    )
    down_edge = move(below, True)
    above = call(
        copy_kernel, (own_edge, below), [shape(HALO, 2 * PAD, c)], [], in_specs=[VMEM, ANY]
    )[0]
    up_edge = move(above, False)
    tables = (cells, lon_total, modes, lon_size)
    inverse = call(
        inverse_kernel,
        (np.stack(inverse_parts(*tables)[1:]), phase_table(*tables), above),
        [shape(2, half, 2 * modes)],
        [],
        in_specs=[VMEM, VMEM, ANY],
    )[0]
    forward, leak = forward_table(*tables)
    turn = turn_table(lon_size, local, 1.0 / lon_total)

    line = pltpu.VMEM((2, width + 2 * half // RUNS + 8, c), F32)
    weights = shape(CONVS, 4 if WINOGRAD else 3, 4 * c, 2 * c)
    lower = [shape(n, wide, 2 * c) for n in (rows + HALO, 3, 2)]
    early = [shape(2, wide, 2 * c), jax.ShapeDtypeStruct((4, half, 2 * c), F32)]
    gathered = pltpu.VMEM((2 * modes, HALO * c), BF)
    upper = [pltpu.VMEM((4, wide, 2 * c), BF)] * 2 + [pltpu.VMEM((rows, half, 2 * c), BF)]
    hidden_shape = shape(rows, half, 2 * c)
    part_shape = [jax.ShapeDtypeStruct((modes, rows * c), F32)] * 2

    own_rows = shape(rows, wide, 2 * c)
    own, packed, later, *inner = call(
        prepare_kernel,
        (field, own_edge, conv_weight, conv_bias[0], inverse),
        [own_rows, weights, weights] + early,
        [line],
        in_specs=[VMEM] * 4 + [ANY],
        cost=4,
    )
    low = call(
        first_lower_kernel,
        (down, down_edge, own, packed, *inner, conv_bias[0]),
        lower,
        [line],
    )
    kept, sent, hidden, to_partner, to_other, before = call(
        first_upper_kernel,
        (up, up_edge, *low, *inner, packed, conv_bias[0], forward, leak),
        part_shape
        + [hidden_shape]
        + [shape(HALO, half, 2 * c)] * 2
        + [shape(HALO, wide, 2 * c)],
        [line] + upper,
    )
    def swap(array, step):
        return lax.ppermute(array, "lon", [(i, i ^ step) for i in range(lon_size)])

    chunk = shape(2 * local, rows * c)

    def pair(kept, sent):
        return call(pair_kernel, (kept, swap(sent, 1)), [chunk] * (lon_size // 2), [])

    def mix(own, others, block):
        sums = [own] + [swap(other, 2 * i + 2) for i, other in enumerate(others)]
        turned = pltpu.VMEM((2 * rows * (local + 1), c), F32)
        weights = pl.BlockSpec((1, local, c, c), lambda i: (block, 0, 0, 0))
        (mixed,) = call(
            mix_kernel,
            (turn, spec_real, spec_imag, conv_bias[block], *sums),
            [chunk],
            [turned, turned],
            in_specs=[VMEM, weights, weights] + [VMEM] * (1 + len(sums)),
            grid=(1,),
        )
        return lax.all_gather(mixed, "lon", axis=0, tiled=True)

    from_down, from_up = move(to_partner, True), move(to_other, False)
    own, *others = pair(kept, sent)
    mixed = mix(own, others, 0)
    halo = call(halo_kernel, (mixed,), [shape(2 * modes, HALO * c)], [])[0]
    lat_size = lax.axis_size("lat")
    ways = []
    for i in range(lon_size):
        ways += [(i * lat_size + j, i * lat_size + k) for j, k in lat_pairs(i % 2 == 0)]
    mine = lax.ppermute(halo, ("lon", "lat"), ways)
    own, *inner = call(
        middle_own_kernel,
        (low[0], hidden, mixed, inverse, later, conv_bias[1]),
        [own_rows] + early,
        [],
        cost=3,
    )
    other = swap(lax.optimization_barrier((mine, own))[0], 1)
    state, *low = call(
        middle_lower_kernel,
        (low[0], from_down, mine, other, own, *inner, inverse, later, conv_bias[1]),
        lower,
        [gathered],
    )
    kept, sent, hidden = call(
        middle_upper_kernel,
        (before, from_up, mine, other, inverse, state, *low, *inner)
        + (later, conv_bias[1], forward, leak),
        part_shape + [hidden_shape],
        [pltpu.VMEM((HALO, wide, 2 * c), BF), gathered] + upper,
    )
    own, *others = pair(kept, sent)
    mixed = mix(own, others, 1)
    (result,) = call(
        last_kernel,
        (state, hidden, mixed, inverse),
        [shape(rows, cells, c)],
        [line, pltpu.VMEM((rows, cells, c), BF), pltpu.SemaphoreType.DMA((rows,))],
        out_specs=[ANY],
    )
    return result


def solution(mesh):
    return jax.shard_map(
        per_device,
        mesh=mesh,
        in_specs=(
            P("lat", "lon", None),
            P(),
            P(),
            P(None, "lon", None, None),
            P(None, "lon", None, None),
        ),
        out_specs=P("lat", "lon", None),
        check_vma=False,
    )
```

```python
import math

import jax
import jax.numpy as jnp
import ml_dtypes
import numpy as np
from jax import lax
from jax.experimental import pallas as pl
from jax.experimental.pallas import tpu as pltpu
from jax.sharding import PartitionSpec as P

BLOCKS = 2
CONVS = 3
PAD = 16
RUNS = 16
HALO = 3
WINOGRAD = True
BF = jnp.bfloat16
F32 = jnp.float32
VMEM = pl.BlockSpec(memory_space=pltpu.VMEM)
ANY = pl.BlockSpec(memory_space=pl.ANY)
HBM = pl.BlockSpec(memory_space=pltpu.HBM)
DMA = pltpu.SemaphoreType.DMA
PARAMS = pltpu.CompilerParams(vmem_limit_bytes=28 << 20)


def odd_lat():
    return lax.rem(lax.axis_index("lat"), 2)


def flip(row, rows):
    return row + odd_lat() * (rows - 1 - 2 * row)


def tile_of(tiles):
    return max(n for n in range(1, 34) if tiles % n == 0) * RUNS


def pack_row(line, wide, row):
    c = line.shape[1]
    run = 2 * (wide.shape[1] // RUNS - 2)
    for cell in range(run):
        lanes = slice(cell % 2 * c, (cell % 2 + 1) * c)
        at = RUNS * (cell // 2 + 1)
        wide[row, at : at + RUNS, lanes] = line[pl.ds(cell, RUNS, stride=run), :].astype(BF)


def close_row(wide, row):
    c = wide.shape[2] // 2
    end = wide.shape[1] - RUNS
    before = wide[row, end - RUNS : end, c:].astype(F32)
    wide[row, 0:RUNS, c:] = pltpu.roll(before, 1, 0).astype(BF)
    after = wide[row, RUNS : 2 * RUNS, :c].astype(F32)
    wide[row, end : end + RUNS, :c] = pltpu.roll(after, RUNS - 1, 0).astype(BF)


def build_weights(kernels, block, packed, layer):
    c = kernels.shape[-1]
    zero = jnp.zeros((c, c), BF)
    for tap in range(3):
        g0, g1, g2 = (kernels[block, layer, flip(a, 3), tap].astype(F32) for a in range(3))
        if WINOGRAD:
            outer = g0 + g2
            parts = (0.5 * g0, 0.25 * (outer + g1), 0.25 * (outer - g1), 0.5 * g2)
        else:
            parts = (0.5 * g0, 0.5 * g1, 0.5 * g2)
        for i, part in enumerate(parts):
            value = part.astype(BF)
            for cell in range(2):
                source = cell + tap - 1
                at = {0: 0, 1: c, 2: 2 * c, -1: 3 * c}[source]
                packed[layer, i, at : at + c, cell * c : (cell + 1) * c] = value
    for i in range(packed.shape[1]):
        packed[layer, i, 2 * c : 3 * c, :c] = zero
        packed[layer, i, 3 * c :, c:] = zero


def window(wide, row, start, size):
    c = wide.shape[2] // 2
    here = wide[row, start + RUNS : start + RUNS + size]
    after = wide[row, start + 2 * RUNS : start + 2 * RUNS + size, :c]
    before = wide[row, start : start + size, c:]
    return jnp.concatenate([here, after, before], axis=1)


def dot(a, b):
    return jnp.dot(a, b, preferred_element_type=F32)


def halves(x):
    high = x.astype(BF)
    return high, (x - high.astype(F32)).astype(BF)


def silu_of_half(half):
    return half + half * jnp.tanh(half)


def conv_pair(d, packed, layer):
    if WINOGRAD:
        inputs = (d[0] - d[2], d[1] + d[2], d[2] - d[1], d[1] - d[3])
        m = [dot(x, packed[layer, i]) for i, x in enumerate(inputs)]
        return (m[1] + m[2]) + m[0], m[1] - m[2] - m[3]
    w = jnp.concatenate([packed[layer, i] for i in range(3)], axis=0)
    return tuple(dot(jnp.concatenate(d[i : i + 3], axis=1), w) for i in range(2))


class Rows:
    def __init__(self, *held):
        self.at = {}
        for ref, first in held:
            self.at.update({first + i: (ref, i) for i in range(ref.shape[0])})

    def __getitem__(self, row):
        return self.at[row]


def conv_rows(src, dst, span, layer, packed, bias, edge, rows):
    ref = src[span[0]][0]
    width = ref.shape[1] - 2 * RUNS
    tile = tile_of(width // RUNS)
    both = 0.5 * jnp.concatenate([bias[layer : layer + 1]] * 2, axis=1)
    for pair in range(*span, 2):
        for start in range(0, width, tile):
            sums = conv_pair(
                [window(*src[pair + i - 1], start, tile) for i in range(4)], packed, layer
            )
            for i, total in enumerate(sums):
                row = pair + i
                y = silu_of_half(total + both)
                if row < 0:
                    y = y * edge[0]
                elif row >= rows:
                    y = y * edge[1]
                if callable(dst):
                    dst(row, start, y.astype(BF))
                else:
                    ref, at = dst[row]
                    ref[at, start + RUNS : start + RUNS + tile] = y.astype(BF)
        if not callable(dst):
            for i in range(2):
                close_row(*dst[pair + i])


def transform(forward, held, kept, sent):
    core = lax.rem(lax.axis_index("lon"), 2)
    rows, c = held.shape[0], held.shape[2] // 2
    for row in range(0, rows, 2):
        cells = [
            jnp.concatenate([held[row + i, :, e * c : (e + 1) * c] for i in range(2)], axis=1)
            for e in range(2)
        ]
        total = dot(forward[core], jnp.concatenate(cells, axis=0))
        half = total.shape[0] // 2
        lanes = slice(row * c, (row + 2) * c)
        kept[:, lanes] = total[:half]
        sent[:, lanes] = total[half:]


def pack_cells(body, ends, source, line, wide, at):
    cells = body.shape[1]
    line[0:PAD] = ends[source, :PAD].astype(F32)
    line[PAD : PAD + cells] = body[source].astype(F32)
    line[PAD + cells : 2 * PAD + cells] = ends[source, PAD:].astype(F32)
    pack_row(line, wide, at)
    close_row(wide, at)


def product(a, b, sign, start, tile, packed, layer, index):
    left, right = window(*a, start, tile), window(*b, start, tile)
    return dot(left + right if sign > 0 else left - right, packed[layer, index])


def put(dst, start, half, bias, layer):
    ref, at = dst
    both = 0.5 * jnp.concatenate([bias[layer : layer + 1]] * 2, axis=1)
    y = silu_of_half(half + both).astype(BF)
    ref[at, start + RUNS : start + RUNS + y.shape[0]] = y


def spans(ref):
    width = ref.shape[1] - 2 * RUNS
    tile = tile_of(width // RUNS)
    return [(start, tile) for start in range(0, width, tile)]


def early_part(field, inner, sums, packed, bias):
    x, y = Rows((field, 0)), Rows((inner, 1))
    for start, tile in spans(field):
        span = slice(start, start + tile)
        args = (start, tile, packed, 0)
        m1 = product(x[0], x[1], 1, *args, 1)
        m2 = product(x[1], x[0], -1, *args, 2)
        m3 = product(x[0], x[2], -1, *args, 3)
        sums[0, span] = m1 + m2
        put(y[1], start, m1 - m2 - m3, bias, 0)
        m0 = product(x[1], x[3], -1, *args, 0)
        m1 = product(x[2], x[3], 1, *args, 1)
        m2 = product(x[3], x[2], -1, *args, 2)
        sums[1, span] = m1 - m2
        put(y[2], start, (m1 + m2) + m0, bias, 0)
    close_row(*y[1])
    close_row(*y[2])
    for start, tile in spans(field):
        span = slice(start, start + tile)
        args = (start, tile, packed, 1)
        m1 = product(y[1], y[2], 1, *args, 1)
        m2 = product(y[2], y[1], -1, *args, 2)
        sums[2, span] = m1 + m2
        sums[3, span] = m1 - m2


def lower_part(field, inner, sums, first, second, packed, bias, edge, rows):
    x, y, z = Rows((field, 0)), Rows((inner, 1), (first, 3)), Rows((second, 3))
    for start, tile in spans(field):
        m3 = product(x[2], x[4], -1, start, tile, packed, 0, 3)
        put(y[3], start, sums[1, start : start + tile] - m3, bias, 0)
    close_row(*y[3])
    conv_rows(x, y, (4, 6), 0, packed, bias, edge, rows)
    conv_rows(y, z, (3, 5), 1, packed, bias, edge, rows)


def upper_part(before, field, inner, sums, first, second, more, packed, bias, edge, emit):
    rows = field.shape[0] - HALO
    x = Rows((before, -HALO), (field, 0))
    y = Rows((more[0], -2), (inner, 1), (first, 3))
    z = Rows((more[1], -1), (second, 3))
    conv_rows(x, y, (-2, 0), 0, packed, bias, edge, rows)
    for start, tile in spans(field):
        m0 = product(x[-1], x[1], -1, start, tile, packed, 0, 0)
        put(y[0], start, sums[0, start : start + tile] + m0, bias, 0)
    close_row(*y[0])
    conv_rows(y, z, (-1, 1), 1, packed, bias, edge, rows)
    for start, tile in spans(field):
        span = slice(start, start + tile)
        m0 = product(y[0], y[2], -1, start, tile, packed, 1, 0)
        m3 = product(y[1], y[3], -1, start, tile, packed, 1, 3)
        put(z[1], start, sums[2, span] + m0, bias, 1)
        put(z[2], start, sums[3, span] - m3, bias, 1)
    close_row(*z[1])
    close_row(*z[2])
    conv_rows(z, emit, (0, rows), 2, packed, bias, edge, rows)


def prepare_kernel(own, own_edge, kernels, bias, after, field, packed, later, inner, sums, line):
    rows = own.shape[0]
    for layer in range(CONVS):
        build_weights(kernels, 0, packed, layer)
        build_weights(kernels, 1, later, layer)
    for row in range(rows):
        pack_cells(own, own_edge, flip(row, rows), line.at[row % 2], field, row)
    early_part(field, inner, sums, packed, bias)


def first_lower_kernel(
    down, down_edge, own, packed, inner, sums, bias, field, first, second, line
):
    rows = own.shape[0]
    field[:rows] = own[...]
    for row in range(HALO):
        pack_cells(down, down_edge, flip(row, HALO), line.at[row % 2], field, rows + row)
    lower_part(field, inner, sums, first, second, packed, bias, lat_edges(), rows)


def first_upper_kernel(
    up, up_edge, field, first, second, inner, sums, packed, bias, forward,
    kept, sent, hidden, to_partner, to_other, before,
    line, more, most, held,
):
    rows = field.shape[0] - HALO
    for row in range(HALO):
        pack_cells(up, up_edge, flip(row, HALO), line.at[row % 2], before, row)

    def emit(row, start, y):
        span = slice(start, start + y.shape[0])
        held[row, span] = y
        hidden[row, span] = y
        if row < HALO:
            to_other[HALO - 1 - row, span] = y
        if row >= rows - HALO:
            to_partner[rows - 1 - row, span] = y

    args = (before, field, inner, sums, first, second, (more, most), packed, bias)
    upper_part(*args, lat_edges(), emit)
    transform(forward, held, kept, sent)


def pair_kernel(kept, got, *outs):
    chip = lax.div(lax.axis_index("lon"), 2)
    rows = outs[0].shape[0]
    for step, out in enumerate(outs):
        span = pl.ds(pl.multiple_of((chip ^ step) * rows, rows), rows)
        out[...] = kept[span, :] + got[span, :]


def mix_kernel(turn, real, imag, *rest):
    *sums, mixed, spread_in, spread_out = rest
    me = lax.axis_index("lon")
    modes, c = real.shape[1], real.shape[2]
    high, low = halves(jnp.concatenate([x[...] for x in sums], axis=0))
    summed = dot(turn[me], high)
    summed = summed[: 2 * modes] + summed[2 * modes :]
    summed = summed + dot(turn[me, : 2 * modes], low)
    rows = summed.shape[1] // c
    for half in range(2):
        for row in range(rows):
            spread_in[pl.ds(half * rows + row, modes, stride=2 * rows), :] = summed[
                half * modes : (half + 1) * modes, row * c : (row + 1) * c
            ]
    sign = jnp.where(lax.broadcasted_iota(jnp.int32, (2 * rows, c), 0) < rows, -1.0, 1.0)
    for k in range(modes):
        wide = spread_in[2 * rows * k : 2 * rows * (k + 1)]
        both = jnp.concatenate(halves(wide), axis=0)
        weight = jnp.concatenate([real[0, k], imag[0, k]], axis=1)
        out = jnp.dot(both, weight, preferred_element_type=F32)
        out = out[: 2 * rows] + out[2 * rows :]
        turned = pltpu.roll(out[:, c:], rows, 0)
        spread_out[2 * rows * k : 2 * rows * (k + 1)] = out[:, :c] + sign * turned
    for row in range(rows):
        parts = [spread_out[pl.ds(i * rows + row, modes, stride=2 * rows), :] for i in range(2)]
        mixed[:, row * c : (row + 1) * c] = jnp.concatenate(parts, axis=0)


def halo_kernel(mixed, out):
    c = out.shape[1] // HALO
    rows = mixed.shape[1] // c
    even = lax.rem(lax.axis_index("lon"), 2) == 0
    for at in range(HALO):
        last = mixed[:, (rows - 1 - at) * c : (rows - at) * c]
        leading = mixed[:, (HALO - 1 - at) * c : (HALO - at) * c]
        out[:, at * c : (at + 1) * c] = jnp.where(even, last, leading).astype(BF)


def pick(mine, other, first):
    even = lax.rem(lax.axis_index("lon"), 2) == 0
    return jnp.where(even == first, mine[...], other[...])


def wave_of(inverse, mixed):
    if mixed.dtype == BF:
        return dot(inverse, mixed)
    high, low = halves(mixed)
    return dot(inverse, high) + dot(inverse, low)


def next_state(old, conv, mixed, inverse, new, at, count, mask):
    c = mixed.shape[1] // conv[0].shape[0]
    width = conv[0].shape[1]
    tile = tile_of(width // RUNS)
    for pair in range(0, count, 2):
        lanes = slice(pair * c, min(pair + 2, count) * c)
        for start in range(0, width, tile):
            span = slice(start, start + tile)
            wide = slice(start + RUNS, start + RUNS + tile)
            waves = [wave_of(inverse[e, span], mixed[:, lanes]) for e in range(2)]
            for i in range(min(2, count - pair)):
                wave = jnp.concatenate([w[:, i * c : (i + 1) * c] for w in waves], axis=1)
                total = old[0][old[1] + pair + i, wide].astype(F32)
                total = total + conv[0][pair + i, span].astype(F32) + wave
                total = jnp.tanh(total)
                if mask is not None:
                    total = total * mask
                new[at + pair + i, wide] = total.astype(BF)
        for i in range(min(2, count - pair)):
            close_row(new, at + pair + i)


def middle_own_kernel(field, hidden, mixed, inverse, packed, bias, state, inner, sums):
    next_state((field, 0), (hidden,), mixed, inverse, state, 0, hidden.shape[0], None)
    early_part(state, inner, sums, packed, bias)


def middle_lower_kernel(
    field, from_down, mine, other, own, inner, sums, inverse, packed, bias,
    state, first, second, mixed_down,
):
    rows = own.shape[0]
    edge = lat_edges()
    state[:rows] = own[...]
    mixed_down[...] = pick(mine, other, True)
    next_state((field, rows), (from_down,), mixed_down, inverse, state, rows, HALO, edge[1])
    lower_part(state, inner, sums, first, second, packed, bias, edge, rows)


def middle_upper_kernel(
    before, from_up, mine, other, inverse, state, first, second, inner, sums,
    packed, bias, forward,
    kept, sent, hidden, above, mixed_up, more, most, held,
):
    edge = lat_edges()
    mixed_up[...] = pick(mine, other, False)
    next_state((before, 0), (from_up,), mixed_up, inverse, above, 0, HALO, edge[0])

    def emit(row, start, y):
        span = slice(start, start + y.shape[0])
        held[row, span] = y
        hidden[row, span] = y

    args = (above, state, inner, sums, first, second, (more, most), packed, bias)
    upper_part(*args, edge, emit)
    transform(forward, held, kept, sent)


def last_kernel(state, hidden, mixed, inverse, result, line, done, sems):
    rows, width, c = hidden.shape[0], hidden.shape[1], hidden.shape[2] // 2
    cells = result.shape[1]
    run = 2 * width // RUNS
    copies = []
    for pair in range(0, rows, 2):
        lanes = slice(pair * c, (pair + 2) * c)
        waves = [wave_of(inverse[e], mixed[:, lanes]) for e in range(2)]
        for i in range(2):
            row = pair + i
            for e in range(2):
                lanes = slice(e * c, (e + 1) * c)
                total = state[row, RUNS : RUNS + width, lanes].astype(F32) + hidden[row, :, lanes].astype(F32)
                total = jnp.tanh(total + waves[e][:, i * c : (i + 1) * c])
                for u in range(width // RUNS):
                    value = total[u * RUNS : (u + 1) * RUNS]
                    line[i, pl.ds(2 * u + e, RUNS, stride=run), :] = value
            done[row] = line[i, PAD : PAD + cells].astype(BF)
            copy = pltpu.make_async_copy(done.at[row], result.at[flip(row, rows)], sems.at[row])
            copy.start()
            copies.append(copy)
    for copy in copies:
        copy.wait()


def cell_order(width):
    run = width // RUNS
    cell = np.arange(width // 2) // RUNS * 2 + np.arange(width // 2) % RUNS * run
    return np.stack([cell, cell + 1])


def forward_table(cells, lon_total, modes, lon_size):
    order = cell_order(cells + 2 * PAD).reshape(-1) - PAD
    inside = (order >= 0) & (order < cells)
    waves = np.arange(modes)
    tables = []
    for core in range(2):
        theta = (2 * np.pi / lon_total) * (np.outer(waves, order + core * cells) % lon_total)
        full = np.stack([np.cos(theta), -np.sin(theta)], 0) * inside
        full = full.reshape(2, lon_size // 2, 2, modes // lon_size, -1)
        full = full.transpose(2, 1, 0, 3, 4)[[core, 1 - core]]
        tables.append(full.reshape(2 * modes, -1).astype(ml_dtypes.bfloat16))
    return np.stack(tables)


def turn_table(lon_size, local, scale):
    chips = lon_size // 2
    me = np.arange(lon_size)[:, None, None]
    waves = me * local + np.arange(local)[:, None]
    source = 2 * ((me // 2) ^ np.arange(chips))
    phase = source * waves % lon_size * (2 * np.pi / lon_size)
    cos, sin = scale * np.cos(phase), scale * np.sin(phase)
    eye = np.eye(local)
    cos, sin = (x[:, :, :, None] * eye[:, None, :] for x in (cos, sin))
    real = np.stack([cos, sin], axis=3)
    imag = np.stack([-sin, cos], axis=3)
    full = np.concatenate([real, imag], axis=1)
    full = full.reshape(lon_size, 2 * local, chips * 2 * local).astype(np.float32)
    high = full.astype(ml_dtypes.bfloat16)
    low = (full - high.astype(np.float32)).astype(ml_dtypes.bfloat16)
    return np.concatenate([high, low], axis=1)


def inverse_parts(cells, lon_total, modes, lon_size):
    column = np.arange(2 * modes)
    local = modes // lon_size
    waves = column // (2 * local) * local + column % local
    imaginary = column // local % 2 == 1
    order = cell_order(cells + 2 * PAD) - PAD
    theta = (2 * np.pi / lon_total) * (order[:, :, None] * waves % lon_total)
    weight = np.where(waves == 0, 1.0, 2.0)
    cos, sin = weight * np.cos(theta), weight * np.sin(theta)
    by_cos = np.where(imaginary, -sin, cos).astype(np.float32)
    by_sin = np.where(imaginary, -cos, -sin).astype(np.float32)
    return waves.astype(np.int32), by_cos, by_sin


def phase_table(cells, lon_total, modes, lon_size):
    waves = inverse_parts(cells, lon_total, modes, lon_size)[0]
    phase = np.arange(lon_size)[:, None] * waves % lon_size * (2 * np.pi / lon_size)
    return np.stack([np.cos(phase), np.sin(phase)], 1).astype(np.float32)


def facing(rows, partner):
    odd = odd_lat()
    return (rows - HALO) * ((1 - odd) if partner else odd)


def slice_kernel(field, *rest):
    out, sem = rest[-2:]
    at = facing(field.shape[0], len(rest) == 2)
    copy = pltpu.make_async_copy(field.at[pl.ds(at, HALO)], out, sem)
    copy.start()
    copy.wait()


def side_kernel(field, after, last, leading, sems):
    cells = field.shape[1]
    first = pltpu.make_async_copy(field.at[:, cells - PAD :], last, sems.at[0])
    second = pltpu.make_async_copy(field.at[:, :PAD], leading, sems.at[1])
    first.start()
    second.start()
    first.wait()
    second.wait()


def edge_kernel(from_left, from_right, edges, near):
    rows = from_left.shape[0]
    for row in range(rows):
        edges[row] = jnp.concatenate([from_left[row], from_right[row]], axis=0)
    at = facing(rows, True)
    for row in range(HALO):
        near[row] = jnp.concatenate([from_left[at + row], from_right[at + row]], axis=0)


def copy_kernel(edges, near, other):
    at = facing(edges.shape[0], False)
    for row in range(HALO):
        other[row] = edges[at + row]


def inverse_kernel(parts, phase, after, inverse):
    turn = phase[lax.axis_index("lon")]
    for e in range(2):
        inverse[e] = (parts[0, e] * turn[0:1] + parts[1, e] * turn[1:2]).astype(BF)


def lat_edges():
    me, size, odd = lax.axis_index("lat"), lax.axis_size("lat"), odd_lat()
    after, before = (me < size - 1).astype(F32), (me > 0).astype(F32)
    even = (1 - odd).astype(F32)
    return [even * before + (1.0 - even) * after, even * after + (1.0 - even) * before]


def lat_pairs(partner):
    pairs = [(i, i + 1) for i in range(0 if partner else 1, lax.axis_size("lat") - 1, 2)]
    return pairs + [(j, i) for i, j in pairs]


def move(array, partner):
    return lax.ppermute(array, "lat", lat_pairs(partner))


def shape(*dims):
    return jax.ShapeDtypeStruct(dims, BF)


def call(kernel, args, outs, scratch, in_specs=None, out_specs=None, grid=(), cost=0):
    estimate = pl.CostEstimate(flops=int(cost * 8e8), bytes_accessed=0, transcendentals=0)
    return pl.pallas_call(
        kernel,
        grid=grid,
        out_shape=outs,
        in_specs=in_specs or [VMEM] * len(args),
        out_specs=out_specs or [VMEM] * len(outs),
        scratch_shapes=scratch,
        compiler_params=PARAMS,
        cost_estimate=estimate if cost else None,
    )(*(jnp.asarray(arg) for arg in args))


def per_device(field, conv_weight, conv_bias, spec_real, spec_imag):
    rows, cells, c = field.shape
    width = cells + 2 * PAD
    half = width // 2
    lon_size = lax.axis_size("lon")
    lon_total = cells * lon_size
    local = spec_real.shape[1]
    modes = local * lon_size

    wide = half + 2 * RUNS
    below = call(
        slice_kernel, (field,), [shape(HALO, cells, c)], [DMA], in_specs=[HBM], out_specs=[ANY]
    )[0]
    down = move(below, True)
    above = call(
        slice_kernel,
        (field, below),
        [shape(HALO, cells, c)],
        [DMA],
        in_specs=[HBM, ANY],
        out_specs=[ANY],
    )[0]
    up = move(above, False)
    last, leading = call(
        side_kernel,
        (field, above),
        [shape(rows, PAD, c)] * 2,
        [pltpu.SemaphoreType.DMA((2,))],
        in_specs=[HBM, ANY],
        out_specs=[ANY] * 2,
    )
    right = [(i, (i + 1) % lon_size) for i in range(lon_size)]
    left = [(j, i) for i, j in right]
    from_left = lax.ppermute(last, "lon", right)
    from_right = lax.ppermute(leading, "lon", left)
    own_edge, below = call(
        edge_kernel,
        (from_left, from_right),
        [shape(rows, 2 * PAD, c), shape(HALO, 2 * PAD, c)],
        [],
    )
    down_edge = move(below, True)
    above = call(
        copy_kernel, (own_edge, below), [shape(HALO, 2 * PAD, c)], [], in_specs=[VMEM, ANY]
    )[0]
    up_edge = move(above, False)
    tables = (cells, lon_total, modes, lon_size)
    inverse = call(
        inverse_kernel,
        (np.stack(inverse_parts(*tables)[1:]), phase_table(*tables), above),
        [shape(2, half, 2 * modes)],
        [],
        in_specs=[VMEM, VMEM, ANY],
    )[0]
    forward = forward_table(*tables)
    turn = turn_table(lon_size, local, 1.0 / lon_total)

    line = pltpu.VMEM((2, width + 2 * half // RUNS + 8, c), F32)
    weights = shape(CONVS, 4 if WINOGRAD else 3, 4 * c, 2 * c)
    lower = [shape(n, wide, 2 * c) for n in (rows + HALO, 3, 2)]
    early = [shape(2, wide, 2 * c), jax.ShapeDtypeStruct((4, half, 2 * c), F32)]
    gathered = pltpu.VMEM((2 * modes, HALO * c), BF)
    upper = [pltpu.VMEM((4, wide, 2 * c), BF)] * 2 + [pltpu.VMEM((rows, half, 2 * c), BF)]
    hidden_shape = shape(rows, half, 2 * c)
    part_shape = [jax.ShapeDtypeStruct((modes, rows * c), F32)] * 2

    own_rows = shape(rows, wide, 2 * c)
    own, packed, later, *inner = call(
        prepare_kernel,
        (field, own_edge, conv_weight, conv_bias[0], inverse),
        [own_rows, weights, weights] + early,
        [line],
        in_specs=[VMEM] * 4 + [ANY],
        cost=4,
    )
    low = call(
        first_lower_kernel,
        (down, down_edge, own, packed, *inner, conv_bias[0]),
        lower,
        [line],
    )
    kept, sent, hidden, to_partner, to_other, before = call(
        first_upper_kernel,
        (up, up_edge, *low, *inner, packed, conv_bias[0], forward),
        part_shape
        + [hidden_shape]
        + [shape(HALO, half, 2 * c)] * 2
        + [shape(HALO, wide, 2 * c)],
        [line] + upper,
    )
    def swap(array, step):
        return lax.ppermute(array, "lon", [(i, i ^ step) for i in range(lon_size)])

    chunk = jax.ShapeDtypeStruct((2 * local, rows * c), F32)

    def pair(kept, sent):
        return call(pair_kernel, (kept, swap(sent, 1)), [chunk] * (lon_size // 2), [])

    def mix(own, others, block):
        sums = [own] + [swap(other, 2 * i + 2) for i, other in enumerate(others)]
        turned = pltpu.VMEM((2 * rows * (local + 1), c), F32)
        weights = pl.BlockSpec((1, local, c, c), lambda i: (block, 0, 0, 0))
        (mixed,) = call(
            mix_kernel,
            (turn, spec_real, spec_imag, *sums),
            [chunk],
            [turned, turned],
            in_specs=[VMEM, weights, weights] + [VMEM] * len(sums),
            grid=(1,),
        )
        return lax.all_gather(mixed, "lon", axis=0, tiled=True)

    from_down, from_up = move(to_partner, True), move(to_other, False)
    own, *others = pair(kept, sent)
    mixed = mix(own, others, 0)
    halo = call(halo_kernel, (mixed,), [shape(2 * modes, HALO * c)], [])[0]
    lat_size = lax.axis_size("lat")
    ways = []
    for i in range(lon_size):
        ways += [(i * lat_size + j, i * lat_size + k) for j, k in lat_pairs(i % 2 == 0)]
    mine = lax.ppermute(halo, ("lon", "lat"), ways)
    own, *inner = call(
        middle_own_kernel,
        (low[0], hidden, mixed, inverse, later, conv_bias[1]),
        [own_rows] + early,
        [],
        cost=3,
    )
    other = swap(lax.optimization_barrier((mine, own))[0], 1)
    state, *low = call(
        middle_lower_kernel,
        (low[0], from_down, mine, other, own, *inner, inverse, later, conv_bias[1]),
        lower,
        [gathered],
    )
    kept, sent, hidden = call(
        middle_upper_kernel,
        (before, from_up, mine, other, inverse, state, *low, *inner)
        + (later, conv_bias[1], forward),
        part_shape + [hidden_shape],
        [pltpu.VMEM((HALO, wide, 2 * c), BF), gathered] + upper,
    )
    own, *others = pair(kept, sent)
    mixed = mix(own, others, 1)
    (result,) = call(
        last_kernel,
        (state, hidden, mixed, inverse),
        [shape(rows, cells, c)],
        [line, pltpu.VMEM((rows, cells, c), BF), pltpu.SemaphoreType.DMA((rows,))],
        out_specs=[ANY],
    )
    return result


def solution(mesh):
    return jax.shard_map(
        per_device,
        mesh=mesh,
        in_specs=(
            P("lat", "lon", None),
            P(),
            P(),
            P(None, "lon", None, None),
            P(None, "lon", None, None),
        ),
        out_specs=P("lat", "lon", None),
        check_vma=False,
    )
```

```python
import math

import jax
import jax.numpy as jnp
import ml_dtypes
import numpy as np
from jax import lax
from jax.experimental import pallas as pl
from jax.experimental.pallas import tpu as pltpu
from jax.sharding import PartitionSpec as P

BLOCKS = 2
CONVS = 3
PAD = 16
RUNS = 16
HALO = 3
WINOGRAD = True
BF = jnp.bfloat16
F32 = jnp.float32
VMEM = pl.BlockSpec(memory_space=pltpu.VMEM)
ANY = pl.BlockSpec(memory_space=pl.ANY)
HBM = pl.BlockSpec(memory_space=pltpu.HBM)
DMA = pltpu.SemaphoreType.DMA
PARAMS = pltpu.CompilerParams(vmem_limit_bytes=28 << 20)


def odd_lat():
    return lax.rem(lax.axis_index("lat"), 2)


def flip(row, rows):
    return row + odd_lat() * (rows - 1 - 2 * row)


def tile_of(tiles):
    return max(n for n in range(1, 34) if tiles % n == 0) * RUNS


def pack_row(line, wide, row):
    c = line.shape[1]
    run = 2 * (wide.shape[1] // RUNS - 2)
    for cell in range(run):
        lanes = slice(cell % 2 * c, (cell % 2 + 1) * c)
        at = RUNS * (cell // 2 + 1)
        wide[row, at : at + RUNS, lanes] = line[pl.ds(cell, RUNS, stride=run), :].astype(BF)


def close_row(wide, row):
    c = wide.shape[2] // 2
    end = wide.shape[1] - RUNS
    before = wide[row, end - RUNS : end, c:].astype(F32)
    wide[row, 0:RUNS, c:] = pltpu.roll(before, 1, 0).astype(BF)
    after = wide[row, RUNS : 2 * RUNS, :c].astype(F32)
    wide[row, end : end + RUNS, :c] = pltpu.roll(after, RUNS - 1, 0).astype(BF)


def build_weights(kernels, block, packed, layer):
    c = kernels.shape[-1]
    zero = jnp.zeros((c, c), BF)
    for tap in range(3):
        g0, g1, g2 = (kernels[block, layer, flip(a, 3), tap].astype(F32) for a in range(3))
        if WINOGRAD:
            outer = g0 + g2
            parts = (0.5 * g0, 0.25 * (outer + g1), 0.25 * (outer - g1), 0.5 * g2)
        else:
            parts = (0.5 * g0, 0.5 * g1, 0.5 * g2)
        for i, part in enumerate(parts):
            value = part.astype(BF)
            for cell in range(2):
                source = cell + tap - 1
                at = {0: 0, 1: c, 2: 2 * c, -1: 3 * c}[source]
                packed[layer, i, at : at + c, cell * c : (cell + 1) * c] = value
    for i in range(packed.shape[1]):
        packed[layer, i, 2 * c : 3 * c, :c] = zero
        packed[layer, i, 3 * c :, c:] = zero


def window(wide, row, start, size):
    c = wide.shape[2] // 2
    here = wide[row, start + RUNS : start + RUNS + size]
    after = wide[row, start + 2 * RUNS : start + 2 * RUNS + size, :c]
    before = wide[row, start : start + size, c:]
    return jnp.concatenate([here, after, before], axis=1)


def dot(a, b):
    return jnp.dot(a, b, preferred_element_type=F32)


def silu_of_half(half):
    return half + half * jnp.tanh(half)


def conv_pair(d, packed, layer):
    if WINOGRAD:
        inputs = (d[0] - d[2], d[1] + d[2], d[2] - d[1], d[1] - d[3])
        m = [dot(x, packed[layer, i]) for i, x in enumerate(inputs)]
        return (m[1] + m[2]) + m[0], m[1] - m[2] - m[3]
    w = jnp.concatenate([packed[layer, i] for i in range(3)], axis=0)
    return tuple(dot(jnp.concatenate(d[i : i + 3], axis=1), w) for i in range(2))


class Rows:
    def __init__(self, *held):
        self.at = {}
        for ref, first in held:
            self.at.update({first + i: (ref, i) for i in range(ref.shape[0])})

    def __getitem__(self, row):
        return self.at[row]


def conv_rows(src, dst, span, layer, packed, bias, edge, rows):
    ref = src[span[0]][0]
    width = ref.shape[1] - 2 * RUNS
    tile = tile_of(width // RUNS)
    both = 0.5 * jnp.concatenate([bias[layer : layer + 1]] * 2, axis=1)
    for pair in range(*span, 2):
        for start in range(0, width, tile):
            sums = conv_pair(
                [window(*src[pair + i - 1], start, tile) for i in range(4)], packed, layer
            )
            for i, total in enumerate(sums):
                row = pair + i
                y = silu_of_half(total + both)
                if row < 0:
                    y = y * edge[0]
                elif row >= rows:
                    y = y * edge[1]
                if callable(dst):
                    dst(row, start, y.astype(BF))
                else:
                    ref, at = dst[row]
                    ref[at, start + RUNS : start + RUNS + tile] = y.astype(BF)
        if not callable(dst):
            for i in range(2):
                close_row(*dst[pair + i])


def transform(forward, leak, bias, held, kept, sent):
    core = lax.rem(lax.axis_index("lon"), 2)
    rows, c = held.shape[0], held.shape[2] // 2
    half = 0.5 * bias[CONVS - 1 : CONVS]
    level = silu_of_half(half)
    for row in range(0, rows, 2):
        cells = [
            jnp.concatenate([held[row + i, :, e * c : (e + 1) * c] for i in range(2)], axis=1)
            for e in range(2)
        ]
        total = dot(forward[core], jnp.concatenate(cells, axis=0))
        modes2 = total.shape[0]
        total = total - leak[core] * jnp.concatenate([level, level], axis=1)
        lanes = slice(row * c, (row + 2) * c)
        kept[:, lanes] = total[: modes2 // 2]
        sent[:, lanes] = total[modes2 // 2 :]


def pack_cells(body, ends, source, line, wide, at):
    cells = body.shape[1]
    line[0:PAD] = ends[source, :PAD].astype(F32)
    line[PAD : PAD + cells] = body[source].astype(F32)
    line[PAD + cells : 2 * PAD + cells] = ends[source, PAD:].astype(F32)
    pack_row(line, wide, at)
    close_row(wide, at)


def product(a, b, sign, start, tile, packed, layer, index):
    left, right = window(*a, start, tile), window(*b, start, tile)
    return dot(left + right if sign > 0 else left - right, packed[layer, index])


def put(dst, start, half, bias, layer):
    ref, at = dst
    both = 0.5 * jnp.concatenate([bias[layer : layer + 1]] * 2, axis=1)
    y = silu_of_half(half + both).astype(BF)
    ref[at, start + RUNS : start + RUNS + y.shape[0]] = y


def spans(ref):
    width = ref.shape[1] - 2 * RUNS
    tile = tile_of(width // RUNS)
    return [(start, tile) for start in range(0, width, tile)]


def early_part(field, inner, sums, packed, bias):
    x, y = Rows((field, 0)), Rows((inner, 1))
    for start, tile in spans(field):
        span = slice(start, start + tile)
        args = (start, tile, packed, 0)
        m1 = product(x[0], x[1], 1, *args, 1)
        m2 = product(x[1], x[0], -1, *args, 2)
        m3 = product(x[0], x[2], -1, *args, 3)
        sums[0, span] = m1 + m2
        put(y[1], start, m1 - m2 - m3, bias, 0)
        m0 = product(x[1], x[3], -1, *args, 0)
        m1 = product(x[2], x[3], 1, *args, 1)
        m2 = product(x[3], x[2], -1, *args, 2)
        sums[1, span] = m1 - m2
        put(y[2], start, (m1 + m2) + m0, bias, 0)
    close_row(*y[1])
    close_row(*y[2])
    for start, tile in spans(field):
        span = slice(start, start + tile)
        args = (start, tile, packed, 1)
        m1 = product(y[1], y[2], 1, *args, 1)
        m2 = product(y[2], y[1], -1, *args, 2)
        sums[2, span] = m1 + m2
        sums[3, span] = m1 - m2


def lower_part(field, inner, sums, first, second, packed, bias, edge, rows):
    x, y, z = Rows((field, 0)), Rows((inner, 1), (first, 3)), Rows((second, 3))
    for start, tile in spans(field):
        m3 = product(x[2], x[4], -1, start, tile, packed, 0, 3)
        put(y[3], start, sums[1, start : start + tile] - m3, bias, 0)
    close_row(*y[3])
    conv_rows(x, y, (4, 6), 0, packed, bias, edge, rows)
    conv_rows(y, z, (3, 5), 1, packed, bias, edge, rows)


def upper_part(before, field, inner, sums, first, second, more, packed, bias, edge, emit):
    rows = field.shape[0] - HALO
    x = Rows((before, -HALO), (field, 0))
    y = Rows((more[0], -2), (inner, 1), (first, 3))
    z = Rows((more[1], -1), (second, 3))
    conv_rows(x, y, (-2, 0), 0, packed, bias, edge, rows)
    for start, tile in spans(field):
        m0 = product(x[-1], x[1], -1, start, tile, packed, 0, 0)
        put(y[0], start, sums[0, start : start + tile] + m0, bias, 0)
    close_row(*y[0])
    conv_rows(y, z, (-1, 1), 1, packed, bias, edge, rows)
    for start, tile in spans(field):
        span = slice(start, start + tile)
        m0 = product(y[0], y[2], -1, start, tile, packed, 1, 0)
        m3 = product(y[1], y[3], -1, start, tile, packed, 1, 3)
        put(z[1], start, sums[2, span] + m0, bias, 1)
        put(z[2], start, sums[3, span] - m3, bias, 1)
    close_row(*z[1])
    close_row(*z[2])
    conv_rows(z, emit, (0, rows), 2, packed, bias, edge, rows)


def prepare_kernel(own, own_edge, kernels, bias, after, field, packed, later, inner, sums, line):
    rows = own.shape[0]
    for layer in range(CONVS):
        build_weights(kernels, 0, packed, layer)
        build_weights(kernels, 1, later, layer)
    for row in range(rows):
        pack_cells(own, own_edge, flip(row, rows), line.at[row % 2], field, row)
    early_part(field, inner, sums, packed, bias)


def first_lower_kernel(
    down, down_edge, own, packed, inner, sums, bias, field, first, second, line
):
    rows = own.shape[0]
    field[:rows] = own[...]
    for row in range(HALO):
        pack_cells(down, down_edge, flip(row, HALO), line.at[row % 2], field, rows + row)
    lower_part(field, inner, sums, first, second, packed, bias, lat_edges(), rows)


def first_upper_kernel(
    up, up_edge, field, first, second, inner, sums, packed, bias, forward, leak,
    kept, sent, hidden, to_partner, to_other, before,
    line, more, most, held,
):
    rows = field.shape[0] - HALO
    for row in range(HALO):
        pack_cells(up, up_edge, flip(row, HALO), line.at[row % 2], before, row)

    def emit(row, start, y):
        span = slice(start, start + y.shape[0])
        held[row, span] = y
        hidden[row, span] = y
        if row < HALO:
            to_other[HALO - 1 - row, span] = y
        if row >= rows - HALO:
            to_partner[rows - 1 - row, span] = y

    args = (before, field, inner, sums, first, second, (more, most), packed, bias)
    upper_part(*args, lat_edges(), emit)
    transform(forward, leak, bias, held, kept, sent)


def pair_kernel(kept, got, *outs):
    chip = lax.div(lax.axis_index("lon"), 2)
    rows = outs[0].shape[0]
    for step, out in enumerate(outs):
        span = pl.ds(pl.multiple_of((chip ^ step) * rows, rows), rows)
        out[...] = (kept[span, :] + got[span, :]).astype(BF)


def mix_kernel(turn, real, imag, bias, *rest):
    *sums, mixed, spread_in, spread_out = rest
    me = lax.axis_index("lon")
    modes, c = real.shape[1], real.shape[2]
    summed = dot(turn[me], jnp.concatenate([x[...] for x in sums], axis=0))
    summed = summed[: 2 * modes] + summed[2 * modes :]
    rows = summed.shape[1] // c
    level = (me == 0).astype(F32) * silu_of_half(0.5 * bias[CONVS - 1 : CONVS])
    for half in range(2):
        for row in range(rows):
            spread_in[pl.ds(half * rows + row, modes, stride=2 * rows), :] = summed[
                half * modes : (half + 1) * modes, row * c : (row + 1) * c
            ]
    spread_in[0:rows] = spread_in[0:rows] + level
    sign = jnp.where(lax.broadcasted_iota(jnp.int32, (2 * rows, c), 0) < rows, -1.0, 1.0)
    for k in range(modes):
        wide = spread_in[2 * rows * k : 2 * rows * (k + 1)]
        high = wide.astype(BF)
        low = (wide - high.astype(F32)).astype(BF)
        both = jnp.concatenate([high, low], axis=0)
        weight = jnp.concatenate([real[0, k], imag[0, k]], axis=1)
        out = jnp.dot(both, weight, preferred_element_type=F32)
        out = out[: 2 * rows] + out[2 * rows :]
        turned = pltpu.roll(out[:, c:], rows, 0)
        spread_out[2 * rows * k : 2 * rows * (k + 1)] = out[:, :c] + sign * turned
    for row in range(rows):
        parts = [spread_out[pl.ds(i * rows + row, modes, stride=2 * rows), :] for i in range(2)]
        mixed[:, row * c : (row + 1) * c] = jnp.concatenate(parts, axis=0).astype(BF)


def halo_kernel(mixed, out):
    c = out.shape[1] // HALO
    rows = mixed.shape[1] // c
    even = lax.rem(lax.axis_index("lon"), 2) == 0
    for at in range(HALO):
        last = mixed[:, (rows - 1 - at) * c : (rows - at) * c]
        leading = mixed[:, (HALO - 1 - at) * c : (HALO - at) * c]
        out[:, at * c : (at + 1) * c] = jnp.where(even, last, leading)


def pick(mine, other, first):
    even = lax.rem(lax.axis_index("lon"), 2) == 0
    return jnp.where(even == first, mine[...], other[...])


def next_state(old, conv, mixed, inverse, new, at, count, mask):
    c = mixed.shape[1] // conv[0].shape[0]
    width = conv[0].shape[1]
    tile = tile_of(width // RUNS)
    for pair in range(0, count, 2):
        lanes = slice(pair * c, min(pair + 2, count) * c)
        for start in range(0, width, tile):
            span = slice(start, start + tile)
            wide = slice(start + RUNS, start + RUNS + tile)
            waves = [dot(inverse[e, span], mixed[:, lanes]) for e in range(2)]
            for i in range(min(2, count - pair)):
                wave = jnp.concatenate([w[:, i * c : (i + 1) * c] for w in waves], axis=1)
                total = old[0][old[1] + pair + i, wide].astype(F32)
                total = total + conv[0][pair + i, span].astype(F32) + wave
                total = jnp.tanh(total)
                if mask is not None:
                    total = total * mask
                new[at + pair + i, wide] = total.astype(BF)
        for i in range(min(2, count - pair)):
            close_row(new, at + pair + i)


def middle_own_kernel(field, hidden, mixed, inverse, packed, bias, state, inner, sums):
    next_state((field, 0), (hidden,), mixed, inverse, state, 0, hidden.shape[0], None)
    early_part(state, inner, sums, packed, bias)


def middle_lower_kernel(
    field, from_down, mine, other, own, inner, sums, inverse, packed, bias,
    state, first, second, mixed_down,
):
    rows = own.shape[0]
    edge = lat_edges()
    state[:rows] = own[...]
    mixed_down[...] = pick(mine, other, True)
    next_state((field, rows), (from_down,), mixed_down, inverse, state, rows, HALO, edge[1])
    lower_part(state, inner, sums, first, second, packed, bias, edge, rows)


def middle_upper_kernel(
    before, from_up, mine, other, inverse, state, first, second, inner, sums,
    packed, bias, forward, leak,
    kept, sent, hidden, above, mixed_up, more, most, held,
):
    edge = lat_edges()
    mixed_up[...] = pick(mine, other, False)
    next_state((before, 0), (from_up,), mixed_up, inverse, above, 0, HALO, edge[0])

    def emit(row, start, y):
        span = slice(start, start + y.shape[0])
        held[row, span] = y
        hidden[row, span] = y

    args = (above, state, inner, sums, first, second, (more, most), packed, bias)
    upper_part(*args, edge, emit)
    transform(forward, leak, bias, held, kept, sent)


def last_kernel(state, hidden, mixed, inverse, result, line, done, sems):
    rows, width, c = hidden.shape[0], hidden.shape[1], hidden.shape[2] // 2
    cells = result.shape[1]
    run = 2 * width // RUNS
    copies = []
    for pair in range(0, rows, 2):
        waves = [dot(inverse[e], mixed[:, pair * c : (pair + 2) * c]) for e in range(2)]
        for i in range(2):
            row = pair + i
            for e in range(2):
                lanes = slice(e * c, (e + 1) * c)
                total = state[row, RUNS : RUNS + width, lanes].astype(F32) + hidden[row, :, lanes].astype(F32)
                total = jnp.tanh(total + waves[e][:, i * c : (i + 1) * c])
                for u in range(width // RUNS):
                    value = total[u * RUNS : (u + 1) * RUNS]
                    line[i, pl.ds(2 * u + e, RUNS, stride=run), :] = value
            done[row] = line[i, PAD : PAD + cells].astype(BF)
            copy = pltpu.make_async_copy(done.at[row], result.at[flip(row, rows)], sems.at[row])
            copy.start()
            copies.append(copy)
    for copy in copies:
        copy.wait()


def cell_order(width):
    run = width // RUNS
    cell = np.arange(width // 2) // RUNS * 2 + np.arange(width // 2) % RUNS * run
    return np.stack([cell, cell + 1])


def forward_table(cells, lon_total, modes, lon_size):
    order = cell_order(cells + 2 * PAD).reshape(-1) - PAD
    inside = (order >= 0) & (order < cells)
    waves = np.arange(modes)
    tables, leaks = [], []
    for core in range(2):
        theta = (2 * np.pi / lon_total) * (np.outer(waves, order + core * cells) % lon_total)
        full = np.stack([np.cos(theta), -np.sin(theta)], 0) * inside
        full = full.reshape(2, lon_size // 2, 2, modes // lon_size, -1)
        full = full.transpose(2, 1, 0, 3, 4)[[core, 1 - core]]
        tables.append(full.reshape(2 * modes, -1).astype(ml_dtypes.bfloat16))
        leaks.append(tables[-1].astype(np.float64).sum(1, keepdims=True).astype(np.float32))
    return np.stack(tables), np.stack(leaks)


def turn_table(lon_size, local, scale):
    chips = lon_size // 2
    me = np.arange(lon_size)[:, None, None]
    waves = me * local + np.arange(local)[:, None]
    source = 2 * ((me // 2) ^ np.arange(chips))
    phase = source * waves % lon_size * (2 * np.pi / lon_size)
    cos, sin = scale * np.cos(phase), scale * np.sin(phase)
    eye = np.eye(local)
    cos, sin = (x[:, :, :, None] * eye[:, None, :] for x in (cos, sin))
    real = np.stack([cos, sin], axis=3)
    imag = np.stack([-sin, cos], axis=3)
    full = np.concatenate([real, imag], axis=1)
    full = full.reshape(lon_size, 2 * local, chips * 2 * local).astype(np.float32)
    high = full.astype(ml_dtypes.bfloat16)
    low = (full - high.astype(np.float32)).astype(ml_dtypes.bfloat16)
    return np.concatenate([high, low], axis=1)


def inverse_parts(cells, lon_total, modes, lon_size):
    column = np.arange(2 * modes)
    local = modes // lon_size
    waves = column // (2 * local) * local + column % local
    imaginary = column // local % 2 == 1
    order = cell_order(cells + 2 * PAD) - PAD
    theta = (2 * np.pi / lon_total) * (order[:, :, None] * waves % lon_total)
    weight = np.where(waves == 0, 1.0, 2.0)
    cos, sin = weight * np.cos(theta), weight * np.sin(theta)
    by_cos = np.where(imaginary, -sin, cos).astype(np.float32)
    by_sin = np.where(imaginary, -cos, -sin).astype(np.float32)
    return waves.astype(np.int32), by_cos, by_sin


def phase_table(cells, lon_total, modes, lon_size):
    waves = inverse_parts(cells, lon_total, modes, lon_size)[0]
    phase = np.arange(lon_size)[:, None] * waves % lon_size * (2 * np.pi / lon_size)
    return np.stack([np.cos(phase), np.sin(phase)], 1).astype(np.float32)


def facing(rows, partner):
    odd = odd_lat()
    return (rows - HALO) * ((1 - odd) if partner else odd)


def slice_kernel(field, *rest):
    out, sem = rest[-2:]
    at = facing(field.shape[0], len(rest) == 2)
    copy = pltpu.make_async_copy(field.at[pl.ds(at, HALO)], out, sem)
    copy.start()
    copy.wait()


def side_kernel(field, after, last, leading, sems):
    cells = field.shape[1]
    first = pltpu.make_async_copy(field.at[:, cells - PAD :], last, sems.at[0])
    second = pltpu.make_async_copy(field.at[:, :PAD], leading, sems.at[1])
    first.start()
    second.start()
    first.wait()
    second.wait()


def edge_kernel(from_left, from_right, edges, near):
    rows = from_left.shape[0]
    for row in range(rows):
        edges[row] = jnp.concatenate([from_left[row], from_right[row]], axis=0)
    at = facing(rows, True)
    for row in range(HALO):
        near[row] = jnp.concatenate([from_left[at + row], from_right[at + row]], axis=0)


def copy_kernel(edges, near, other):
    at = facing(edges.shape[0], False)
    for row in range(HALO):
        other[row] = edges[at + row]


def inverse_kernel(parts, phase, after, inverse):
    turn = phase[lax.axis_index("lon")]
    for e in range(2):
        inverse[e] = (parts[0, e] * turn[0:1] + parts[1, e] * turn[1:2]).astype(BF)


def lat_edges():
    me, size, odd = lax.axis_index("lat"), lax.axis_size("lat"), odd_lat()
    after, before = (me < size - 1).astype(F32), (me > 0).astype(F32)
    even = (1 - odd).astype(F32)
    return [even * before + (1.0 - even) * after, even * after + (1.0 - even) * before]


def lat_pairs(partner):
    pairs = [(i, i + 1) for i in range(0 if partner else 1, lax.axis_size("lat") - 1, 2)]
    return pairs + [(j, i) for i, j in pairs]


def move(array, partner):
    return lax.ppermute(array, "lat", lat_pairs(partner))


def shape(*dims):
    return jax.ShapeDtypeStruct(dims, BF)


def call(kernel, args, outs, scratch, in_specs=None, out_specs=None, grid=(), cost=0):
    estimate = pl.CostEstimate(flops=int(cost * 8e8), bytes_accessed=0, transcendentals=0)
    return pl.pallas_call(
        kernel,
        grid=grid,
        out_shape=outs,
        in_specs=in_specs or [VMEM] * len(args),
        out_specs=out_specs or [VMEM] * len(outs),
        scratch_shapes=scratch,
        compiler_params=PARAMS,
        cost_estimate=estimate if cost else None,
    )(*(jnp.asarray(arg) for arg in args))


def per_device(field, conv_weight, conv_bias, spec_real, spec_imag):
    rows, cells, c = field.shape
    width = cells + 2 * PAD
    half = width // 2
    lon_size = lax.axis_size("lon")
    lon_total = cells * lon_size
    local = spec_real.shape[1]
    modes = local * lon_size

    wide = half + 2 * RUNS
    below = call(
        slice_kernel, (field,), [shape(HALO, cells, c)], [DMA], in_specs=[HBM], out_specs=[ANY]
    )[0]
    down = move(below, True)
    above = call(
        slice_kernel,
        (field, below),
        [shape(HALO, cells, c)],
        [DMA],
        in_specs=[HBM, ANY],
        out_specs=[ANY],
    )[0]
    up = move(above, False)
    last, leading = call(
        side_kernel,
        (field, above),
        [shape(rows, PAD, c)] * 2,
        [pltpu.SemaphoreType.DMA((2,))],
        in_specs=[HBM, ANY],
        out_specs=[ANY] * 2,
    )
    right = [(i, (i + 1) % lon_size) for i in range(lon_size)]
    left = [(j, i) for i, j in right]
    from_left = lax.ppermute(last, "lon", right)
    from_right = lax.ppermute(leading, "lon", left)
    own_edge, below = call(
        edge_kernel,
        (from_left, from_right),
        [shape(rows, 2 * PAD, c), shape(HALO, 2 * PAD, c)],
        [],
    )
    down_edge = move(below, True)
    above = call(
        copy_kernel, (own_edge, below), [shape(HALO, 2 * PAD, c)], [], in_specs=[VMEM, ANY]
    )[0]
    up_edge = move(above, False)
    tables = (cells, lon_total, modes, lon_size)
    inverse = call(
        inverse_kernel,
        (np.stack(inverse_parts(*tables)[1:]), phase_table(*tables), above),
        [shape(2, half, 2 * modes)],
        [],
        in_specs=[VMEM, VMEM, ANY],
    )[0]
    forward, leak = forward_table(*tables)
    turn = turn_table(lon_size, local, 1.0 / lon_total)

    line = pltpu.VMEM((2, width + 2 * half // RUNS + 8, c), F32)
    weights = shape(CONVS, 4 if WINOGRAD else 3, 4 * c, 2 * c)
    lower = [shape(n, wide, 2 * c) for n in (rows + HALO, 3, 2)]
    early = [shape(2, wide, 2 * c), jax.ShapeDtypeStruct((4, half, 2 * c), F32)]
    gathered = pltpu.VMEM((2 * modes, HALO * c), BF)
    upper = [pltpu.VMEM((4, wide, 2 * c), BF)] * 2 + [pltpu.VMEM((rows, half, 2 * c), BF)]
    hidden_shape = shape(rows, half, 2 * c)
    part_shape = [jax.ShapeDtypeStruct((modes, rows * c), F32)] * 2

    own_rows = shape(rows, wide, 2 * c)
    own, packed, later, *inner = call(
        prepare_kernel,
        (field, own_edge, conv_weight, conv_bias[0], inverse),
        [own_rows, weights, weights] + early,
        [line],
        in_specs=[VMEM] * 4 + [ANY],
        cost=4,
    )
    low = call(
        first_lower_kernel,
        (down, down_edge, own, packed, *inner, conv_bias[0]),
        lower,
        [line],
    )
    kept, sent, hidden, to_partner, to_other, before = call(
        first_upper_kernel,
        (up, up_edge, *low, *inner, packed, conv_bias[0], forward, leak),
        part_shape
        + [hidden_shape]
        + [shape(HALO, half, 2 * c)] * 2
        + [shape(HALO, wide, 2 * c)],
        [line] + upper,
    )
    def swap(array, step):
        return lax.ppermute(array, "lon", [(i, i ^ step) for i in range(lon_size)])

    chunk = shape(2 * local, rows * c)

    def pair(kept, sent):
        return call(pair_kernel, (kept, swap(sent, 1)), [chunk] * (lon_size // 2), [])

    def mix(own, others, block):
        sums = [own] + [swap(other, 2 * i + 2) for i, other in enumerate(others)]
        turned = pltpu.VMEM((2 * rows * (local + 1), c), F32)
        weights = pl.BlockSpec((1, local, c, c), lambda i: (block, 0, 0, 0))
        (mixed,) = call(
            mix_kernel,
            (turn, spec_real, spec_imag, conv_bias[block], *sums),
            [chunk],
            [turned, turned],
            in_specs=[VMEM, weights, weights] + [VMEM] * (1 + len(sums)),
            grid=(1,),
        )
        return lax.all_gather(mixed, "lon", axis=0, tiled=True)

    from_down, from_up = move(to_partner, True), move(to_other, False)
    own, *others = pair(kept, sent)
    mixed = mix(own, others, 0)
    halo = call(halo_kernel, (mixed,), [shape(2 * modes, HALO * c)], [])[0]
    lat_size = lax.axis_size("lat")
    ways = []
    for i in range(lon_size):
        ways += [(i * lat_size + j, i * lat_size + k) for j, k in lat_pairs(i % 2 == 0)]
    mine = lax.ppermute(halo, ("lon", "lat"), ways)
    own, *inner = call(
        middle_own_kernel,
        (low[0], hidden, mixed, inverse, later, conv_bias[1]),
        [own_rows] + early,
        [],
        cost=12,
    )
    other = swap(lax.optimization_barrier((mine, own))[0], 1)
    state, *low = call(
        middle_lower_kernel,
        (low[0], from_down, mine, other, own, *inner, inverse, later, conv_bias[1]),
        lower,
        [gathered],
    )
    kept, sent, hidden = call(
        middle_upper_kernel,
        (before, from_up, mine, other, inverse, state, *low, *inner)
        + (later, conv_bias[1], forward, leak),
        part_shape + [hidden_shape],
        [pltpu.VMEM((HALO, wide, 2 * c), BF), gathered] + upper,
    )
    own, *others = pair(kept, sent)
    mixed = mix(own, others, 1)
    (result,) = call(
        last_kernel,
        (state, hidden, mixed, inverse),
        [shape(rows, cells, c)],
        [line, pltpu.VMEM((rows, cells, c), BF), pltpu.SemaphoreType.DMA((rows,))],
        out_specs=[ANY],
    )
    return result


def solution(mesh):
    return jax.shard_map(
        per_device,
        mesh=mesh,
        in_specs=(
            P("lat", "lon", None),
            P(),
            P(),
            P(None, "lon", None, None),
            P(None, "lon", None, None),
        ),
        out_specs=P("lat", "lon", None),
        check_vma=False,
    )
```

```python
import math

import jax
import jax.numpy as jnp
import ml_dtypes
import numpy as np
from jax import lax
from jax.experimental import pallas as pl
from jax.experimental.pallas import tpu as pltpu
from jax.sharding import PartitionSpec as P

BLOCKS = 2
CONVS = 3
PAD = 16
RUNS = 16
HALO = 3
WINOGRAD = True
BF = jnp.bfloat16
F32 = jnp.float32
VMEM = pl.BlockSpec(memory_space=pltpu.VMEM)
ANY = pl.BlockSpec(memory_space=pl.ANY)
HBM = pl.BlockSpec(memory_space=pltpu.HBM)
DMA = pltpu.SemaphoreType.DMA
PARAMS = pltpu.CompilerParams(vmem_limit_bytes=28 << 20)


def odd_lat():
    return lax.rem(lax.axis_index("lat"), 2)


def flip(row, rows):
    return row + odd_lat() * (rows - 1 - 2 * row)


def tile_of(tiles):
    return max(n for n in range(1, 34) if tiles % n == 0) * RUNS


def pack_row(line, wide, row):
    c = line.shape[1]
    run = 2 * (wide.shape[1] // RUNS - 2)
    for cell in range(run):
        lanes = slice(cell % 2 * c, (cell % 2 + 1) * c)
        at = RUNS * (cell // 2 + 1)
        wide[row, at : at + RUNS, lanes] = line[pl.ds(cell, RUNS, stride=run), :].astype(BF)


def close_row(wide, row):
    c = wide.shape[2] // 2
    end = wide.shape[1] - RUNS
    before = wide[row, end - RUNS : end, c:].astype(F32)
    wide[row, 0:RUNS, c:] = pltpu.roll(before, 1, 0).astype(BF)
    after = wide[row, RUNS : 2 * RUNS, :c].astype(F32)
    wide[row, end : end + RUNS, :c] = pltpu.roll(after, RUNS - 1, 0).astype(BF)


def build_weights(kernels, block, packed, layer):
    c = kernels.shape[-1]
    zero = jnp.zeros((c, c), BF)
    for tap in range(3):
        g0, g1, g2 = (kernels[block, layer, flip(a, 3), tap].astype(F32) for a in range(3))
        if WINOGRAD:
            outer = g0 + g2
            parts = (0.5 * g0, 0.25 * (outer + g1), 0.25 * (outer - g1), 0.5 * g2)
        else:
            parts = (0.5 * g0, 0.5 * g1, 0.5 * g2)
        for i, part in enumerate(parts):
            value = part.astype(BF)
            for cell in range(2):
                source = cell + tap - 1
                at = {0: 0, 1: c, 2: 2 * c, -1: 3 * c}[source]
                packed[layer, i, at : at + c, cell * c : (cell + 1) * c] = value
    for i in range(packed.shape[1]):
        packed[layer, i, 2 * c : 3 * c, :c] = zero
        packed[layer, i, 3 * c :, c:] = zero


def window(wide, row, start, size):
    c = wide.shape[2] // 2
    here = wide[row, start + RUNS : start + RUNS + size]
    after = wide[row, start + 2 * RUNS : start + 2 * RUNS + size, :c]
    before = wide[row, start : start + size, c:]
    return jnp.concatenate([here, after, before], axis=1)


def dot(a, b):
    return jnp.dot(a, b, preferred_element_type=F32)


def halves(x):
    high = x.astype(BF)
    return high, (x - high.astype(F32)).astype(BF)


def silu_of_half(half):
    return half + half * jnp.tanh(half)


def conv_pair(d, packed, layer):
    if WINOGRAD:
        inputs = (d[0] - d[2], d[1] + d[2], d[2] - d[1], d[1] - d[3])
        m = [dot(x, packed[layer, i]) for i, x in enumerate(inputs)]
        return (m[1] + m[2]) + m[0], m[1] - m[2] - m[3]
    w = jnp.concatenate([packed[layer, i] for i in range(3)], axis=0)
    return tuple(dot(jnp.concatenate(d[i : i + 3], axis=1), w) for i in range(2))


class Rows:
    def __init__(self, *held):
        self.at = {}
        for ref, first in held:
            self.at.update({first + i: (ref, i) for i in range(ref.shape[0])})

    def __getitem__(self, row):
        return self.at[row]


def conv_rows(src, dst, span, layer, packed, bias, edge, rows):
    ref = src[span[0]][0]
    width = ref.shape[1] - 2 * RUNS
    tile = tile_of(width // RUNS)
    both = 0.5 * jnp.concatenate([bias[layer : layer + 1]] * 2, axis=1)
    for pair in range(*span, 2):
        for start in range(0, width, tile):
            sums = conv_pair(
                [window(*src[pair + i - 1], start, tile) for i in range(4)], packed, layer
            )
            for i, total in enumerate(sums):
                row = pair + i
                y = silu_of_half(total + both)
                if row < 0:
                    y = y * edge[0]
                elif row >= rows:
                    y = y * edge[1]
                if callable(dst):
                    dst(row, start, y.astype(BF))
                else:
                    ref, at = dst[row]
                    ref[at, start + RUNS : start + RUNS + tile] = y.astype(BF)
        if not callable(dst):
            for i in range(2):
                close_row(*dst[pair + i])


def transform(forward, held, kept, sent):
    core = lax.rem(lax.axis_index("lon"), 2)
    rows, c = held.shape[0], held.shape[2] // 2
    for row in range(0, rows, 2):
        cells = [
            jnp.concatenate([held[row + i, :, e * c : (e + 1) * c] for i in range(2)], axis=1)
            for e in range(2)
        ]
        total = dot(forward[core], jnp.concatenate(cells, axis=0))
        half = total.shape[0] // 2
        lanes = slice(row * c, (row + 2) * c)
        kept[:, lanes] = total[:half]
        sent[:, lanes] = total[half:]


def pack_cells(body, ends, source, line, wide, at):
    cells = body.shape[1]
    line[0:PAD] = ends[source, :PAD].astype(F32)
    line[PAD : PAD + cells] = body[source].astype(F32)
    line[PAD + cells : 2 * PAD + cells] = ends[source, PAD:].astype(F32)
    pack_row(line, wide, at)
    close_row(wide, at)


def product(a, b, sign, start, tile, packed, layer, index):
    left, right = window(*a, start, tile), window(*b, start, tile)
    return dot(left + right if sign > 0 else left - right, packed[layer, index])


def put(dst, start, half, bias, layer):
    ref, at = dst
    both = 0.5 * jnp.concatenate([bias[layer : layer + 1]] * 2, axis=1)
    y = silu_of_half(half + both).astype(BF)
    ref[at, start + RUNS : start + RUNS + y.shape[0]] = y


def spans(ref):
    width = ref.shape[1] - 2 * RUNS
    tile = tile_of(width // RUNS)
    return [(start, tile) for start in range(0, width, tile)]


def early_part(field, inner, sums, packed, bias):
    x, y = Rows((field, 0)), Rows((inner, 1))
    for start, tile in spans(field):
        span = slice(start, start + tile)
        args = (start, tile, packed, 0)
        m1 = product(x[0], x[1], 1, *args, 1)
        m2 = product(x[1], x[0], -1, *args, 2)
        m3 = product(x[0], x[2], -1, *args, 3)
        sums[0, span] = m1 + m2
        put(y[1], start, m1 - m2 - m3, bias, 0)
        m0 = product(x[1], x[3], -1, *args, 0)
        m1 = product(x[2], x[3], 1, *args, 1)
        m2 = product(x[3], x[2], -1, *args, 2)
        sums[1, span] = m1 - m2
        put(y[2], start, (m1 + m2) + m0, bias, 0)
    close_row(*y[1])
    close_row(*y[2])
    for start, tile in spans(field):
        span = slice(start, start + tile)
        args = (start, tile, packed, 1)
        m1 = product(y[1], y[2], 1, *args, 1)
        m2 = product(y[2], y[1], -1, *args, 2)
        sums[2, span] = m1 + m2
        sums[3, span] = m1 - m2


def lower_part(field, inner, sums, first, second, packed, bias, edge, rows):
    x, y, z = Rows((field, 0)), Rows((inner, 1), (first, 3)), Rows((second, 3))
    for start, tile in spans(field):
        m3 = product(x[2], x[4], -1, start, tile, packed, 0, 3)
        put(y[3], start, sums[1, start : start + tile] - m3, bias, 0)
    close_row(*y[3])
    conv_rows(x, y, (4, 6), 0, packed, bias, edge, rows)
    conv_rows(y, z, (3, 5), 1, packed, bias, edge, rows)


def upper_part(before, field, inner, sums, first, second, more, packed, bias, edge, emit):
    rows = field.shape[0] - HALO
    x = Rows((before, -HALO), (field, 0))
    y = Rows((more[0], -2), (inner, 1), (first, 3))
    z = Rows((more[1], -1), (second, 3))
    conv_rows(x, y, (-2, 0), 0, packed, bias, edge, rows)
    for start, tile in spans(field):
        m0 = product(x[-1], x[1], -1, start, tile, packed, 0, 0)
        put(y[0], start, sums[0, start : start + tile] + m0, bias, 0)
    close_row(*y[0])
    conv_rows(y, z, (-1, 1), 1, packed, bias, edge, rows)
    for start, tile in spans(field):
        span = slice(start, start + tile)
        m0 = product(y[0], y[2], -1, start, tile, packed, 1, 0)
        m3 = product(y[1], y[3], -1, start, tile, packed, 1, 3)
        put(z[1], start, sums[2, span] + m0, bias, 1)
        put(z[2], start, sums[3, span] - m3, bias, 1)
    close_row(*z[1])
    close_row(*z[2])
    conv_rows(z, emit, (0, rows), 2, packed, bias, edge, rows)


def prepare_kernel(own, own_edge, kernels, bias, after, field, packed, later, inner, sums, line):
    rows = own.shape[0]
    for layer in range(CONVS):
        build_weights(kernels, 0, packed, layer)
        build_weights(kernels, 1, later, layer)
    for row in range(rows):
        pack_cells(own, own_edge, flip(row, rows), line.at[row % 2], field, row)
    early_part(field, inner, sums, packed, bias)


def first_lower_kernel(
    down, down_edge, own, packed, inner, sums, bias, field, first, second, line
):
    rows = own.shape[0]
    field[:rows] = own[...]
    for row in range(HALO):
        pack_cells(down, down_edge, flip(row, HALO), line.at[row % 2], field, rows + row)
    lower_part(field, inner, sums, first, second, packed, bias, lat_edges(), rows)


def first_upper_kernel(
    up, up_edge, field, first, second, inner, sums, packed, bias, forward,
    kept, sent, hidden, to_partner, to_other, before,
    line, more, most, held,
):
    rows = field.shape[0] - HALO
    for row in range(HALO):
        pack_cells(up, up_edge, flip(row, HALO), line.at[row % 2], before, row)

    def emit(row, start, y):
        span = slice(start, start + y.shape[0])
        held[row, span] = y
        hidden[row, span] = y
        if row < HALO:
            to_other[HALO - 1 - row, span] = y
        if row >= rows - HALO:
            to_partner[rows - 1 - row, span] = y

    args = (before, field, inner, sums, first, second, (more, most), packed, bias)
    upper_part(*args, lat_edges(), emit)
    transform(forward, held, kept, sent)


def pair_kernel(kept, got, *outs):
    chip = lax.div(lax.axis_index("lon"), 2)
    rows = outs[0].shape[0]
    for step, out in enumerate(outs):
        span = pl.ds(pl.multiple_of((chip ^ step) * rows, rows), rows)
        out[...] = kept[span, :] + got[span, :]


def mix_kernel(turn, real, imag, *rest):
    *sums, mixed, spread_in, spread_out = rest
    me = lax.axis_index("lon")
    modes, c = real.shape[1], real.shape[2]
    high, low = halves(jnp.concatenate([x[...] for x in sums], axis=0))
    summed = dot(turn[me], high)
    summed = summed[: 2 * modes] + summed[2 * modes :]
    summed = summed + dot(turn[me, : 2 * modes], low)
    rows = summed.shape[1] // c
    for half in range(2):
        for row in range(rows):
            spread_in[pl.ds(half * rows + row, modes, stride=2 * rows), :] = summed[
                half * modes : (half + 1) * modes, row * c : (row + 1) * c
            ]
    sign = jnp.where(lax.broadcasted_iota(jnp.int32, (2 * rows, c), 0) < rows, -1.0, 1.0)
    for k in range(modes):
        wide = spread_in[2 * rows * k : 2 * rows * (k + 1)]
        both = jnp.concatenate(halves(wide), axis=0)
        weight = jnp.concatenate([real[0, k], imag[0, k]], axis=1)
        out = jnp.dot(both, weight, preferred_element_type=F32)
        out = out[: 2 * rows] + out[2 * rows :]
        turned = pltpu.roll(out[:, c:], rows, 0)
        spread_out[2 * rows * k : 2 * rows * (k + 1)] = out[:, :c] + sign * turned
    for row in range(rows):
        parts = [spread_out[pl.ds(i * rows + row, modes, stride=2 * rows), :] for i in range(2)]
        mixed[:, row * c : (row + 1) * c] = jnp.concatenate(parts, axis=0).astype(mixed.dtype)


def halo_kernel(mixed, out):
    c = out.shape[1] // HALO
    rows = mixed.shape[1] // c
    even = lax.rem(lax.axis_index("lon"), 2) == 0
    for at in range(HALO):
        last = mixed[:, (rows - 1 - at) * c : (rows - at) * c]
        leading = mixed[:, (HALO - 1 - at) * c : (HALO - at) * c]
        out[:, at * c : (at + 1) * c] = jnp.where(even, last, leading).astype(BF)


def pick(mine, other, first):
    even = lax.rem(lax.axis_index("lon"), 2) == 0
    return jnp.where(even == first, mine[...], other[...])


def wave_of(inverse, mixed):
    if mixed.dtype == BF:
        return dot(inverse, mixed)
    high, low = halves(mixed)
    return dot(inverse, high) + dot(inverse, low)


def next_state(old, conv, mixed, inverse, new, at, count, mask):
    c = mixed.shape[1] // conv[0].shape[0]
    width = conv[0].shape[1]
    tile = tile_of(width // RUNS)
    for pair in range(0, count, 2):
        lanes = slice(pair * c, min(pair + 2, count) * c)
        for start in range(0, width, tile):
            span = slice(start, start + tile)
            wide = slice(start + RUNS, start + RUNS + tile)
            waves = [wave_of(inverse[e, span], mixed[:, lanes]) for e in range(2)]
            for i in range(min(2, count - pair)):
                wave = jnp.concatenate([w[:, i * c : (i + 1) * c] for w in waves], axis=1)
                total = old[0][old[1] + pair + i, wide].astype(F32)
                total = total + conv[0][pair + i, span].astype(F32) + wave
                total = jnp.tanh(total)
                if mask is not None:
                    total = total * mask
                new[at + pair + i, wide] = total.astype(BF)
        for i in range(min(2, count - pair)):
            close_row(new, at + pair + i)


def middle_own_kernel(field, hidden, mixed, inverse, packed, bias, state, inner, sums):
    next_state((field, 0), (hidden,), mixed, inverse, state, 0, hidden.shape[0], None)
    early_part(state, inner, sums, packed, bias)


def middle_lower_kernel(
    field, from_down, mine, other, own, inner, sums, inverse, packed, bias,
    state, first, second, mixed_down,
):
    rows = own.shape[0]
    edge = lat_edges()
    state[:rows] = own[...]
    mixed_down[...] = pick(mine, other, True)
    next_state((field, rows), (from_down,), mixed_down, inverse, state, rows, HALO, edge[1])
    lower_part(state, inner, sums, first, second, packed, bias, edge, rows)


def middle_upper_kernel(
    before, from_up, mine, other, inverse, state, first, second, inner, sums,
    packed, bias, forward,
    kept, sent, hidden, above, mixed_up, more, most, held,
):
    edge = lat_edges()
    mixed_up[...] = pick(mine, other, False)
    next_state((before, 0), (from_up,), mixed_up, inverse, above, 0, HALO, edge[0])

    def emit(row, start, y):
        span = slice(start, start + y.shape[0])
        held[row, span] = y
        hidden[row, span] = y

    args = (above, state, inner, sums, first, second, (more, most), packed, bias)
    upper_part(*args, edge, emit)
    transform(forward, held, kept, sent)


def last_kernel(state, hidden, mixed, inverse, result, line, done, sems):
    rows, width, c = hidden.shape[0], hidden.shape[1], hidden.shape[2] // 2
    cells = result.shape[1]
    run = 2 * width // RUNS
    copies = []
    for pair in range(0, rows, 2):
        lanes = slice(pair * c, (pair + 2) * c)
        waves = [wave_of(inverse[e], mixed[:, lanes]) for e in range(2)]
        for i in range(2):
            row = pair + i
            for e in range(2):
                lanes = slice(e * c, (e + 1) * c)
                total = state[row, RUNS : RUNS + width, lanes].astype(F32) + hidden[row, :, lanes].astype(F32)
                total = jnp.tanh(total + waves[e][:, i * c : (i + 1) * c])
                for u in range(width // RUNS):
                    value = total[u * RUNS : (u + 1) * RUNS]
                    line[i, pl.ds(2 * u + e, RUNS, stride=run), :] = value
            done[row] = line[i, PAD : PAD + cells].astype(BF)
            copy = pltpu.make_async_copy(done.at[row], result.at[flip(row, rows)], sems.at[row])
            copy.start()
            copies.append(copy)
    for copy in copies:
        copy.wait()


def cell_order(width):
    run = width // RUNS
    cell = np.arange(width // 2) // RUNS * 2 + np.arange(width // 2) % RUNS * run
    return np.stack([cell, cell + 1])


def forward_table(cells, lon_total, modes, lon_size):
    order = cell_order(cells + 2 * PAD).reshape(-1) - PAD
    inside = (order >= 0) & (order < cells)
    waves = np.arange(modes)
    tables = []
    for core in range(2):
        theta = (2 * np.pi / lon_total) * (np.outer(waves, order + core * cells) % lon_total)
        full = np.stack([np.cos(theta), -np.sin(theta)], 0) * inside
        full = full.reshape(2, lon_size // 2, 2, modes // lon_size, -1)
        full = full.transpose(2, 1, 0, 3, 4)[[core, 1 - core]]
        tables.append(full.reshape(2 * modes, -1).astype(ml_dtypes.bfloat16))
    return np.stack(tables)


def turn_table(lon_size, local, scale):
    chips = lon_size // 2
    me = np.arange(lon_size)[:, None, None]
    waves = me * local + np.arange(local)[:, None]
    source = 2 * ((me // 2) ^ np.arange(chips))
    phase = source * waves % lon_size * (2 * np.pi / lon_size)
    cos, sin = scale * np.cos(phase), scale * np.sin(phase)
    eye = np.eye(local)
    cos, sin = (x[:, :, :, None] * eye[:, None, :] for x in (cos, sin))
    real = np.stack([cos, sin], axis=3)
    imag = np.stack([-sin, cos], axis=3)
    full = np.concatenate([real, imag], axis=1)
    full = full.reshape(lon_size, 2 * local, chips * 2 * local).astype(np.float32)
    high = full.astype(ml_dtypes.bfloat16)
    low = (full - high.astype(np.float32)).astype(ml_dtypes.bfloat16)
    return np.concatenate([high, low], axis=1)


def inverse_parts(cells, lon_total, modes, lon_size):
    column = np.arange(2 * modes)
    local = modes // lon_size
    waves = column // (2 * local) * local + column % local
    imaginary = column // local % 2 == 1
    order = cell_order(cells + 2 * PAD) - PAD
    theta = (2 * np.pi / lon_total) * (order[:, :, None] * waves % lon_total)
    weight = np.where(waves == 0, 1.0, 2.0)
    cos, sin = weight * np.cos(theta), weight * np.sin(theta)
    by_cos = np.where(imaginary, -sin, cos).astype(np.float32)
    by_sin = np.where(imaginary, -cos, -sin).astype(np.float32)
    return waves.astype(np.int32), by_cos, by_sin


def phase_table(cells, lon_total, modes, lon_size):
    waves = inverse_parts(cells, lon_total, modes, lon_size)[0]
    phase = np.arange(lon_size)[:, None] * waves % lon_size * (2 * np.pi / lon_size)
    return np.stack([np.cos(phase), np.sin(phase)], 1).astype(np.float32)


def facing(rows, partner):
    odd = odd_lat()
    return (rows - HALO) * ((1 - odd) if partner else odd)


def slice_kernel(field, *rest):
    out, sem = rest[-2:]
    at = facing(field.shape[0], len(rest) == 2)
    copy = pltpu.make_async_copy(field.at[pl.ds(at, HALO)], out, sem)
    copy.start()
    copy.wait()


def side_kernel(field, after, last, leading, sems):
    cells = field.shape[1]
    first = pltpu.make_async_copy(field.at[:, cells - PAD :], last, sems.at[0])
    second = pltpu.make_async_copy(field.at[:, :PAD], leading, sems.at[1])
    first.start()
    second.start()
    first.wait()
    second.wait()


def edge_kernel(from_left, from_right, edges, near):
    rows = from_left.shape[0]
    for row in range(rows):
        edges[row] = jnp.concatenate([from_left[row], from_right[row]], axis=0)
    at = facing(rows, True)
    for row in range(HALO):
        near[row] = jnp.concatenate([from_left[at + row], from_right[at + row]], axis=0)


def copy_kernel(edges, near, other):
    at = facing(edges.shape[0], False)
    for row in range(HALO):
        other[row] = edges[at + row]


def inverse_kernel(parts, phase, after, inverse):
    turn = phase[lax.axis_index("lon")]
    for e in range(2):
        inverse[e] = (parts[0, e] * turn[0:1] + parts[1, e] * turn[1:2]).astype(BF)


def lat_edges():
    me, size, odd = lax.axis_index("lat"), lax.axis_size("lat"), odd_lat()
    after, before = (me < size - 1).astype(F32), (me > 0).astype(F32)
    even = (1 - odd).astype(F32)
    return [even * before + (1.0 - even) * after, even * after + (1.0 - even) * before]


def lat_pairs(partner):
    pairs = [(i, i + 1) for i in range(0 if partner else 1, lax.axis_size("lat") - 1, 2)]
    return pairs + [(j, i) for i, j in pairs]


def move(array, partner):
    return lax.ppermute(array, "lat", lat_pairs(partner))


def shape(*dims):
    return jax.ShapeDtypeStruct(dims, BF)


def call(kernel, args, outs, scratch, in_specs=None, out_specs=None, grid=(), cost=0):
    estimate = pl.CostEstimate(flops=int(cost * 8e8), bytes_accessed=0, transcendentals=0)
    return pl.pallas_call(
        kernel,
        grid=grid,
        out_shape=outs,
        in_specs=in_specs or [VMEM] * len(args),
        out_specs=out_specs or [VMEM] * len(outs),
        scratch_shapes=scratch,
        compiler_params=PARAMS,
        cost_estimate=estimate if cost else None,
    )(*(jnp.asarray(arg) for arg in args))


def per_device(field, conv_weight, conv_bias, spec_real, spec_imag):
    rows, cells, c = field.shape
    width = cells + 2 * PAD
    half = width // 2
    lon_size = lax.axis_size("lon")
    lon_total = cells * lon_size
    local = spec_real.shape[1]
    modes = local * lon_size

    wide = half + 2 * RUNS
    below = call(
        slice_kernel, (field,), [shape(HALO, cells, c)], [DMA], in_specs=[HBM], out_specs=[ANY]
    )[0]
    down = move(below, True)
    above = call(
        slice_kernel,
        (field, below),
        [shape(HALO, cells, c)],
        [DMA],
        in_specs=[HBM, ANY],
        out_specs=[ANY],
    )[0]
    up = move(above, False)
    last, leading = call(
        side_kernel,
        (field, above),
        [shape(rows, PAD, c)] * 2,
        [pltpu.SemaphoreType.DMA((2,))],
        in_specs=[HBM, ANY],
        out_specs=[ANY] * 2,
    )
    right = [(i, (i + 1) % lon_size) for i in range(lon_size)]
    left = [(j, i) for i, j in right]
    from_left = lax.ppermute(last, "lon", right)
    from_right = lax.ppermute(leading, "lon", left)
    own_edge, below = call(
        edge_kernel,
        (from_left, from_right),
        [shape(rows, 2 * PAD, c), shape(HALO, 2 * PAD, c)],
        [],
    )
    down_edge = move(below, True)
    above = call(
        copy_kernel, (own_edge, below), [shape(HALO, 2 * PAD, c)], [], in_specs=[VMEM, ANY]
    )[0]
    up_edge = move(above, False)
    tables = (cells, lon_total, modes, lon_size)
    inverse = call(
        inverse_kernel,
        (np.stack(inverse_parts(*tables)[1:]), phase_table(*tables), above),
        [shape(2, half, 2 * modes)],
        [],
        in_specs=[VMEM, VMEM, ANY],
    )[0]
    forward = forward_table(*tables)
    turn = turn_table(lon_size, local, 1.0 / lon_total)

    line = pltpu.VMEM((2, width + 2 * half // RUNS + 8, c), F32)
    weights = shape(CONVS, 4 if WINOGRAD else 3, 4 * c, 2 * c)
    lower = [shape(n, wide, 2 * c) for n in (rows + HALO, 3, 2)]
    early = [shape(2, wide, 2 * c), jax.ShapeDtypeStruct((4, half, 2 * c), F32)]
    gathered = pltpu.VMEM((2 * modes, HALO * c), BF)
    upper = [pltpu.VMEM((4, wide, 2 * c), BF)] * 2 + [pltpu.VMEM((rows, half, 2 * c), BF)]
    hidden_shape = shape(rows, half, 2 * c)
    part_shape = [jax.ShapeDtypeStruct((modes, rows * c), F32)] * 2

    own_rows = shape(rows, wide, 2 * c)
    own, packed, later, *inner = call(
        prepare_kernel,
        (field, own_edge, conv_weight, conv_bias[0], inverse),
        [own_rows, weights, weights] + early,
        [line],
        in_specs=[VMEM] * 4 + [ANY],
        cost=4,
    )
    low = call(
        first_lower_kernel,
        (down, down_edge, own, packed, *inner, conv_bias[0]),
        lower,
        [line],
    )
    kept, sent, hidden, to_partner, to_other, before = call(
        first_upper_kernel,
        (up, up_edge, *low, *inner, packed, conv_bias[0], forward),
        part_shape
        + [hidden_shape]
        + [shape(HALO, half, 2 * c)] * 2
        + [shape(HALO, wide, 2 * c)],
        [line] + upper,
    )
    def swap(array, step):
        return lax.ppermute(array, "lon", [(i, i ^ step) for i in range(lon_size)])

    chunk = jax.ShapeDtypeStruct((2 * local, rows * c), F32)

    def pair(kept, sent):
        return call(pair_kernel, (kept, swap(sent, 1)), [chunk] * (lon_size // 2), [])

    def mix(own, others, block):
        sums = [own] + [swap(other, 2 * i + 2) for i, other in enumerate(others)]
        turned = pltpu.VMEM((2 * rows * (local + 1), c), F32)
        weights = pl.BlockSpec((1, local, c, c), lambda i: (block, 0, 0, 0))
        (mixed,) = call(
            mix_kernel,
            (turn, spec_real, spec_imag, *sums),
            [shape(2 * local, rows * c) if block == 0 else chunk],
            [turned, turned],
            in_specs=[VMEM, weights, weights] + [VMEM] * len(sums),
            grid=(1,),
        )
        return lax.all_gather(mixed, "lon", axis=0, tiled=True)

    from_down, from_up = move(to_partner, True), move(to_other, False)
    own, *others = pair(kept, sent)
    mixed = mix(own, others, 0)
    halo = call(halo_kernel, (mixed,), [shape(2 * modes, HALO * c)], [])[0]
    lat_size = lax.axis_size("lat")
    ways = []
    for i in range(lon_size):
        ways += [(i * lat_size + j, i * lat_size + k) for j, k in lat_pairs(i % 2 == 0)]
    mine = lax.ppermute(halo, ("lon", "lat"), ways)
    own, *inner = call(
        middle_own_kernel,
        (low[0], hidden, mixed, inverse, later, conv_bias[1]),
        [own_rows] + early,
        [],
        cost=12,
    )
    other = swap(lax.optimization_barrier((mine, own))[0], 1)
    state, *low = call(
        middle_lower_kernel,
        (low[0], from_down, mine, other, own, *inner, inverse, later, conv_bias[1]),
        lower,
        [gathered],
    )
    kept, sent, hidden = call(
        middle_upper_kernel,
        (before, from_up, mine, other, inverse, state, *low, *inner)
        + (later, conv_bias[1], forward),
        part_shape + [hidden_shape],
        [pltpu.VMEM((HALO, wide, 2 * c), BF), gathered] + upper,
    )
    own, *others = pair(kept, sent)
    mixed = mix(own, others, 1)
    (result,) = call(
        last_kernel,
        (state, hidden, mixed, inverse),
        [shape(rows, cells, c)],
        [line, pltpu.VMEM((rows, cells, c), BF), pltpu.SemaphoreType.DMA((rows,))],
        out_specs=[ANY],
    )
    return result


def solution(mesh):
    return jax.shard_map(
        per_device,
        mesh=mesh,
        in_specs=(
            P("lat", "lon", None),
            P(),
            P(),
            P(None, "lon", None, None),
            P(None, "lon", None, None),
        ),
        out_specs=P("lat", "lon", None),
        check_vma=False,
    )
```
